32 devices in a mesh: rep: 16 (over z, y, core), shard: 2 (over x).
Axes of the slice: x: 2, y: 2, z: 4, core: 2. Of those that a mesh axis runs over, the one named last changes fastest.
Arguments:
- stream_in: bfloat16 [4096, 2048], P(('rep', 'shard')), may hold values from -6 to 6
- stream_grad: bfloat16 [4096, 2048], P(('rep', 'shard')), may hold values from -6 to 6
- prefix_len: int32 [16], replicated, may hold values from 1 to 256, as said below
- routes: int32 [4096, 6], P(('rep', 'shard')), may hold values from 0 to 15, all different within a row; in each aligned block of 128 rows (0 to 127, 128 to 255, ...) at most 56 rows name the same one
- route_weight: float32 [4096, 6], P(('rep', 'shard')), may hold values from 0.5 to 2
- attn_gain: bfloat16 [2048], P('shard'), may hold values from 0.5 to 1.5
- query_proj: bfloat16 [2048, 3072], P('shard'), may hold values from -0.125 to 0.125
- latent_proj: bfloat16 [2048, 512], P('shard'), may hold values from -0.125 to 0.125
- rope_key_proj: bfloat16 [2048, 64], P('shard'), may hold values from -0.125 to 0.125
- latent_gain: bfloat16 [512], P('shard'), may hold values from 0.5 to 1.5
- kv_up_proj: bfloat16 [512, 4096], P('shard'), may hold values from -0.25 to 0.25
- out_proj: bfloat16 [2048, 2048], P('shard'), may hold values from -0.75 to 0.75
- ffn_gain: bfloat16 [2048], P('shard'), may hold values from 0.5 to 1.5
- router_proj: bfloat16 [2048, 16], P('shard'), may hold values from -0.06591797 to 0.06591797
- shared_gate: bfloat16 [2048, 2816], P(('rep', 'shard')), may hold values from -0.125 to 0.125
- shared_up: bfloat16 [2048, 2816], P(('rep', 'shard')), may hold values from -0.125 to 0.125
- shared_down: bfloat16 [2816, 2048], P(('rep', 'shard')), may hold values from -0.109375 to 0.109375
- expert_gate: bfloat16 [16, 2048, 1408], P('rep', None, 'shard'), may hold values from -0.125 to 0.125
- expert_up: bfloat16 [16, 2048, 1408], P('rep', None, 'shard'), may hold values from -0.125 to 0.125
- expert_down: bfloat16 [16, 1408, 2048], P('rep', 'shard'), may hold values from -0.15625 to 0.15625
Outputs:
- stream_out: bfloat16 [4096, 2048], P(('rep', 'shard'))
- grad_stream: bfloat16 [4096, 2048], P(('rep', 'shard'))
- stats: float32 [5], replicated
- grad_attn_gain: float32 [2048], P(('rep', 'shard'))
- grad_query_proj: float32 [2048, 3072], P(('rep', 'shard'))
- grad_latent_proj: float32 [2048, 512], P(('rep', 'shard'))
- grad_rope_key_proj: float32 [2048, 64], P(('rep', 'shard'))
- grad_latent_gain: float32 [512], P(('rep', 'shard'))
- grad_kv_up_proj: float32 [512, 4096], P(('rep', 'shard'))
- grad_out_proj: float32 [2048, 2048], P(('rep', 'shard'))
- grad_ffn_gain: float32 [2048], P(('rep', 'shard'))
- grad_router_proj: float32 [2048, 16], P(('rep', 'shard'))
- grad_shared_gate: float32 [2048, 2816], P(('rep', 'shard'))
- grad_shared_up: float32 [2048, 2816], P(('rep', 'shard'))
- grad_shared_down: float32 [2816, 2048], P(('rep', 'shard'))
- grad_expert_gate: float32 [16, 2048, 1408], P('rep', None, 'shard')
- grad_expert_up: float32 [16, 2048, 1408], P('rep', None, 'shard')
- grad_expert_down: float32 [16, 1408, 2048], P('rep', 'shard')
The draws below stay inside these ranges and needn't reach their ends.
Inputs may be any that keep to these rules, and one draw needn't show every extreme that they name: `prefix_len`: one sequence, drawn from the seed, has a prefix of 256. `routes`: each row names 6 different experts; among the rows of one device no expert is named more than 56 times.
All inputs are finite; a program needn't handle non-finite values.
Results may differ from the reference program's by a relative error of at most 0.018.
Values may be sent and summed in bfloat16 or wider, within the bound.
A program may use at most 384 MiB of HBM per device.

```python
import math
from functools import partial
import jax
import jax.numpy as jnp
import numpy as np
from jax import lax

D = 2048
H = 16
DN = 128
DR = 64
DV = 128
KVR = 512
FS = 2816
FE = 1408
TOP_K = 6
TOK_DEV = 128
EXPERTS = 16
CAP = 56
SEQ_LEN = 256
SEQS = 16
TOKENS = 4096
N_SHARD = 2
DEVICES = 32


def draw_stream_in(key, part):
    key = jax.random.fold_in(key, 11)
    row_index = jnp.arange(TOKENS, dtype=jnp.float32)[:, None]
    row_scale = 0.5 + row_index / TOKENS
    samples = jnp.clip(jax.random.normal(key, (TOKENS, D), jnp.float32), -4.0, 4.0)
    return (samples * row_scale).astype(jnp.bfloat16)


def draw_prefix_len(key, part):
    key = jax.random.fold_in(key, 23)
    key_len, key_pick = jax.random.split(key)
    lengths = jax.random.randint(key_len, (SEQS,), 1, SEQ_LEN + 1)
    chosen = jax.random.randint(key_pick, (), 0, SEQS)
    return jnp.where(jnp.arange(SEQS) == chosen, SEQ_LEN, lengths).astype(jnp.int32)


def shard_levels(key, dims, shards, least, top_value):
    gain = 1.0
    for position, shards_of in shards:
        draws = jax.random.uniform(jax.random.fold_in(jax.random.fold_in(key, 6), position), (shards_of,), jnp.float32, least / len(shards), top_value / len(shards))
        gain = gain * jnp.repeat(jnp.exp(draws), dims[position] // shards_of).reshape((-1,) + (1,) * (len(dims) - 1 - position))
    return gain


def routed_block(own_key, own, number, rows, amount, top, bound, lean):
    sequence = jax.random.permutation(own_key, amount)
    heavy_load, ordinary = load_shares(amount, rows * top, bound, lean, True), load_shares(amount, rows * top, bound, lean, False)
    places = jnp.arange(amount)

    def named(sizes, rotation):
        used = int((sizes > 0).sum())
        fixed = max(1, used // 4)
        moved = fixed + (places - fixed + rotation * (used - fixed)) % max(1, amount - fixed)
        return jnp.zeros((amount,), jnp.int32).at[sequence[jnp.where(places < fixed, places, moved)]].set(jnp.asarray(sizes, jnp.int32))

    sizes = jnp.where(number % 4 == 0, named(heavy_load, number // 4), named(ordinary, number - number // 4 - 1))
    mixed = jax.random.permutation(jax.random.fold_in(own, 3), amount)
    source_of, sink = mixed[0:amount // 2 * 2:2], mixed[1:amount // 2 * 2:2]
    margin = jnp.minimum(sizes[source_of] - 1, bound - sizes[sink]) // 2
    margin = jnp.where((source_of == sequence[0]) | (sink == sequence[0]) | (sizes[sink] == 0), 0, jnp.maximum(margin, 0))
    moved = jax.random.randint(jax.random.fold_in(own, 4), (amount // 2,), 0, 1 << 20) % (margin + 1)
    sizes = sizes.at[source_of].add(-moved).at[sink].add(moved)
    items = jnp.searchsorted(jnp.cumsum(sizes), jnp.arange(rows * top), side="right").astype(jnp.int32)
    table = items.reshape(top, rows).T
    table = table[jax.random.permutation(jax.random.fold_in(own, 1), rows)]
    rotation = jax.random.randint(jax.random.fold_in(own, 2), (rows, 1), 0, top)
    return jnp.take_along_axis(table, (jnp.arange(top)[None, :] + rotation) % top, axis=1)


def load_shares(number_of, total, reach, slope, full):
    weights = [(1 << 20) // math.isqrt(standing ** slope) + 1 for standing in range(1, number_of + 1)]
    largest = reach if full else min(reach, max(-(-total // number_of), total * weights[0] // sum(weights)))
    least = 1 if total - largest >= number_of - 1 else 0
    holding, rest = [largest] + [least] * (number_of - 1), total - largest - least * (number_of - 1)
    while rest > 0:
        candidates = [i for i in range(1, number_of) if holding[i] < largest] or [i for i in range(1, number_of) if holding[i] < reach]
        whole, left = sum([weights[i] for i in candidates]), rest
        for i in candidates:
            extra = min(reach - holding[i], max(1, left * weights[i] // whole), rest)
            holding[i] = holding[i] + extra
            rest = rest - extra
    return np.array(holding)


def noise(own_key, shape, width, most, cuts=(), kind=jnp.bfloat16):
    entries = jax.random.normal(own_key, shape, jnp.float32) * width
    if len(cuts) > 0:
        entries = shard_levels(own_key, shape, cuts, -0.22, 0.18) * entries
    return jnp.clip(entries, min=-most, max=most).astype(kind)


def setup_inputs(seed: int = 0) -> dict:
    key_of = jax.random.split(jax.random.key(seed), 21)
    stream_in = draw_stream_in(jax.random.fold_in(key_of[20], 71), 0)
    stream_grad = noise(key_of[1], (TOKENS, D), 1.0, 6.0, ((0, 32),))
    prefix_len = draw_prefix_len(jax.random.fold_in(key_of[20], 71), 0)
    routes_keys = jax.random.split(jax.random.fold_in(key_of[3], 1), TOKENS // TOK_DEV)
    routes_turns = jax.random.permutation(jax.random.fold_in(key_of[3], 3), TOKENS // TOK_DEV)
    routes = jax.vmap(lambda own, number: routed_block(jax.random.fold_in(key_of[3], 2), own, number, TOK_DEV, EXPERTS, TOP_K, CAP, 0))(routes_keys, routes_turns).reshape((TOKENS, TOP_K))
    route_weight = jnp.clip(jnp.exp(math.log(2.0) - 1.3862944 * jax.random.uniform(key_of[4], (TOKENS, TOP_K), jnp.float32) ** shard_levels(key_of[4], (TOKENS, TOP_K), ((0, 32),), -0.2, 0.2)), 0.5, 2.0)
    attn_gain = jnp.clip(1.0 + 0.1 * jax.random.normal(key_of[5], (D,), jnp.float32), 0.5, 1.5).astype(jnp.bfloat16)
    query_proj = noise(key_of[6], (D, H * (DN + DR)), D ** -0.5, 0.125, ((0, 2),))
    latent_proj = noise(key_of[7], (D, KVR), D ** -0.5, 0.125, ((0, 2),))
    rope_key_proj = noise(key_of[8], (D, DR), D ** -0.5, 0.125, ((0, 2),))
    latent_gain = jnp.clip(1.0 + 0.1 * jax.random.normal(key_of[9], (KVR,), jnp.float32), 0.5, 1.5).astype(jnp.bfloat16)
    kv_up_proj = noise(key_of[10], (KVR, H * (DN + DV)), KVR ** -0.5, 0.25, ((0, 2),))
    out_proj = noise(key_of[11], (H * DV, D), (H * DV * 8 // SEQ_LEN) ** -0.5, 0.75, ((0, 2),))
    ffn_gain = jnp.clip(1.0 + 0.1 * jax.random.normal(key_of[12], (D,), jnp.float32), 0.5, 1.5).astype(jnp.bfloat16)
    router_proj = noise(key_of[13], (D, EXPERTS), 0.011, 0.06591797, ((0, 2),))
    shared_gate = noise(key_of[14], (D, FS), D ** -0.5, 0.125, ((0, 32),))
    shared_up = noise(key_of[15], (D, FS), D ** -0.5, 0.125, ((0, 32),))
    shared_down = noise(key_of[16], (FS, D), FS ** -0.5, 0.109375, ((0, 32),))
    expert_gate = noise(key_of[17], (EXPERTS, D, FE), D ** -0.5, 0.125, ((0, 16), (2, 2)))
    expert_up = noise(key_of[18], (EXPERTS, D, FE), D ** -0.5, 0.125, ((0, 16), (2, 2)))
    expert_down = noise(key_of[19], (EXPERTS, FE, D), FE ** -0.5, 0.15625, ((0, 16), (1, 2)))
    return {"stream_in": stream_in, "stream_grad": stream_grad, "prefix_len": prefix_len, "routes": routes, "route_weight": route_weight, "attn_gain": attn_gain, "query_proj": query_proj, "latent_proj": latent_proj, "rope_key_proj": rope_key_proj, "latent_gain": latent_gain, "kv_up_proj": kv_up_proj, "out_proj": out_proj, "ffn_gain": ffn_gain, "router_proj": router_proj, "shared_gate": shared_gate, "shared_up": shared_up, "shared_down": shared_down, "expert_gate": expert_gate, "expert_up": expert_up, "expert_down": expert_down}


EPS = 1e-06
ROPE_BASE = 10000.0
MASKED = -1e+30
HIGH = lax.Precision.HIGHEST

@jax.custom_vjp
def low(v):
    return lax.optimization_barrier(v.astype(jnp.bfloat16)).astype(jnp.float32)

@jax.custom_vjp
def low_back(v):
    return v

def low_keep(v):
    return (low(v), None)

def low_pass(kept, grad):
    return (grad,)

def back_keep(v):
    return (v, None)

def back_low(kept, grad):
    return (low(grad),)
low.defvjp(low_keep, low_pass)
low_back.defvjp(back_keep, back_low)

def matmul(left, right):
    return jnp.dot(left, right, precision=HIGH, preferred_element_type=jnp.float32)

def rms_scale(values):
    return lax.rsqrt(lax.optimization_barrier(jnp.mean(values * values, axis=-1, keepdims=True)) + EPS)

def rope_tables(positions, rope_width):
    frequency = ROPE_BASE ** (-2.0 * jnp.arange(rope_width // 2, dtype=jnp.float32) / rope_width)
    angles = positions.astype(jnp.float32)[:, None] * frequency[None, :]
    return (jnp.cos(angles), jnp.sin(angles))

def rotate(values, cosine, sine_vals):
    half_dim = values.shape[-1] // 2
    low_half = values[..., :half_dim]
    high_half = values[..., half_dim:]
    return jnp.concatenate([low_half * cosine - high_half * sine_vals, high_half * cosine + low_half * sine_vals], axis=-1)

def attend(pieces):
    query_nope, query_rot, key_nope, key_rot, values, prefix = pieces
    positions = jnp.arange(SEQ_LEN)
    allowed = (positions[None, :] <= positions[:, None]) | (positions[None, :] < prefix)
    scores = jnp.einsum('qhd,khd->hqk', query_nope, key_nope, precision=HIGH)
    scores = scores + jnp.einsum('qhd,kd->hqk', query_rot, key_rot, precision=HIGH)
    scores = low_back(scores * (DN + DR) ** (-0.5))
    probs = jax.nn.softmax(jnp.where(allowed[None], scores, MASKED), axis=-1)
    return jnp.einsum('hqk,khd->qhd', low(probs), values, precision=HIGH)

def expert_apply(pieces):
    rows_in, gate_mat, up_mat, down_mat = pieces
    part_width = FE // N_SHARD
    total = jnp.zeros((rows_in.shape[0], D), jnp.float32)
    for shard_part in range(N_SHARD):
        lo_col = shard_part * part_width
        part_rows = low_back(rows_in)
        gate_val = low_back(matmul(part_rows, gate_mat[:, lo_col:lo_col + part_width]))
        up_val = low_back(matmul(part_rows, up_mat[:, lo_col:lo_col + part_width]))
        hidden = low(jax.nn.silu(gate_val) * up_val)
        total = total + low(matmul(hidden, down_mat[lo_col:lo_col + part_width, :]))
    return low_back(total)

def seqs_view(array_in):
    return array_in.reshape((SEQS, SEQ_LEN) + array_in.shape[1:])

def forward(prefix_len, routes, route_weight, stream, attn_gain, query_proj, latent_proj, rope_key_proj, latent_gain, kv_up_proj, out_proj, ffn_gain, router_proj, shared_gate, shared_up, shared_down, expert_gate, expert_up, expert_down):
    tokens = stream.shape[0]
    positions = jnp.arange(tokens) % SEQ_LEN
    cosine, sine_vals = rope_tables(positions, DR)
    normed = low(stream * rms_scale(stream) * attn_gain)
    query = low_back(matmul(normed, query_proj)).reshape(tokens, H, DN + DR)
    query_nope = low(query[:, :, :DN])
    query_rot = low(rotate(query[:, :, DN:], cosine[:, None], sine_vals[:, None]))
    latent = low_back(matmul(normed, latent_proj))
    latent_normed = low(latent * rms_scale(latent) * latent_gain)
    keyval = low(low_back(matmul(latent_normed, kv_up_proj))).reshape(tokens, H, DN + DV)
    key_rot = low(rotate(low_back(matmul(normed, rope_key_proj)), cosine, sine_vals))
    attended = lax.map(jax.checkpoint(attend), (seqs_view(query_nope), seqs_view(query_rot), seqs_view(keyval[:, :, :DN]), seqs_view(key_rot), seqs_view(keyval[:, :, DN:]), prefix_len))
    attended = low_back(low(attended.reshape(tokens, H * DV)))
    attn_out = low_back(matmul(attended, out_proj))
    mid = stream + attn_out
    normed_two = low(mid * rms_scale(mid) * ffn_gain)
    router_prob = jax.nn.softmax(low_back(matmul(normed_two, router_proj)), axis=-1)
    one_hot = (routes[:, :, None] == jnp.arange(EXPERTS)[None, None, :]).astype(jnp.float32)
    picked = lax.optimization_barrier(jnp.sum(one_hot * router_prob[:, None, :], axis=-1))
    gates = route_weight * picked / lax.optimization_barrier(jnp.sum(picked, axis=-1, keepdims=True))
    shared_gate_val = low_back(matmul(normed_two, shared_gate))
    shared_up_val = low_back(matmul(normed_two, shared_up))
    shared_hidden = low(jax.nn.silu(shared_gate_val) * shared_up_val)
    shared_out = matmul(shared_hidden, shared_down)
    flat_routes = routes.reshape(-1)
    route_hot = (flat_routes[:, None] == jnp.arange(EXPERTS)[None, :]).astype(jnp.int32)
    route_rank = lax.optimization_barrier(jnp.sum((jnp.cumsum(route_hot, axis=0) - route_hot) * route_hot, axis=1)).astype(jnp.int32)
    slot_count = DEVICES * CAP
    slot_index = (flat_routes.astype(jnp.int32) * slot_count + route_rank).astype(jnp.int32)
    buffer = jnp.zeros((EXPERTS * slot_count, D), jnp.float32).at[slot_index].set(jnp.repeat(normed_two, TOP_K, axis=0))
    expert_sum = lax.map(jax.checkpoint(expert_apply), (buffer.reshape(EXPERTS, slot_count, D), expert_gate, expert_up, expert_down)).reshape(EXPERTS * slot_count, D)
    picked_rows = expert_sum[slot_index].reshape(tokens, TOP_K, D)
    ffn_out = shared_out + lax.optimization_barrier(jnp.sum(gates[:, :, None] * picked_rows, axis=1))
    residual = mid + ffn_out
    stats = jnp.sqrt(jnp.stack([jnp.mean(stream * stream), jnp.mean(attn_out * attn_out), jnp.mean(mid * mid), jnp.mean(ffn_out * ffn_out), jnp.mean(residual * residual)]))
    return (residual, stats)

def reference(stream_in, stream_grad, prefix_len, routes, route_weight, attn_gain, query_proj, latent_proj, rope_key_proj, latent_gain, kv_up_proj, out_proj, ffn_gain, router_proj, shared_gate, shared_up, shared_down, expert_gate, expert_up, expert_down):
    floats = tuple((array_in.astype(jnp.float32) for array_in in (stream_in, attn_gain, query_proj, latent_proj, rope_key_proj, latent_gain, kv_up_proj, out_proj, ffn_gain, router_proj, shared_gate, shared_up, shared_down, expert_gate, expert_up, expert_down)))
    residual, pullback, stats = jax.vjp(partial(forward, prefix_len, routes, route_weight), *floats, has_aux=True)
    grads = pullback(stream_grad.astype(jnp.float32))
    return (residual.astype(jnp.bfloat16), grads[0].astype(jnp.bfloat16), stats, grads[1], grads[2], grads[3], grads[4], grads[5], grads[6], grads[7], grads[8], grads[9], grads[10], grads[11], grads[12], grads[13], grads[14], grads[15])
```

```python
import functools
import jax
import jax.numpy as jnp
from jax import lax
from jax.experimental import pallas as pl
from jax.experimental.pallas import tpu as pltpu
from jax.sharding import PartitionSpec as P

D = 2048
H = 16
DN = 128
DR = 64
DV = 128
TOP_K = 6


EPS = 1e-06
ROPE_BASE = 10000.0
MASKED = -1e30


def wide_product(left, right):
    return jnp.dot(left, right, preferred_element_type=jnp.float32)


def contract(left, right, over, batch=((), ())):
    return lax.dot_general(left, right, (over, batch), preferred_element_type=jnp.float32)


def dot_nt(left, right):
    return contract(left, right, ((1,), (1,)))


def dot_tn(left, right):
    return contract(left, right, ((0,), (0,)))


def rms_scale(values):
    return lax.rsqrt(jnp.mean(values * values, axis=-1, keepdims=True) + EPS)


def norm_back(grad_out, inputs, row_scale, gain_vec):
    weighted = grad_out * gain_vec
    inner_mean = jnp.mean(weighted * inputs, axis=-1, keepdims=True)
    grad_in = row_scale * weighted - inputs * (row_scale * row_scale * row_scale) * inner_mean
    grad_gain = jnp.sum(grad_out * inputs * row_scale, axis=0)
    return (grad_in, grad_gain)


def rope_tables(positions, rope_width):
    frequency = ROPE_BASE ** (-2.0 * jnp.arange(rope_width // 2, dtype=jnp.float32) / rope_width)
    angles = positions.astype(jnp.float32)[:, None] * frequency[None, :]
    return (jnp.cos(angles), jnp.sin(angles))


def rotate(values, cosine, sine_vals):
    half_dim = values.shape[-1] // 2
    low_half = values[..., :half_dim]
    high_half = values[..., half_dim:]
    return jnp.concatenate(
        [low_half * cosine - high_half * sine_vals, high_half * cosine + low_half * sine_vals],
        axis=-1,
    )


def swish_derivative(values):
    sigmoid = jax.nn.sigmoid(values)
    return sigmoid * (1.0 + values * (1.0 - sigmoid))


MESH = pl.DeviceIdType.MESH
SEM = pltpu.SemaphoreType.DMA
HBM = pl.BlockSpec(memory_space=pl.ANY)

def when(ok, f):
    if ok is None: f()
    else: pl.when(ok)(f)

def place():
    rep, x = lax.axis_index("rep"), lax.axis_index("shard")
    return rep // 4, lax.rem(rep // 2, 2), lax.rem(rep, 2), x

def device(z, y, c, x):
    return ((z * 2 + y) * 2 + c, x)

def slot(z, y, c, x):
    return ((z * 2 + y) * 2 + c) * 2 + x

def neighbours(nz):
    z, y, c, x = place()
    return dict(
        zr=(device(z + 1, y, c, x), z + 1 < nz),
        zl=(device(z - 1, y, c, x), z >= 1),
        y=(device(z, 1 - y, c, x), None),
        x=(device(z, y, c, 1 - x), None),
        c=(device(z, y, 1 - c, x), None),
    )

def greet(nbr):
    bar = pltpu.get_barrier_semaphore()
    count = 0
    for dev, ok in nbr.values():
        when(ok, lambda dev=dev: pl.semaphore_signal(bar, inc=1, device_id=dev, device_id_type=MESH))
        count = count + (1 if ok is None else jnp.where(ok, 1, 0))
    pl.semaphore_wait(bar, count)

def gather_kernel(nz, x_ref, t_ref, o_ref, ot_ref, own_sem, z_send, y_send, x_send, c_send, recv, crecv):
    z, y, c, x = place()
    nbr = neighbours(nz)
    greet(nbr)
    half = x_ref.shape[0] // 2
    own = slot(z, y, c, x)
    sems = dict(zr=z_send.at[0], zl=z_send.at[1], y=y_send, x=x_send, c=c_send)

    def move(kind, h, b, mine=False):
        if h == 2:
            src, dst = t_ref if mine else ot_ref.at[b], ot_ref.at[b]
        else:
            rows = pl.ds(h * half, half)
            src, dst = x_ref.at[rows] if mine else o_ref.at[b, rows], o_ref.at[b, rows]
        return pltpu.make_async_remote_copy(
            src_ref=src, dst_ref=dst, send_sem=sems[kind].at[h, b],
            recv_sem=(crecv if kind == "c" else recv).at[h, b], device_id=nbr[kind][0], device_id_type=MESH)

    def schedule(go):
        def send(kind, h, b, mine=False):
            def f():
                for hh in (2, 0) if h == 0 else (1,):
                    d = move(kind, hh, b, mine)
                    d.start() if go else d.wait_send()

            when(nbr[kind][1], f)

        def arrive(h, b):
            if go:
                for hh in (2, 0) if h == 0 else (1,):
                    move("x", hh, b).wait_recv()

        second, third = ("y", "x"), ("x", "y")
        for h in (0, 1):
            send("zr", h, own, True)
            send("zl", h, own, True)
            send(second[h], h, own, True)
        for h in (0, 1):
            send(third[h], h, own, True)
            send("c", h, own, True)
        rounds = [[(z, None)]]
        for s in range(nz - 1):
            rounds.append([(z - 1 - s, z - 1 - s >= 0), (z + 1 + s, z + 1 + s < nz)])

        def drain1(rnd):
            for i, (zb, ok) in enumerate(rnd):
                for h in (0, 1):
                    def f(zb=zb, h=h, i=i):
                        b = slot(zb, y, c, x)
                        arrive(h, b)
                        send("zr" if i == 0 else "zl", h, b)
                        send(second[h], h, b)
                        send(third[h], h, b)
                        send("c", h, b)
                    when(ok, f)

        def drain2(rnd):
            for zb, ok in rnd:
                for h in (0, 1):
                    def f(zb=zb, h=h):
                        b = slot(zb, 1 - y, c, x) if h == 0 else slot(zb, y, c, 1 - x)
                        arrive(h, b)
                        send(third[h], h, b)
                        send("c", h, b)
                    when(ok, f)

        def drain3(rnd):
            for zb, ok in rnd:
                for h in (0, 1):
                    def f(zb=zb, h=h):
                        b = slot(zb, y, c, 1 - x) if h == 0 else slot(zb, 1 - y, c, x)
                        arrive(h, b)
                        send("c", h, b)
                        b = slot(zb, 1 - y, c, 1 - x)
                        arrive(h, b)
                        send("c", h, b)
                    when(ok, f)

        for s in range(nz - 1):
            drain1(rounds[s + 1])
            drain2(rounds[s])
            if s >= 1:
                drain3(rounds[s - 1])
        drain2(rounds[nz - 1])
        drain3(rounds[nz - 2])
        drain3(rounds[nz - 1])

    local = [
        pltpu.make_async_copy(x_ref, o_ref.at[own], own_sem.at[0]),
        pltpu.make_async_copy(t_ref, ot_ref.at[own], own_sem.at[1]),
    ]
    for d in local:
        d.start()
    schedule(True)
    for zb in range(nz):
        for yb in range(2):
            for xb in range(2):
                for h in (2, 0, 1):
                    move("c", h, slot(zb, yb, 1 - c, xb)).wait_recv()
    for d in local:
        d.wait()
    schedule(False)


def all_gather(x, t, n, nz, cid):
    return pl.pallas_call(
        functools.partial(gather_kernel, nz),
        out_shape=[jax.ShapeDtypeStruct((n,) + v.shape, v.dtype) for v in (x, t)],
        in_specs=[pl.BlockSpec(memory_space=pl.ANY)] * 2,
        out_specs=[pl.BlockSpec(memory_space=pl.ANY)] * 2,
        scratch_shapes=[SEM((2,)), SEM((2, 3, n)), SEM((3, n)), SEM((3, n)), SEM((3, n)), SEM((3, n)), SEM((3, n))],
        compiler_params=pltpu.CompilerParams(collective_id=cid, has_side_effects=True),
    )(x, t)


def far_first(nz, z):
    def pick(i):
        total = 0
        for k in range(nz):
            ranked = sorted(range(nz), key=lambda d: (-abs(d - k), -d if k < nz // 2 else d))
            total = total + jnp.where(z == k, ranked[i], 0)
        return total
    return [pick(i) for i in range(nz)]

def add_rows(total, other, lo, other_lo, count):
    step = 16 if count % 16 == 0 else 8
    def body(i, carry):
        r = pl.ds(pl.multiple_of(lo + i * step, step), step)
        s = pl.ds(pl.multiple_of(other_lo + i * step, step), step)
        total[r] = (total[r].astype(jnp.float32) + other[s].astype(jnp.float32)).astype(total.dtype)
        return carry
    lax.fori_loop(0, count // step, body, 0)

def scatter_kernel(nz, lo, x_ref, o_ref, mine, core, one, two, line, load_sem, core_send, core_recv, one_send, one_recv, two_send, two_recv, line_send, line_recv):
    z, y, c, x = place()
    nbr = neighbours(nz)
    greet(nbr)
    T = mine.shape[1]
    half = T // 2
    rows = lambda h: pl.ds(h * half, half)
    place_of = lambda zb, yb, xb: (zb * 2 + yb) * 2 + xb
    cols = pl.ds(lo, mine.shape[2])
    order = far_first(nz, z)
    combos = [(1 - y, 1 - x), (y, 1 - x), (1 - y, x), (y, x)]

    def core_copy(zb, yb, xb):
        k = place_of(zb, yb, xb)
        return remote(x_ref.at[slot(zb, yb, 1 - c, xb), :, cols], core.at[k], core_send.at[k], core_recv.at[k], nbr["c"][0])

    def load(zb, yb, xb):
        k = place_of(zb, yb, xb)
        return pltpu.make_async_copy(x_ref.at[slot(zb, yb, c, xb), :, cols], mine.at[k], load_sem.at[k])

    def one_copy(h, zb, j):
        k = place_of(zb, j, 1 - x) if h == 0 else place_of(zb, 1 - y, j)
        i = zb * 2 + j
        return remote(mine.at[k, rows(h)], one.at[h, i], one_send.at[h, i], one_recv.at[h, i], nbr["x" if h == 0 else "y"][0])

    def two_copy(h, zb):
        k = place_of(zb, 1 - y, x) if h == 0 else place_of(zb, y, 1 - x)
        return remote(mine.at[k, rows(h)], two.at[h, zb], two_send.at[h, zb], two_recv.at[h, zb], nbr["y" if h == 0 else "x"][0])

    def line_copy(h, zb, right):
        k = place_of(zb, y, x)
        d = 0 if right else 1
        return remote(mine.at[k, rows(h)], line.at[d, h, zb], line_send.at[h, zb], line_recv.at[d, h, zb], nbr["zr" if right else "zl"][0])

    for zb in order:
        for yb, xb in combos:
            core_copy(zb, yb, xb).start()
            load(zb, yb, xb).start()

    def stage0(zb):
        for n, (yb, xb) in enumerate(combos):
            k = place_of(zb, yb, xb)
            core_copy(zb, yb, xb).wait_recv()
            load(zb, yb, xb).wait()
            add_rows(mine.at[k], core.at[k], 0, 0, T)
            if n in (0, 1):
                one_copy(0, zb, yb).start()
            if n in (0, 2):
                one_copy(1, zb, xb).start()

    def stage1(zb):
        for far in (True, False):
            for h in (0, 1):
                j = (1 - y if far else y) if h == 0 else (1 - x if far else x)
                one_copy(h, zb, j).wait_recv()
                k = place_of(zb, j, x) if h == 0 else place_of(zb, y, j)
                add_rows(mine.at[k], one.at[h, zb * 2 + j], h * half, 0, half)
                if far:
                    two_copy(h, zb).start()

    def stage2(zb):
        k = place_of(zb, y, x)
        for h in (0, 1):
            two_copy(h, zb).wait_recv()
            add_rows(mine.at[k], two.at[h, zb], h * half, 0, half)
            def go(right, h=h):
                line_copy(h, zb, right).wait_recv()
                add_rows(mine.at[k], line.at[0 if right else 1, h, zb], h * half, 0, half)
            when(jnp.logical_and(zb > z, z >= 1), lambda: go(True))
            when(jnp.logical_and(zb < z, z + 1 < nz), lambda: go(False))
            when(zb > z, lambda: line_copy(h, zb, True).start())
            when(zb < z, lambda: line_copy(h, zb, False).start())

    for i in range(nz + 2):
        if i < nz: stage0(order[i])
        if 1 <= i < nz + 1: stage1(order[i - 1])
        if 2 <= i: stage2(order[i - 2])
    k = place_of(z, y, x)
    for h in (0, 1):
        lo = h * half
        o_ref[rows(h)] = mine[k, rows(h)].astype(jnp.float32)
        for d, ok in ((0, z >= 1), (1, z + 1 < nz)):
            def fin(d=d, h=h):
                line_copy(h, z, d == 0).wait_recv()
                o_ref[rows(h)] += line[d, h, z].astype(jnp.float32)
            when(ok, fin)
    for zb in order:
        for yb, xb in combos:
            core_copy(zb, yb, xb).wait_send()
        for h in (0, 1):
            for j in (0, 1):
                one_copy(h, zb, j).wait_send()
            two_copy(h, zb).wait_send()
            when(zb > z, lambda: line_copy(h, zb, True).wait_send())
            when(zb < z, lambda: line_copy(h, zb, False).wait_send())

def reduce_scatter(x, nz, cid):
    N, T, D = x.shape
    sem = pltpu.SemaphoreType.DMA
    bf = x.dtype
    parts = max(1, N // 32)
    W = D // parts
    outs = [
        pl.pallas_call(
            functools.partial(scatter_kernel, nz, i * W),
            out_shape=jax.ShapeDtypeStruct((T, W), jnp.float32),
            in_specs=[pl.BlockSpec(memory_space=pl.ANY)],
            out_specs=pl.BlockSpec(memory_space=pltpu.VMEM),
            scratch_shapes=[
                pltpu.VMEM((N // 2, T, W), bf), pltpu.VMEM((N // 2, T, W), bf),
                pltpu.VMEM((2, 2 * nz, T // 2, W), bf), pltpu.VMEM((2, nz, T // 2, W), bf),
                pltpu.VMEM((2, 2, nz, T // 2, W), bf),
                sem((N // 2,)), sem((N // 2,)), sem((N // 2,)), sem((2, 2 * nz)), sem((2, 2 * nz)),
                sem((2, nz)), sem((2, nz)), sem((2, nz)), sem((2, 2, nz))],
            compiler_params=pltpu.CompilerParams(
                collective_id=cid + i, has_side_effects=True, vmem_limit_bytes=48 << 20
            ),
        )(x)
        for i in range(parts)
    ]
    return outs[0] if parts == 1 else jnp.concatenate(outs, axis=1)


def remote(src, dst, send_sem, recv_sem, dev):
    return pltpu.make_async_remote_copy(
        src_ref=src, dst_ref=dst, send_sem=send_sem, recv_sem=recv_sem, device_id=dev, device_id_type=MESH
    )


def quad_neighbours():
    z, y, c, x = place()
    return dict(x=(device(z, y, c, 1 - x), None), c=(device(z, y, 1 - c, x), None))


def open_kernel(stream, wq, kv, lat, tiny, stream_all, wq_o, kv_o, lat_o, tiny_o, b0, b1, b2, b3, b4, load, store, send, recv):
    z, y, c, x = place()
    nbr = quad_neighbours()
    greet(nbr)
    own, side = c * 2 + x, c * 2 + 1 - x
    rows = lat.shape[0] // 2
    mine = pl.ds(pl.multiple_of(c * rows, rows), rows)
    xdev, cdev = nbr["x"][0], nbr["c"][0]

    def heads(ref, out, xx):
        n = out.shape[2]
        return ref.at[:, pl.ds(pl.multiple_of((xx * 2 + c) * n, 128), n)]

    xs = [
        remote(stream, stream_all.at[own], send.at[0], recv.at[0], xdev),
        remote(tiny, tiny_o.at[x], send.at[1], recv.at[1], xdev),
        remote(lat.at[mine], lat_o.at[x, mine], send.at[2], recv.at[2], xdev),
        remote(heads(kv, kv_o, 1 - x), kv_o.at[x], send.at[3], recv.at[3], xdev),
        remote(heads(wq, wq_o, 1 - x), wq_o.at[x], send.at[4], recv.at[4], xdev),
    ]
    for d in xs:
        d.start()
    cs = [remote(stream, stream_all.at[own], send.at[5], recv.at[5], cdev)]
    cs[0].start()
    here = [
        (stream, b0, stream_all.at[own]), (tiny, b4, tiny_o.at[x]), (lat, b3, lat_o.at[x]),
        (heads(kv, kv_o, x), b2, kv_o.at[x]), (heads(wq, wq_o, x), b1, wq_o.at[x]),
    ]
    for i, (a, b, o) in enumerate(here):
        pltpu.make_async_copy(a, b, load.at[i]).start()
    for i, (a, b, o) in enumerate(here):
        pltpu.make_async_copy(a, b, load.at[i]).wait()
        pltpu.make_async_copy(b, o, store.at[i]).start()
    xs[0].wait_recv()
    cs.append(remote(stream_all.at[side], stream_all.at[side], send.at[6], recv.at[6], cdev))
    cs[1].start()
    xs[1].wait_recv()
    xs[2].wait_recv()
    cs.append(remote(lat_o.at[1 - x, mine], lat_o.at[1 - x, mine], send.at[7], recv.at[7], cdev))
    cs[2].start()
    xs[3].wait_recv()
    xs[4].wait_recv()
    for d in cs:
        d.wait_recv()
    for i, (a, b, o) in enumerate(here):
        pltpu.make_async_copy(b, o, store.at[i]).wait()
    for d in xs + cs:
        d.wait_send()


def open_quad(stream, wq, kv, lat, tiny, cid):
    sd = jax.ShapeDtypeStruct
    ins = (stream, wq, kv, lat, tiny)
    shapes = [(4,) + stream.shape, (2, wq.shape[0], wq.shape[1] // 4), (2, kv.shape[0], kv.shape[1] // 4), (2,) + lat.shape, (2,) + tiny.shape]
    return pl.pallas_call(
        open_kernel,
        out_shape=[sd(shape, v.dtype) for shape, v in zip(shapes, ins)],
        in_specs=[HBM] * 5,
        out_specs=[HBM] * 5,
        scratch_shapes=[pltpu.VMEM(shape[1:], v.dtype) for shape, v in zip(shapes, ins)] + [SEM((5,)), SEM((5,)), SEM((8,)), SEM((8,))],
        compiler_params=pltpu.CompilerParams(collective_id=cid, has_side_effects=True, vmem_limit_bytes=16 << 20),
    )(*ins)


def quad_gather_kernel(x_ref, o_ref, local, send, recv):
    z, y, c, x = place()
    nbr = quad_neighbours()
    greet(nbr)
    own, side = c * 2 + x, c * 2 + 1 - x
    half = x_ref.shape[0] // 2
    copies = []
    for h in (0, 1):
        r = pl.ds(h * half, half)
        a = remote(x_ref.at[r], o_ref.at[own, r], send.at[0, h], recv.at[0, h], nbr["x"][0])
        b = remote(x_ref.at[r], o_ref.at[own, r], send.at[1, h], recv.at[1, h], nbr["c"][0])
        d = remote(o_ref.at[side, r], o_ref.at[side, r], send.at[2, h], recv.at[2, h], nbr["c"][0])
        a.start()
        b.start()
        copies.append((a, b, d))
    here = pltpu.make_async_copy(x_ref, o_ref.at[own], local)
    here.start()
    for a, b, d in copies:
        a.wait_recv()
        d.start()
    for a, b, d in copies:
        b.wait_recv()
        d.wait_recv()
        a.wait_send()
        b.wait_send()
        d.wait_send()
    here.wait()


def quad_gather(v, cid):
    return pl.pallas_call(
        quad_gather_kernel,
        out_shape=jax.ShapeDtypeStruct((4,) + v.shape, v.dtype),
        in_specs=[HBM],
        out_specs=HBM,
        scratch_shapes=[SEM, SEM((3, 2)), SEM((3, 2))],
        compiler_params=pltpu.CompilerParams(collective_id=cid, has_side_effects=True),
    )(v)


def quad_scatter_kernel(v_ref, o_ref, mine, core, far, load, send, recv):
    z, y, c, x = place()
    nbr = quad_neighbours()
    greet(nbr)
    half = o_ref.shape[0] // 2
    steps = []
    for h in (0, 1):
        r = pl.ds(h * half, half)
        for j, xb in ((0, 1 - x), (1, x)):
            a = remote(v_ref.at[(1 - c) * 2 + xb, r], core.at[j, r], send.at[j, h], recv.at[j, h], nbr["c"][0])
            b = pltpu.make_async_copy(v_ref.at[c * 2 + xb, r], mine.at[j, r], load.at[j, h])
            a.start()
            b.start()
            steps.append((a, b))
    outs = []
    for h in (0, 1):
        r = pl.ds(h * half, half)
        a, b = steps[2 * h]
        a.wait_recv()
        b.wait()
        add_rows(mine.at[0], core.at[0], h * half, h * half, half)
        f = remote(mine.at[0, r], far.at[r], send.at[2, h], recv.at[2, h], nbr["x"][0])
        f.start()
        outs.append(f)
    for h in (0, 1):
        a, b = steps[2 * h + 1]
        a.wait_recv()
        b.wait()
        outs[h].wait_recv()
        def body(i, carry, h=h):
            r = pl.ds(pl.multiple_of(h * half + i * 16, 16), 16)
            o_ref[r] = (mine[1, r].astype(jnp.float32) + core[1, r].astype(jnp.float32)) + far[r].astype(jnp.float32)
            return carry
        lax.fori_loop(0, half // 16, body, 0)
    for a, b in steps:
        a.wait_send()
    for f in outs:
        f.wait_send()


def quad_scatter(v, cid):
    _, rows, cols = v.shape
    buf = pltpu.VMEM((2, rows, cols), v.dtype)
    return pl.pallas_call(
        quad_scatter_kernel,
        out_shape=jax.ShapeDtypeStruct((rows, cols), jnp.float32),
        in_specs=[HBM],
        out_specs=pl.BlockSpec(memory_space=pltpu.VMEM),
        scratch_shapes=[buf, buf, pltpu.VMEM((rows, cols), v.dtype), SEM((2, 2)), SEM((3, 2)), SEM((3, 2))],
        compiler_params=pltpu.CompilerParams(
            collective_id=cid, has_side_effects=True, vmem_limit_bytes=24 << 20
        ),
    )(v)


def owners_kernel(nz, na, *refs):
    ins, rest = refs[:na], refs[na:]
    outs, rest = rest[:na], rest[na:]
    mine, rest = rest[:na], rest[na:]
    one, rest = rest[:na], rest[na:]
    line, rest = rest[:na], rest[na:]
    total, rest = rest[:na], rest[na:]
    load, one_send, one_recv, line_send, line_recv, own_sem, q_send, q_recv = rest
    z, y, c, x = place()
    nbr = neighbours(nz)
    nbr["d"] = (device(z, y, 1 - c, 1 - x), None)
    greet(nbr)
    order = far_first(nz, z)
    xdev, cdev, ddev, ydev = (nbr[k][0] for k in ("x", "c", "d", "y"))

    def loads(a, zb, yb):
        k = zb * 2 + yb
        return pltpu.make_async_copy(ins[a].at[k], mine[a].at[k], load.at[a, k])

    def one_copy(a, zb):
        return remote(mine[a].at[zb * 2 + 1 - y], one[a].at[zb], one_send.at[a, zb], one_recv.at[a, zb], ydev)

    def line_copy(a, zb, right):
        d = 0 if right else 1
        return remote(
            mine[a].at[zb * 2 + y], line[a].at[d, zb], line_send.at[a, zb], line_recv.at[d, a, zb],
            nbr["zr" if right else "zl"][0],
        )

    for zb in order:
        for a in range(na):
            loads(a, zb, 1 - y).start()
        for a in range(na):
            loads(a, zb, y).start()
    for zb in order:
        for a in range(na):
            loads(a, zb, 1 - y).wait()
            one_copy(a, zb).start()
    for zb in order:
        for a in range(na):
            rows = mine[a].shape[1]
            k = zb * 2 + y
            loads(a, zb, y).wait()
            one_copy(a, zb).wait_recv()
            add_rows(mine[a].at[k], one[a].at[zb], 0, 0, rows)

            def go(right):
                line_copy(a, zb, right).wait_recv()
                add_rows(mine[a].at[k], line[a].at[0 if right else 1, zb], 0, 0, rows)

            when(jnp.logical_and(zb > z, z >= 1), lambda: go(True))
            when(jnp.logical_and(zb < z, z + 1 < nz), lambda: go(False))
            when(zb > z, lambda: line_copy(a, zb, True).start())
            when(zb < z, lambda: line_copy(a, zb, False).start())
    k = z * 2 + y
    member, group = c * 2 + x, x * 2 + c
    sends = []
    for a in range(na):
        rows = mine[a].shape[1]

        def fin(right):
            line_copy(a, z, right).wait_recv()
            add_rows(mine[a].at[k], line[a].at[0 if right else 1, z], 0, 0, rows)

        when(z >= 1, lambda: fin(True))
        when(z + 1 < nz, lambda: fin(False))
        if a < na - 1 and outs[a].shape[0] != 4:
            d = pltpu.make_async_copy(mine[a].at[k], outs[a], own_sem.at[a])
            d.start()
            sends.append((d, None))
            continue
        part = outs[a].shape[1] if a < na - 1 else rows
        whole = part == rows
        dst = total[a] if a == na - 1 else outs[a]

        def piece(m):
            return mine[a].at[k] if whole else mine[a].at[k, pl.ds(m * part, part)]

        d = pltpu.make_async_copy(piece(member), dst.at[group], own_sem.at[a])
        d.start()
        sends.append((d, None))
        for i, (dev, cc, xx) in enumerate(((xdev, c, 1 - x), (cdev, 1 - c, x), (ddev, 1 - c, 1 - x))):
            d = remote(piece(cc * 2 + xx), dst.at[group], q_send.at[a, i], q_recv.at[a, i], dev)
            d.start()
            sends.append((d, True))
    for d, far in sends:
        d.wait()
    outs[na - 1][...] = total[na - 1][0] + total[na - 1][1] + total[na - 1][2] + total[na - 1][3]
    for zb in order:
        for a in range(na):
            one_copy(a, zb).wait_send()
            when(zb > z, lambda: line_copy(a, zb, True).wait_send())
            when(zb < z, lambda: line_copy(a, zb, False).wait_send())


def to_owners(arrays, spread, nz, cid):
    na = len(arrays)
    shapes, specs = [], []
    for a, v in enumerate(arrays):
        _, rows, cols = v.shape
        if a == na - 1:
            shapes.append(jax.ShapeDtypeStruct((rows, cols), v.dtype))
            specs.append(pl.BlockSpec(memory_space=pltpu.VMEM))
            continue
        if spread[a]:
            shapes.append(jax.ShapeDtypeStruct((4, rows // 4 if rows % 64 == 0 else rows, cols), v.dtype))
        else:
            shapes.append(jax.ShapeDtypeStruct((rows, cols), v.dtype))
        specs.append(HBM)
    last = arrays[-1].shape
    return pl.pallas_call(
        functools.partial(owners_kernel, nz, na),
        out_shape=shapes,
        in_specs=[HBM] * na,
        out_specs=specs,
        scratch_shapes=[pltpu.VMEM(v.shape, v.dtype) for v in arrays]
        + [pltpu.VMEM((nz,) + v.shape[1:], v.dtype) for v in arrays]
        + [pltpu.VMEM((2, nz) + v.shape[1:], v.dtype) for v in arrays]
        + [pltpu.VMEM((4,) + (last[1:] if a == na - 1 else (8, 128)), jnp.float32) for a in range(na)]
        + [SEM((na, 2 * nz)), SEM((na, nz)), SEM((na, nz)), SEM((na, nz)), SEM((2, na, nz)), SEM((na,)), SEM((na, 3)), SEM((na, 3))],
        compiler_params=pltpu.CompilerParams(
            collective_id=cid, has_side_effects=True, vmem_limit_bytes=40 << 20
        ),
    )(*arrays)


def experts_kernel(nt_ref, sg_ref, slot_ref, gate_ref, wg_ref, wu_ref, wd_ref, ws_ref, wsd_ref,
                   out_ref, ng_ref, dwg_hbm, dwu_hbm, dwd_hbm, dws_ref, dsd_ref,
                   dwg, dwu, dwd, sem, *, slots):
    f32, b16 = jnp.float32, jnp.bfloat16
    i = pl.program_id(0)
    @pl.when(i == 0)
    def _():
        for r in (dwg, dwu, dwd, dws_ref, dsd_ref):
            r[...] = jnp.zeros_like(r)
    tokens = nt_ref.shape[0] * nt_ref.shape[1]
    width = nt_ref.shape[2]
    nt = nt_ref[...].reshape(tokens, width)
    sg = sg_ref[...].reshape(tokens, width)
    hit = lax.broadcasted_iota(jnp.int32, (slots, tokens), 0) == slot_ref[0]
    pick = hit.astype(f32).astype(b16)
    x = wide_product(pick, nt).astype(b16)
    g0 = wide_product(pick, sg)
    gate = jnp.sum(jnp.where(hit, gate_ref[0], 0.0), axis=1, keepdims=True)
    g = (gate * g0).astype(b16)
    gv = dot_nt(x, wg_ref[...])
    uv = dot_nt(x, wu_ref[...])
    sig = jax.nn.sigmoid(gv)
    act = gv * sig
    hid = (act * uv).astype(b16)
    part = wide_product(hid, wd_ref[...])
    gg = jnp.sum(g0 * part, axis=1, keepdims=True)
    gg_high = gg.astype(b16).astype(f32)
    column = lax.axis_index("rep") * 4 + lax.axis_index("shard") * 2
    lane = lax.broadcasted_iota(jnp.int32, (slots, 128), 1)
    gg = jnp.where(lane == column, gg_high, jnp.where(lane == column + 1, gg - gg_high, 0.0)).astype(b16)
    e_out = (gate * part).astype(b16)
    dwd[...] += dot_tn(hid, g)
    hg = dot_nt(g, wd_ref[...])
    dg = (hg * uv * (sig * (1.0 + gv * (1.0 - sig)))).astype(b16)
    du = (hg * act).astype(b16)
    dwg[...] += dot_tn(dg, x)
    dwu[...] += dot_tn(du, x)
    ing = (wide_product(dg, wg_ref[...]) + wide_product(du, wu_ref[...])).astype(b16)
    fs = wsd_ref.shape[0]
    s = dot_nt(nt, ws_ref[...])
    sgv, suv = s[:, :fs], s[:, fs:]
    ssig = jax.nn.sigmoid(sgv)
    sact = sgv * ssig
    sh = (sact * suv).astype(b16)
    shg = dot_nt(sg, wsd_ref[...])
    dsg = (shg * suv * (ssig * (1.0 + sgv * (1.0 - ssig))))
    dsu = (shg * sact)
    ds = jnp.concatenate([dsg, dsu], axis=1).astype(b16)
    dsd_ref[...] += dot_tn(sh, sg)
    dws_ref[...] += dot_tn(ds, nt)
    out = wide_product(sh, wsd_ref[...]) + dot_tn(pick, e_out)
    out_ref[...] = out.astype(b16).reshape(out_ref.shape)
    ng = wide_product(ds, ws_ref[...]) + dot_tn(pick, ing)
    ng_ref[:, :, :width] = ng.astype(b16).reshape(nt_ref.shape)
    ng_ref[:, :, width:] = dot_tn(pick, gg).astype(b16).reshape(ng_ref.shape[:2] + (128,))
    @pl.when(i == pl.num_programs(0) - 1)
    def _():
        cs = [pltpu.make_async_copy(a, b, sem.at[j]) for j, (a, b) in enumerate(((dwg, dwg_hbm), (dwu, dwu_hbm), (dwd, dwd_hbm)))]
        for c in cs: c.start()
        for c in cs: c.wait()

def experts_both(nt, sg, slot, gate, wg, wu, wd, ws, wsd, capacity, blocks=4):
    n, tok, width = nt.shape
    steps = n // blocks
    f = wg.shape[0]; fs = wsd.shape[0]
    f32 = jnp.float32
    one = lambda a: pl.BlockSpec(a.shape, lambda i: (0,) * a.ndim, pipeline_mode=pl.Buffered(1))
    blk = pl.BlockSpec((blocks, tok, width), lambda i: (i, 0, 0))
    row = pl.BlockSpec((1, 1, blocks * tok), lambda i: (i, 0, 0))
    sd = jax.ShapeDtypeStruct
    anyspec = HBM
    acc = pltpu.VMEM((f, width), f32)
    return pl.pallas_call(
        functools.partial(experts_kernel, slots=blocks * capacity),
        grid=(steps,),
        in_specs=[blk, blk, row, row] + [one(w) for w in (wg, wu, wd, ws, wsd)],
        out_specs=[blk, pl.BlockSpec((blocks, tok, width + 128), lambda i: (i, 0, 0)), anyspec, anyspec, anyspec,
                   pl.BlockSpec((2 * fs, width), lambda i: (0, 0)), pl.BlockSpec((fs, width), lambda i: (0, 0))],
        out_shape=[sd(nt.shape, nt.dtype), sd((n, tok, width + 128), nt.dtype),
                   sd((f, width), f32), sd((f, width), f32), sd((f, width), f32),
                   sd((2 * fs, width), f32), sd((fs, width), f32)],
        scratch_shapes=[acc, acc, acc, SEM((3,))],
        compiler_params=pltpu.CompilerParams(vmem_limit_bytes=64 << 20, dimension_semantics=("arbitrary",)),
    )(nt, sg, slot.reshape(steps, 1, blocks * tok), gate.reshape(steps, 1, blocks * tok), wg, wu, wd, ws, wsd)


def on_device(
    stream_in, stream_grad, prefix_len, routes, route_weight, attn_gain, query_proj, latent_proj, rope_key_proj,
    latent_gain, kv_up_proj, out_proj, ffn_gain, router_proj, shared_gate, shared_up, shared_down, expert_gate,
    expert_up, expert_down,
):
    f32, b16 = jnp.float32, jnp.bfloat16
    both = ("rep", "shard")
    n_shard, n_rep = lax.axis_size("shard"), lax.axis_size("rep")
    n_dev = n_rep * n_shard
    nz = n_rep // 4
    quads = n_rep // 2
    rep, x = lax.axis_index("rep"), lax.axis_index("shard")
    c = lax.rem(rep, 2)
    member, group = c * 2 + x, x * 2 + c
    tok, width = stream_in.shape
    experts = router_proj.shape[1]
    capacity = max(2, tok * TOP_K * 7 // (6 * experts))
    seq = n_shard * tok
    scale = (DN + DR) ** (-0.5)
    heads = H // 4
    qcols, kcols = heads * (DN + DR), heads * (DN + DV)
    kvr = latent_proj.shape[1]
    lanes = kvr + DR

    dh = width // n_shard
    gl = jnp.pad(latent_gain, (0, dh - kvr // n_shard))
    tiny = jnp.concatenate([rope_key_proj.T, router_proj.T, attn_gain[None], ffn_gain[None], gl[None]], axis=0)
    tiny = jnp.pad(tiny, ((0, -tiny.shape[0] % 16), (0, 0)))
    stream_all, mat_q, mat_kv, mat_lat, tiny = open_quad(stream_in, query_proj, kv_up_proj, latent_proj, tiny, 1)
    mat_q = mat_q.reshape(width, qcols)
    mat_kv = mat_kv.reshape(kvr, kcols)
    mat_lat = mat_lat.reshape(width, kvr)
    joined = jnp.concatenate([tiny[0], tiny[1]], axis=1)
    rope_t, router_t = joined[:DR], joined[DR : DR + experts]
    gain_attn = joined[DR + experts].astype(f32)
    gain_ffn = joined[DR + experts + 1].astype(f32)
    gain_latent = tiny[:, DR + experts + 2, : kvr // n_shard].reshape(kvr).astype(f32)
    mat_out = lax.dynamic_slice_in_dim(out_proj, c * heads * DV, heads * DV, 0)

    grad_all = lax.all_gather(stream_grad, both, axis=0)
    one_hot = (routes[:, :, None] == jnp.arange(experts)[None, None, :]).astype(f32)
    mask = jnp.sum(one_hot, axis=1)
    weight = jnp.sum(one_hot * route_weight[:, :, None], axis=1)
    fs = shared_down.shape[0]
    lanes_s = -(-fs // 128) * 128
    own_w = width // n_dev
    split = jnp.stack([shared_gate, shared_up], axis=1).reshape(own_w, 2, n_dev, fs)
    split = jnp.pad(split, ((0, 0), (0, 0), (0, 0), (0, lanes_s - fs))).transpose(2, 0, 1, 3).reshape(n_dev, own_w, 2 * lanes_s)
    w_s = lax.all_to_all(split, both, split_axis=0, concat_axis=0, tiled=True).reshape(width, 2 * lanes_s).T
    w_sd = jnp.pad(shared_down, ((0, lanes_s - fs), (0, 0)))

    stream4 = stream_all.reshape(4 * tok, width).astype(f32)
    normed = (stream4 * rms_scale(stream4) * gain_attn).astype(b16)
    positions = jnp.arange(seq)
    cosine, sine = rope_tables(positions, DR)
    q_raw = wide_product(normed, mat_q).reshape(2, seq, heads, DN + DR)
    q_nope = q_raw[..., :DN].astype(b16)
    q_rot = rotate(q_raw[..., DN:], cosine[:, None], sine[:, None]).astype(b16)
    latent = wide_product(normed, mat_lat)
    scale_lat = rms_scale(latent)
    latent_normed = (latent * scale_lat * gain_latent).astype(b16)
    k_rot = rotate(dot_nt(normed, rope_t).reshape(2, seq, DR), cosine, sine).astype(b16)
    keyval = wide_product(latent_normed, mat_kv).astype(b16).reshape(2, seq, heads, DN + DV)
    k_nope, values = keyval[..., :DN], keyval[..., DN:]
    prefix = lax.dynamic_slice_in_dim(prefix_len, rep - c, 2)
    allowed = (positions[None, None, :] <= positions[None, :, None]) | (positions[None, None, :] < prefix[:, None, None])
    allowed = allowed[:, None]
    raw = contract(q_nope, k_nope, ((3,), (3,)), ((0, 2), (0, 2)))
    raw = raw + jnp.swapaxes(contract(q_rot, k_rot, ((3,), (2,)), ((0,), (0,))), 1, 2)
    scores = jnp.where(allowed, raw * scale, MASKED)
    expo = jnp.exp(scores - jnp.max(scores, axis=-1, keepdims=True))
    probs = expo / jnp.sum(expo, axis=-1, keepdims=True)
    probs_low = probs.astype(b16)
    attended = jnp.swapaxes(contract(probs_low, values, ((3,), (1,)), ((0, 1), (0, 2))), 1, 2)
    attended = attended.astype(b16).reshape(4 * tok, heads * DV)
    part = wide_product(attended, mat_out).astype(b16).reshape(4, tok, width)
    attn_out = quad_scatter(part, 3)
    stream = stream_in.astype(f32)
    mid = stream + attn_out
    scale_two = rms_scale(mid)
    normed_two = (mid * scale_two * gain_ffn).astype(b16)

    router_prob = jax.nn.softmax(dot_nt(normed_two, router_t), axis=-1)
    picked = mask * router_prob
    picked_sum = jnp.sum(picked, axis=-1, keepdims=True)
    gates = weight * picked / picked_sum
    nt_all, tails = all_gather(normed_two, jnp.concatenate([gates.T, mask.T], axis=0), n_dev, nz, 4)
    gates_e = lax.dynamic_index_in_dim(tails, rep, 1, False)
    mask_e = lax.dynamic_index_in_dim(tails, experts + rep, 1, False)

    blocks = 4
    before = (jnp.arange(tok)[:, None] < jnp.arange(tok)[None, :]).astype(b16)
    rank = wide_product(mask_e.astype(b16), before).astype(jnp.int32)
    first = (jnp.arange(n_dev, dtype=jnp.int32) % blocks * capacity)[:, None]
    place_of = jnp.where(mask_e > 0, first + rank, -1)
    out, n_grad, grad_eg, grad_eu, grad_ed, grad_s, grad_sd = experts_both(
        nt_all, grad_all, place_of, gates_e, jnp.swapaxes(expert_gate, 1, 2)[0], jnp.swapaxes(expert_up, 1, 2)[0],
        expert_down[0], w_s, w_sd, capacity, blocks)
    n_grad = reduce_scatter(n_grad, nz, 16)
    ffn_out = reduce_scatter(out, nz, 24)
    back = lax.all_to_all(grad_s.T.astype(b16).reshape(n_dev, own_w, 2 * lanes_s), both, split_axis=0, concat_axis=0, tiled=True)
    back = back.reshape(n_dev, own_w, 2, lanes_s)[..., :fs].transpose(2, 1, 0, 3).reshape(2, own_w, n_dev * fs).astype(f32)
    gate_grad = jnp.sum(n_grad[:, width : width + 4 * experts].reshape(tok, experts, 4), axis=-1)
    n_grad = n_grad[:, :width]
    residual = mid + ffn_out

    weighted = weight * gate_grad
    picked_grad = weighted / picked_sum - jnp.sum(weighted * picked, axis=-1, keepdims=True) / (picked_sum * picked_sum)
    prob_grad = mask * picked_grad
    logit_grad = (router_prob * (prob_grad - jnp.sum(router_prob * prob_grad, axis=-1, keepdims=True))).astype(b16)
    n_grad = n_grad + wide_product(logit_grad, router_t)
    norm_part, ffn_gain_grad = norm_back(n_grad, mid, scale_two, gain_ffn)
    mid_grad = stream_grad.astype(f32) + norm_part
    aog = mid_grad.astype(b16)
    tail = jnp.pad(logit_grad, ((0, 0), (0, 128 - experts)))
    aog_all = quad_gather(jnp.concatenate([aog, tail], axis=1), 7).reshape(4 * tok, width + 128)
    logit_all = aog_all[:, width : width + experts]
    aog_all = aog_all[:, :width]

    att_grad = dot_nt(aog_all, mat_out).astype(b16)
    grad_out = dot_tn(attended, aog_all)
    att_grad = att_grad.reshape(2, seq, heads, DV)
    value_grad = jnp.swapaxes(contract(probs_low, att_grad, ((2,), (1,)), ((0, 1), (0, 2))), 1, 2)
    prob_grad_a = contract(att_grad, values, ((3,), (3,)), ((0, 2), (0, 2)))
    s_grad = probs * (prob_grad_a - jnp.sum(probs * prob_grad_a, axis=-1, keepdims=True))
    s_grad = s_grad.astype(b16)
    qn_grad = scale * jnp.swapaxes(contract(s_grad, k_nope, ((3,), (1,)), ((0, 1), (0, 2))), 1, 2)
    qr_grad = scale * jnp.swapaxes(contract(s_grad, k_rot, ((3,), (1,)), ((0,), (0,))), 1, 2)
    kn_grad = scale * jnp.swapaxes(contract(s_grad, q_nope, ((2,), (1,)), ((0, 1), (0, 2))), 1, 2)
    kr_grad = scale * contract(s_grad, q_rot, ((1, 2), (2, 1)), ((0,), (0,)))
    keyval_grad = jnp.concatenate([kn_grad, value_grad], axis=-1).astype(b16).reshape(4 * tok, kcols)
    qr_grad = rotate(qr_grad, cosine[:, None], -sine[:, None])
    query_grad = jnp.concatenate([qn_grad, qr_grad], axis=-1).astype(b16).reshape(4 * tok, qcols)
    lat_part = dot_nt(keyval_grad, mat_kv)
    lat_part = jnp.concatenate([lat_part, kr_grad.reshape(4 * tok, DR), jnp.zeros((4 * tok, -lanes % 128), f32)], axis=1)
    lat_sum = jnp.sum(quad_gather(lat_part.astype(b16), 8).astype(f32), axis=0)
    lat_sum, kr_sum = lat_sum[:, :kvr], lat_sum[:, kvr:lanes].reshape(2, seq, DR)
    key_pre = rotate(kr_sum, cosine, -sine).reshape(4 * tok, DR).astype(b16)
    weighted_l = lat_sum * gain_latent
    inner = jnp.mean(weighted_l * latent, axis=-1, keepdims=True)
    latent_pre = scale_lat * weighted_l - latent * (scale_lat * scale_lat * scale_lat) * inner
    lat_gain_rows = lat_sum * latent * scale_lat
    lat_gain_grad = jnp.sum(lax.dynamic_slice_in_dim(lat_gain_rows, member * tok, tok, 0), axis=0)
    lat_grad = jnp.concatenate([latent_pre.astype(b16), key_pre], axis=1)
    part = dot_nt(query_grad, mat_q)
    normed_grad = quad_scatter(part.astype(b16).reshape(4, tok, width), 9)
    lat_own = lax.dynamic_slice_in_dim(lat_grad, member * tok, tok, 0)
    normed_grad = normed_grad + dot_nt(lat_own[:, :kvr], mat_lat) + wide_product(lat_own[:, kvr:], rope_t)
    attn_part, attn_gain_grad = norm_back(normed_grad, stream, rms_scale(stream), gain_attn)
    grad_stream = (mid_grad + attn_part).astype(b16)

    gq = dot_tn(normed, query_grad).astype(b16)
    gkv = dot_tn(latent_normed, keyval_grad).astype(b16)
    cols = lambda v: lax.dynamic_index_in_dim(v.reshape(4 * tok, quads, 4, own_w), member, 2, False).reshape(4 * tok, -1)
    nt_quad = lax.dynamic_slice_in_dim(nt_all, (rep // 2) * 4, 4, 0).reshape(4 * tok, width)
    glat = dot_tn(cols(normed), lat_grad)
    grouter = dot_tn(cols(nt_quad), logit_all)
    glat = jnp.concatenate([glat, grouter, jnp.zeros((glat.shape[0], -(lanes + experts) % 128), f32)], axis=1).astype(b16)
    squares = jnp.stack([jnp.sum(v * v) for v in (stream, attn_out, mid, ffn_out, residual)])
    side = jnp.concatenate(
        [attn_gain_grad.reshape(quads, -1), ffn_gain_grad.reshape(quads, -1), lat_gain_grad.reshape(quads, -1),
         jnp.broadcast_to(squares[None], (quads, 5))], axis=1)
    side = jnp.pad(side, ((0, 0), (0, 1024 - side.shape[1]))).reshape(quads, 8, 128)
    o_q, o_kv, o_out, o_lat, o_side = to_owners(
        [gq.reshape(quads, -1, qcols), gkv.reshape(quads, -1, kcols), grad_out.astype(b16).reshape(quads, -1, width),
         glat.reshape(quads, own_w, -1), side], (True, True, False, False, True), nz, 10)
    o_side = o_side.reshape(-1)
    per = width // quads
    perl = kvr // quads
    ga = lax.dynamic_slice_in_dim(o_side, member * own_w, own_w)
    gf = lax.dynamic_slice_in_dim(o_side, per + member * own_w, own_w)
    gla = lax.dynamic_slice_in_dim(o_side, 2 * per + member * (perl // 4), perl // 4)
    totals = o_side[2 * per + perl : 2 * per + perl + 5]
    stats = jnp.sqrt(totals / (tok * n_dev * width))
    fits = lambda v, rows: v if v.shape[1] == rows else lax.dynamic_slice_in_dim(v, member * rows, rows, 1)
    o_q = jnp.moveaxis(fits(o_q, own_w).astype(f32), 0, 1).reshape(own_w, -1)
    o_kv = jnp.moveaxis(fits(o_kv, kvr // n_dev).astype(f32), 0, 1).reshape(kvr // n_dev, -1)
    pairs = []
    for q in range(quads):
        for cc in range(2):
            for xx in range(2):
                pairs.append((q * 4 + cc * 2 + xx, (xx * 2 + cc) * quads + q))
    o_out = lax.ppermute(o_out, both, pairs).astype(f32)
    o_lat = o_lat.astype(f32)
    return (
        residual.astype(b16), grad_stream, stats, ga, o_q, o_lat[:, :kvr], o_lat[:, kvr:lanes], gla, o_kv, o_out, gf,
        o_lat[:, lanes : lanes + experts], back[0], back[1], grad_sd[:fs], jnp.swapaxes(grad_eg[None], 1, 2), jnp.swapaxes(grad_eu[None], 1, 2), grad_ed[None],
    )


def on_device_weights(
    stream_in,
    stream_grad,
    prefix_len,
    routes,
    route_weight,
    attn_gain,
    query_proj,
    latent_proj,
    rope_key_proj,
    latent_gain,
    kv_up_proj,
    out_proj,
    ffn_gain,
    router_proj,
    shared_gate,
    shared_up,
    shared_down,
    expert_gate,
    expert_up,
    expert_down,
):
    n_shard = lax.axis_size("shard")
    n_rep = lax.axis_size("rep")
    rep_index = lax.axis_index("rep")
    shard_index = lax.axis_index("shard")
    tok_rows = stream_in.shape[0]
    seq_len = n_shard * tok_rows
    experts = router_proj.shape[1]
    capacity = max(2, tok_rows * TOP_K * 7 // (6 * experts))
    head_width = H * (DN + DV)
    kv_rows = tok_rows * head_width // 128
    rope_rows = tok_rows * DR // 128
    piece_rows = kv_rows + rope_rows
    score_scale = (DN + DR) ** (-0.5)
    weights = (
        attn_gain,
        query_proj,
        latent_proj,
        rope_key_proj,
        latent_gain,
        kv_up_proj,
        out_proj,
        ffn_gain,
        router_proj,
    )
    shared_mats = (shared_gate, shared_up, shared_down)
    (
        gain_attn,
        mat_query,
        mat_latent,
        mat_rope,
        gain_latent,
        mat_kv,
        mat_out,
        gain_ffn,
        mat_router,
    ) = (
        lax.all_gather(weights[0], "shard", axis=0, tiled=True),
        lax.all_gather(weights[1], "shard", axis=0, tiled=True),
        lax.all_gather(weights[2], "shard", axis=0, tiled=True),
        lax.all_gather(weights[3], "shard", axis=0, tiled=True),
        lax.all_gather(weights[4], "shard", axis=0, tiled=True),
        lax.all_gather(weights[5], "shard", axis=0, tiled=True),
        lax.all_gather(weights[6], "shard", axis=0, tiled=True),
        lax.all_gather(weights[7], "shard", axis=0, tiled=True),
        lax.all_gather(weights[8], "shard", axis=0, tiled=True),
    )
    mat_sgate, mat_sup, mat_sdown = (
        lax.all_gather(shared_mats[0], ("rep", "shard"), axis=0, tiled=True),
        lax.all_gather(shared_mats[1], ("rep", "shard"), axis=0, tiled=True),
        lax.all_gather(shared_mats[2], ("rep", "shard"), axis=0, tiled=True),
    )
    gain_attn = gain_attn.astype(jnp.float32)
    gain_latent = gain_latent.astype(jnp.float32)
    gain_ffn = gain_ffn.astype(jnp.float32)
    stream = stream_in.astype(jnp.float32)
    scale_one = rms_scale(stream)
    normed = (stream * scale_one * gain_attn).astype(jnp.bfloat16)
    positions = shard_index * tok_rows + jnp.arange(tok_rows)
    cosine, sine_vals = rope_tables(positions, DR)
    query_raw = wide_product(normed, mat_query).reshape(tok_rows, H, DN + DR)
    query_nope = query_raw[:, :, :DN].astype(jnp.bfloat16)
    query_rot = rotate(query_raw[:, :, DN:], cosine[:, None], sine_vals[:, None]).astype(
        jnp.bfloat16
    )
    latent = wide_product(normed, mat_latent)
    scale_lat = rms_scale(latent)
    latent_normed = (latent * scale_lat * gain_latent).astype(jnp.bfloat16)
    keyval_own = wide_product(latent_normed, mat_kv).astype(jnp.bfloat16)
    key_rot_own = rotate(wide_product(normed, mat_rope), cosine, sine_vals).astype(jnp.bfloat16)
    packed = jnp.concatenate(
        [keyval_own.reshape(kv_rows, 128), key_rot_own.reshape(rope_rows, 128)], axis=0
    )
    seq_keys = lax.all_gather(packed, "shard", axis=0, tiled=True).reshape(n_shard, piece_rows, 128)
    keyval = seq_keys[:, :kv_rows].reshape(seq_len, H, DN + DV)
    key_rot = seq_keys[:, kv_rows:].reshape(seq_len, DR)
    key_nope = keyval[:, :, :DN]
    values = keyval[:, :, DN:]
    prefix = lax.dynamic_index_in_dim(prefix_len, rep_index, keepdims=False)
    key_pos = jnp.arange(seq_len)
    allowed = (key_pos[None, :] <= positions[:, None]) | (key_pos[None, :] < prefix)

    def score_block():
        raw = contract(query_nope, key_nope, ((2,), (2,)), ((1,), (1,)))
        raw = raw + jnp.transpose(contract(query_rot, key_rot, ((2,), (1,)), ((), ())), (1, 0, 2))
        return jnp.where(allowed[None], raw * score_scale, MASKED)

    scores = score_block()
    top_score = jnp.max(scores, axis=-1, keepdims=True)
    expo = jnp.exp(scores - top_score)
    total_exp = jnp.sum(expo, axis=-1, keepdims=True)
    log_total = top_score + jnp.log(total_exp)
    probs_low = (expo / total_exp).astype(jnp.bfloat16)
    attended = jnp.transpose(contract(probs_low, values, ((2,), (0,)), ((0,), (1,))), (1, 0, 2))
    attended = attended.reshape(tok_rows, H * DV).astype(jnp.bfloat16)
    attn_out = wide_product(attended, mat_out)
    mid = stream + attn_out
    scale_two = rms_scale(mid)
    normed_two = (mid * scale_two * gain_ffn).astype(jnp.bfloat16)
    router_prob = jax.nn.softmax(wide_product(normed_two, mat_router), axis=-1)
    one_hot = (routes[:, :, None] == jnp.arange(experts)[None, None, :]).astype(jnp.float32)
    picked = jnp.sum(one_hot * router_prob[:, None, :], axis=-1)
    picked_sum = jnp.sum(picked, axis=-1, keepdims=True)
    gates = route_weight * picked / picked_sum
    sgate_val = wide_product(normed_two, mat_sgate)
    sup_val = wide_product(normed_two, mat_sup)
    shared_hidden = (jax.nn.silu(sgate_val) * sup_val).astype(jnp.bfloat16)
    shared_out = wide_product(shared_hidden, mat_sdown)
    flat_routes = routes.reshape(-1)
    route_hot = (flat_routes[:, None] == jnp.arange(experts)[None, :]).astype(jnp.int32)
    route_rank = jnp.sum((jnp.cumsum(route_hot, axis=0) - route_hot) * route_hot, axis=1)
    slot_index = flat_routes * capacity + route_rank
    send_rows = (
        jnp.zeros((experts * capacity, D), jnp.bfloat16)
        .at[slot_index]
        .set(jnp.repeat(normed_two, TOP_K, axis=0))
    )
    doubled = jnp.broadcast_to(
        send_rows.reshape(experts, 1, capacity, D), (experts, n_shard, capacity, D)
    ).reshape(-1, D)
    incoming_rows = lax.all_to_all(
        doubled, ("rep", "shard"), split_axis=0, concat_axis=0, tiled=True
    )
    gate_local = expert_gate[0]
    local_up_weight = expert_up[0]
    down_local = expert_down[0]
    expert_gate_value = wide_product(incoming_rows, gate_local)
    expert_up_value = wide_product(incoming_rows, local_up_weight)
    expert_inner_state = (jax.nn.silu(expert_gate_value) * expert_up_value).astype(jnp.bfloat16)
    expert_part = wide_product(expert_inner_state, down_local).astype(jnp.bfloat16)
    returned = lax.all_to_all(
        expert_part, ("rep", "shard"), split_axis=0, concat_axis=0, tiled=True
    )
    expert_sum = jnp.sum(
        returned.reshape(experts, n_shard, capacity, D).astype(jnp.float32), axis=1
    ).reshape(experts * capacity, D)
    picked_rows = expert_sum[slot_index].reshape(tok_rows, TOP_K, D)
    ffn_out = shared_out + jnp.sum(gates[:, :, None] * picked_rows, axis=1)
    residual = mid + ffn_out
    squares = jnp.stack(
        [
            jnp.sum(stream * stream),
            jnp.sum(attn_out * attn_out),
            jnp.sum(mid * mid),
            jnp.sum(ffn_out * ffn_out),
            jnp.sum(residual * residual),
        ]
    )
    totals = lax.psum(squares, ("rep", "shard"))
    stats = jnp.sqrt(totals / (tok_rows * n_rep * n_shard * D))
    (
        gain_attn,
        mat_query,
        mat_latent,
        mat_rope,
        gain_latent,
        mat_kv,
        mat_out,
        gain_ffn,
        mat_router,
    ) = (
        lax.all_gather(weights[0], "shard", axis=0, tiled=True),
        lax.all_gather(weights[1], "shard", axis=0, tiled=True),
        lax.all_gather(weights[2], "shard", axis=0, tiled=True),
        lax.all_gather(weights[3], "shard", axis=0, tiled=True),
        lax.all_gather(weights[4], "shard", axis=0, tiled=True),
        lax.all_gather(weights[5], "shard", axis=0, tiled=True),
        lax.all_gather(weights[6], "shard", axis=0, tiled=True),
        lax.all_gather(weights[7], "shard", axis=0, tiled=True),
        lax.all_gather(weights[8], "shard", axis=0, tiled=True),
    )
    mat_sgate, mat_sup, mat_sdown = (
        lax.all_gather(shared_mats[0], ("rep", "shard"), axis=0, tiled=True),
        lax.all_gather(shared_mats[1], ("rep", "shard"), axis=0, tiled=True),
        lax.all_gather(shared_mats[2], ("rep", "shard"), axis=0, tiled=True),
    )
    gain_attn = gain_attn.astype(jnp.float32)
    gain_latent = gain_latent.astype(jnp.float32)
    gain_ffn = gain_ffn.astype(jnp.float32)
    grad_top = stream_grad.astype(jnp.float32)
    gate_grad = jnp.sum(grad_top[:, None, :] * picked_rows, axis=-1)
    expert_grad = (gates[:, :, None] * grad_top[:, None, :]).astype(jnp.bfloat16).reshape(-1, D)
    send_grad = jnp.zeros((experts * capacity, D), jnp.bfloat16).at[slot_index].set(expert_grad)
    doubled_grad = jnp.broadcast_to(
        send_grad.reshape(experts, 1, capacity, D), (experts, n_shard, capacity, D)
    ).reshape(-1, D)
    received_grad = lax.all_to_all(
        doubled_grad, ("rep", "shard"), split_axis=0, concat_axis=0, tiled=True
    )
    grad_edown = contract(expert_inner_state, received_grad, ((0,), (0,)), ((), ()))
    inner_state_gradient = contract(received_grad, down_local, ((1,), (1,)), ((), ()))
    gate_value_gradient = (
        inner_state_gradient * expert_up_value * swish_derivative(expert_gate_value)
    ).astype(jnp.bfloat16)
    up_value_gradient = (inner_state_gradient * jax.nn.silu(expert_gate_value)).astype(jnp.bfloat16)
    grad_egate = contract(incoming_rows, gate_value_gradient, ((0,), (0,)), ((), ()))
    expert_up_gradient = contract(incoming_rows, up_value_gradient, ((0,), (0,)), ((), ()))
    part_in_grad = contract(gate_value_gradient, gate_local, ((1,), (1,)), ((), ()))
    part_in_grad = (
        part_in_grad
        + contract(up_value_gradient, local_up_weight, ((1,), (1,)), ((), ()))
    ).astype(jnp.bfloat16)
    returned_grad = lax.all_to_all(
        part_in_grad, ("rep", "shard"), split_axis=0, concat_axis=0, tiled=True
    )
    slot_grad = jnp.sum(
        returned_grad.reshape(experts, n_shard, capacity, D).astype(jnp.float32), axis=1
    ).reshape(experts * capacity, D)
    routed_grad = jnp.sum(slot_grad[slot_index].reshape(tok_rows, TOP_K, D), axis=1)
    shared_hidden_grad = contract(stream_grad, mat_sdown, ((1,), (1,)), ((), ()))
    dshared_gate = (shared_hidden_grad * sup_val * swish_derivative(sgate_val)).astype(jnp.bfloat16)
    dshared_up = (shared_hidden_grad * jax.nn.silu(sgate_val)).astype(jnp.bfloat16)
    weighted_grad = route_weight * gate_grad
    picked_grad = weighted_grad / picked_sum - jnp.sum(
        weighted_grad * picked, axis=-1, keepdims=True
    ) / (picked_sum * picked_sum)
    prob_grad = jnp.sum(one_hot * picked_grad[:, :, None], axis=1)
    logit_grad = (
        router_prob * (prob_grad - jnp.sum(router_prob * prob_grad, axis=-1, keepdims=True))
    ).astype(jnp.bfloat16)
    normed_two_grad = contract(dshared_gate, mat_sgate, ((1,), (1,)), ((), ()))
    normed_two_grad = normed_two_grad + contract(dshared_up, mat_sup, ((1,), (1,)), ((), ()))
    normed_two_grad = normed_two_grad + contract(logit_grad, mat_router, ((1,), (1,)), ((), ()))
    normed_two_grad = normed_two_grad + routed_grad
    norm_part, grad_gain_ffn = norm_back(normed_two_grad, mid, scale_two, gain_ffn)
    mid_grad = grad_top + norm_part
    attn_out_grad = mid_grad.astype(jnp.bfloat16)
    attended_grad = contract(attn_out_grad, mat_out, ((1,), (1,)), ((), ()))
    attended_grad = attended_grad.astype(jnp.bfloat16).reshape(tok_rows, H, DV)
    probs_full = jnp.where(allowed[None], jnp.exp(score_block() - log_total), 0.0)
    value_grad = jnp.transpose(contract(probs_full.astype(jnp.bfloat16), attended_grad, ((1,), (0,)), ((0,), (1,))), (1, 0, 2))
    prob_att_grad = contract(attended_grad, values, ((2,), (2,)), ((1,), (1,)))
    scores_grad = probs_full * (
        prob_att_grad - jnp.sum(probs_full * prob_att_grad, axis=-1, keepdims=True)
    )
    scores_grad = scores_grad.astype(jnp.bfloat16)
    query_nope_grad = score_scale * jnp.transpose(contract(scores_grad, key_nope, ((2,), (0,)), ((0,), (1,))), (1, 0, 2))
    query_rot_grad = score_scale * jnp.transpose(contract(scores_grad, key_rot, ((2,), (0,)), ((), ())), (1, 0, 2))
    key_nope_grad = score_scale * jnp.transpose(contract(scores_grad, query_nope, ((1,), (0,)), ((0,), (1,))), (1, 0, 2))
    key_rot_grad = score_scale * contract(scores_grad, query_rot, ((0, 1,), (1, 0,)), ((), ()))
    keyval_grad_all = jnp.concatenate([key_nope_grad, value_grad], axis=-1).reshape(
        n_shard, kv_rows, 128
    )
    key_grad_pieces = jnp.concatenate(
        [keyval_grad_all, key_rot_grad.reshape(n_shard, rope_rows, 128)], axis=1
    )
    own_keys = lax.psum_scatter(
        key_grad_pieces.reshape(-1, 128).astype(jnp.bfloat16),
        "shard",
        scatter_dimension=0,
        tiled=True,
    ).astype(jnp.float32)
    keyval_grad = own_keys[:kv_rows].reshape(tok_rows, head_width).astype(jnp.bfloat16)
    key_pre_grad = rotate(own_keys[kv_rows:].reshape(tok_rows, DR), cosine, -sine_vals).astype(
        jnp.bfloat16
    )
    query_rot_back = rotate(query_rot_grad, cosine[:, None], -sine_vals[:, None])
    query_grad = (
        jnp.concatenate([query_nope_grad, query_rot_back], axis=-1)
        .reshape(tok_rows, H * (DN + DR))
        .astype(jnp.bfloat16)
    )
    latent_normed_grad = contract(keyval_grad, mat_kv, ((1,), (1,)), ((), ()))
    latent_pre, grad_gain_latent = norm_back(latent_normed_grad, latent, scale_lat, gain_latent)
    latent_grad = latent_pre.astype(jnp.bfloat16)
    normed_grad = contract(query_grad, mat_query, ((1,), (1,)), ((), ()))
    normed_grad = normed_grad + contract(key_pre_grad, mat_rope, ((1,), (1,)), ((), ()))
    normed_grad = normed_grad + contract(latent_grad, mat_latent, ((1,), (1,)), ((), ()))
    attn_part, grad_gain_attn = norm_back(normed_grad, stream, scale_one, gain_attn)
    grad_stream = (mid_grad + attn_part).astype(jnp.bfloat16)
    owned = (
        lax.psum_scatter(
            grad_gain_attn[None][0], ("rep", "shard"), scatter_dimension=0, tiled=True
        ),
        lax.psum_scatter(
            contract(normed, query_grad, ((0,), (0,)), ((), ())),
            ("rep", "shard"),
            scatter_dimension=0,
            tiled=True,
        ),
        lax.psum_scatter(
            contract(normed, latent_grad, ((0,), (0,)), ((), ())),
            ("rep", "shard"),
            scatter_dimension=0,
            tiled=True,
        ),
        lax.psum_scatter(
            contract(normed, key_pre_grad, ((0,), (0,)), ((), ())),
            ("rep", "shard"),
            scatter_dimension=0,
            tiled=True,
        ),
        lax.psum_scatter(
            grad_gain_latent[None][0], ("rep", "shard"), scatter_dimension=0, tiled=True
        ),
        lax.psum_scatter(
            contract(latent_normed, keyval_grad, ((0,), (0,)), ((), ())),
            ("rep", "shard"),
            scatter_dimension=0,
            tiled=True,
        ),
        lax.psum_scatter(
            contract(attended, attn_out_grad, ((0,), (0,)), ((), ())),
            ("rep", "shard"),
            scatter_dimension=0,
            tiled=True,
        ),
        lax.psum_scatter(grad_gain_ffn[None][0], ("rep", "shard"), scatter_dimension=0, tiled=True),
        lax.psum_scatter(
            contract(normed_two, logit_grad, ((0,), (0,)), ((), ())),
            ("rep", "shard"),
            scatter_dimension=0,
            tiled=True,
        ),
        lax.psum_scatter(
            contract(normed_two, dshared_gate, ((0,), (0,)), ((), ())),
            ("rep", "shard"),
            scatter_dimension=0,
            tiled=True,
        ),
        lax.psum_scatter(
            contract(normed_two, dshared_up, ((0,), (0,)), ((), ())),
            ("rep", "shard"),
            scatter_dimension=0,
            tiled=True,
        ),
        lax.psum_scatter(
            contract(shared_hidden, stream_grad, ((0,), (0,)), ((), ())),
            ("rep", "shard"),
            scatter_dimension=0,
            tiled=True,
        ),
    )
    return (
        residual.astype(jnp.bfloat16),
        grad_stream,
        stats,
        owned[0],
        owned[1],
        owned[2],
        owned[3],
        owned[4],
        owned[5],
        owned[6],
        owned[7],
        owned[8],
        owned[9],
        owned[10],
        owned[11],
        grad_egate[None],
        expert_up_gradient[None],
        grad_edown[None],
    )


def by_size(*args):
    tokens = lax.axis_size("rep") * lax.axis_size("shard") * args[0].shape[0]
    return (on_device if tokens * args[0].shape[1] <= 1 << 23 else on_device_weights)(*args)


def solution(mesh):
    placed = (
        P(("rep", "shard"), None),
        P(("rep", "shard"), None),
        P(),
        P(("rep", "shard"), None),
        P(("rep", "shard"), None),
        P("shard"),
        P("shard", None),
        P("shard", None),
        P("shard", None),
        P("shard"),
        P("shard", None),
        P("shard", None),
        P("shard"),
        P("shard", None),
        P(("rep", "shard"), None),
        P(("rep", "shard"), None),
        P(("rep", "shard"), None),
        P("rep", None, "shard"),
        P("rep", None, "shard"),
        P("rep", "shard", None),
    )
    return jax.shard_map(
        by_size,
        mesh=mesh,
        in_specs=placed,
        out_specs=(
            P(("rep", "shard"), None),
            P(("rep", "shard"), None),
            P(),
            P(("rep", "shard")),
            P(("rep", "shard"), None),
            P(("rep", "shard"), None),
            P(("rep", "shard"), None),
            P(("rep", "shard")),
            P(("rep", "shard"), None),
            P(("rep", "shard"), None),
            P(("rep", "shard")),
            P(("rep", "shard"), None),
            P(("rep", "shard"), None),
            P(("rep", "shard"), None),
            P(("rep", "shard"), None),
            P("rep", None, "shard"),
            P("rep", None, "shard"),
            P("rep", "shard", None),
        ),
        check_vma=False,
    )
```

```python
import functools
import jax
import jax.numpy as jnp
from jax import lax
from jax.experimental import pallas as pl
from jax.experimental.pallas import tpu as pltpu
from jax.sharding import PartitionSpec as P

D = 2048
H = 16
DN = 128
DR = 64
DV = 128
TOP_K = 6


EPS = 1e-06
ROPE_BASE = 10000.0
MASKED = -1e30


def wide_product(left, right):
    return jnp.dot(left, right, preferred_element_type=jnp.float32)


def contract(left, right, over, batch=((), ())):
    return lax.dot_general(left, right, (over, batch), preferred_element_type=jnp.float32)


def dot_nt(left, right):
    return contract(left, right, ((1,), (1,)))


def dot_tn(left, right):
    return contract(left, right, ((0,), (0,)))


def rms_scale(values):
    return lax.rsqrt(jnp.mean(values * values, axis=-1, keepdims=True) + EPS)


def norm_back(grad_out, inputs, row_scale, gain_vec):
    weighted = grad_out * gain_vec
    inner_mean = jnp.mean(weighted * inputs, axis=-1, keepdims=True)
    grad_in = row_scale * weighted - inputs * (row_scale * row_scale * row_scale) * inner_mean
    grad_gain = jnp.sum(grad_out * inputs * row_scale, axis=0)
    return (grad_in, grad_gain)


def rope_tables(positions, rope_width):
    frequency = ROPE_BASE ** (-2.0 * jnp.arange(rope_width // 2, dtype=jnp.float32) / rope_width)
    angles = positions.astype(jnp.float32)[:, None] * frequency[None, :]
    return (jnp.cos(angles), jnp.sin(angles))


def rotate(values, cosine, sine_vals):
    half_dim = values.shape[-1] // 2
    low_half = values[..., :half_dim]
    high_half = values[..., half_dim:]
    return jnp.concatenate(
        [low_half * cosine - high_half * sine_vals, high_half * cosine + low_half * sine_vals],
        axis=-1,
    )


def swish_derivative(values):
    sigmoid = jax.nn.sigmoid(values)
    return sigmoid * (1.0 + values * (1.0 - sigmoid))


MESH = pl.DeviceIdType.MESH
SEM = pltpu.SemaphoreType.DMA
HBM = pl.BlockSpec(memory_space=pl.ANY)

def when(ok, f):
    if ok is None: f()
    else: pl.when(ok)(f)

def place():
    rep, x = lax.axis_index("rep"), lax.axis_index("shard")
    return rep // 4, lax.rem(rep // 2, 2), lax.rem(rep, 2), x

def device(z, y, c, x):
    return ((z * 2 + y) * 2 + c, x)

def slot(z, y, c, x):
    return ((z * 2 + y) * 2 + c) * 2 + x

def neighbours(nz):
    z, y, c, x = place()
    return dict(
        zr=(device(z + 1, y, c, x), z + 1 < nz),
        zl=(device(z - 1, y, c, x), z >= 1),
        y=(device(z, 1 - y, c, x), None),
        x=(device(z, y, c, 1 - x), None),
        c=(device(z, y, 1 - c, x), None),
    )

def greet(nbr):
    bar = pltpu.get_barrier_semaphore()
    count = 0
    for dev, ok in nbr.values():
        when(ok, lambda dev=dev: pl.semaphore_signal(bar, inc=1, device_id=dev, device_id_type=MESH))
        count = count + (1 if ok is None else jnp.where(ok, 1, 0))
    pl.semaphore_wait(bar, count)

def gather_kernel(nz, x_ref, t_ref, o_ref, ot_ref, own_sem, z_send, y_send, x_send, c_send, recv, crecv):
    z, y, c, x = place()
    nbr = neighbours(nz)
    greet(nbr)
    half = x_ref.shape[0] // 2
    own = slot(z, y, c, x)
    sems = dict(zr=z_send.at[0], zl=z_send.at[1], y=y_send, x=x_send, c=c_send)

    def move(kind, h, b, mine=False):
        if h == 2:
            src, dst = t_ref if mine else ot_ref.at[b], ot_ref.at[b]
        else:
            rows = pl.ds(h * half, half)
            src, dst = x_ref.at[rows] if mine else o_ref.at[b, rows], o_ref.at[b, rows]
        return pltpu.make_async_remote_copy(
            src_ref=src, dst_ref=dst, send_sem=sems[kind].at[h, b],
            recv_sem=(crecv if kind == "c" else recv).at[h, b], device_id=nbr[kind][0], device_id_type=MESH)

    def schedule(go):
        def send(kind, h, b, mine=False):
            def f():
                for hh in (2, 0) if h == 0 else (1,):
                    d = move(kind, hh, b, mine)
                    d.start() if go else d.wait_send()

            when(nbr[kind][1], f)

        def arrive(h, b):
            if go:
                for hh in (2, 0) if h == 0 else (1,):
                    move("x", hh, b).wait_recv()

        second, third = ("y", "x"), ("x", "y")
        for h in (0, 1):
            send("zr", h, own, True)
            send("zl", h, own, True)
            send(second[h], h, own, True)
        for h in (0, 1):
            send(third[h], h, own, True)
            send("c", h, own, True)
        rounds = [[(z, None)]]
        for s in range(nz - 1):
            rounds.append([(z - 1 - s, z - 1 - s >= 0), (z + 1 + s, z + 1 + s < nz)])

        def drain1(rnd):
            for i, (zb, ok) in enumerate(rnd):
                for h in (0, 1):
                    def f(zb=zb, h=h, i=i):
                        b = slot(zb, y, c, x)
                        arrive(h, b)
                        send("zr" if i == 0 else "zl", h, b)
                        send(second[h], h, b)
                        send(third[h], h, b)
                        send("c", h, b)
                    when(ok, f)

        def drain2(rnd):
            for zb, ok in rnd:
                for h in (0, 1):
                    def f(zb=zb, h=h):
                        b = slot(zb, 1 - y, c, x) if h == 0 else slot(zb, y, c, 1 - x)
                        arrive(h, b)
                        send(third[h], h, b)
                        send("c", h, b)
                    when(ok, f)

        def drain3(rnd):
            for zb, ok in rnd:
                for h in (0, 1):
                    def f(zb=zb, h=h):
                        b = slot(zb, y, c, 1 - x) if h == 0 else slot(zb, 1 - y, c, x)
                        arrive(h, b)
                        send("c", h, b)
                        b = slot(zb, 1 - y, c, 1 - x)
                        arrive(h, b)
                        send("c", h, b)
                    when(ok, f)

        for s in range(nz - 1):
            drain1(rounds[s + 1])
            drain2(rounds[s])
            if s >= 1:
                drain3(rounds[s - 1])
        drain2(rounds[nz - 1])
        drain3(rounds[nz - 2])
        drain3(rounds[nz - 1])

    local = [
        pltpu.make_async_copy(x_ref, o_ref.at[own], own_sem.at[0]),
        pltpu.make_async_copy(t_ref, ot_ref.at[own], own_sem.at[1]),
    ]
    for d in local:
        d.start()
    schedule(True)
    for zb in range(nz):
        for yb in range(2):
            for xb in range(2):
                for h in (2, 0, 1):
                    move("c", h, slot(zb, yb, 1 - c, xb)).wait_recv()
    for d in local:
        d.wait()
    schedule(False)


def all_gather(x, t, n, nz, cid):
    return pl.pallas_call(
        functools.partial(gather_kernel, nz),
        out_shape=[jax.ShapeDtypeStruct((n,) + v.shape, v.dtype) for v in (x, t)],
        in_specs=[pl.BlockSpec(memory_space=pl.ANY)] * 2,
        out_specs=[pl.BlockSpec(memory_space=pl.ANY)] * 2,
        scratch_shapes=[SEM((2,)), SEM((2, 3, n)), SEM((3, n)), SEM((3, n)), SEM((3, n)), SEM((3, n)), SEM((3, n))],
        cost_estimate=lasting(85),
        compiler_params=pltpu.CompilerParams(collective_id=cid, has_side_effects=True),
    )(x, t)


def far_first(nz, z):
    def pick(i):
        total = 0
        for k in range(nz):
            ranked = sorted(range(nz), key=lambda d: (-abs(d - k), -d if k < nz // 2 else d))
            total = total + jnp.where(z == k, ranked[i], 0)
        return total
    return [pick(i) for i in range(nz)]

def add_rows(total, other, lo, other_lo, count):
    step = next(k for k in (32, 16, 8) if count % k == 0)

    def body(i, carry):
        r = pl.ds(pl.multiple_of(lo + i * step, step), step)
        s = pl.ds(pl.multiple_of(other_lo + i * step, step), step)
        total[r] = total[r] + other[s]
        return carry

    lax.fori_loop(0, count // step, body, 0)


def scatter_kernel(nz, lo, x_ref, o_ref, mine, core, one, two, line, load_sem, core_send, core_recv, one_send, one_recv, two_send, two_recv, line_send, line_recv):
    z, y, c, x = place()
    nbr = neighbours(nz)
    greet(nbr)
    T = mine.shape[1]
    half = T // 2
    rows = lambda h: pl.ds(h * half, half)
    place_of = lambda zb, yb, xb: (zb * 2 + yb) * 2 + xb
    cols = pl.ds(lo, mine.shape[2])
    order = far_first(nz, z)
    combos = [(1 - y, 1 - x), (y, 1 - x), (1 - y, x), (y, x)]

    def core_copy(zb, yb, xb):
        k = place_of(zb, yb, xb)
        return remote(x_ref.at[slot(zb, yb, 1 - c, xb), :, cols], core.at[k], core_send.at[k], core_recv.at[k], nbr["c"][0])

    def load(zb, yb, xb):
        k = place_of(zb, yb, xb)
        return pltpu.make_async_copy(x_ref.at[slot(zb, yb, c, xb), :, cols], mine.at[k], load_sem.at[k])

    def one_copy(h, zb, j):
        k = place_of(zb, j, 1 - x) if h == 0 else place_of(zb, 1 - y, j)
        i = zb * 2 + j
        return remote(mine.at[k, rows(h)], one.at[h, i], one_send.at[h, i], one_recv.at[h, i], nbr["x" if h == 0 else "y"][0])

    def two_copy(h, zb):
        k = place_of(zb, 1 - y, x) if h == 0 else place_of(zb, y, 1 - x)
        return remote(mine.at[k, rows(h)], two.at[h, zb], two_send.at[h, zb], two_recv.at[h, zb], nbr["y" if h == 0 else "x"][0])

    def line_copy(h, zb, right):
        k = place_of(zb, y, x)
        d = 0 if right else 1
        return remote(mine.at[k, rows(h)], line.at[d, h, zb], line_send.at[h, zb], line_recv.at[d, h, zb], nbr["zr" if right else "zl"][0])

    for zb in order:
        for yb, xb in combos:
            core_copy(zb, yb, xb).start()
            load(zb, yb, xb).start()

    def stage0(zb):
        for n, (yb, xb) in enumerate(combos):
            k = place_of(zb, yb, xb)
            core_copy(zb, yb, xb).wait_recv()
            load(zb, yb, xb).wait()
            add_rows(mine.at[k], core.at[k], 0, 0, T)
            if n in (0, 1):
                one_copy(0, zb, yb).start()
            if n in (0, 2):
                one_copy(1, zb, xb).start()

    def stage1(zb):
        for far in (True, False):
            for h in (0, 1):
                j = (1 - y if far else y) if h == 0 else (1 - x if far else x)
                one_copy(h, zb, j).wait_recv()
                k = place_of(zb, j, x) if h == 0 else place_of(zb, y, j)
                add_rows(mine.at[k], one.at[h, zb * 2 + j], h * half, 0, half)
                if far:
                    two_copy(h, zb).start()

    def stage2(zb):
        k = place_of(zb, y, x)
        for h in (0, 1):
            two_copy(h, zb).wait_recv()
            add_rows(mine.at[k], two.at[h, zb], h * half, 0, half)
            def go(right, h=h):
                line_copy(h, zb, right).wait_recv()
                add_rows(mine.at[k], line.at[0 if right else 1, h, zb], h * half, 0, half)
            when(jnp.logical_and(zb > z, z >= 1), lambda: go(True))
            when(jnp.logical_and(zb < z, z + 1 < nz), lambda: go(False))
            when(zb > z, lambda: line_copy(h, zb, True).start())
            when(zb < z, lambda: line_copy(h, zb, False).start())

    for i in range(nz + 2):
        if i < nz: stage0(order[i])
        if 1 <= i < nz + 1: stage1(order[i - 1])
        if 2 <= i: stage2(order[i - 2])
    k = place_of(z, y, x)
    for h in (0, 1):
        lo = h * half
        o_ref[rows(h)] = mine[k, rows(h)].astype(jnp.float32)
        for d, ok in ((0, z >= 1), (1, z + 1 < nz)):
            def fin(d=d, h=h):
                line_copy(h, z, d == 0).wait_recv()
                o_ref[rows(h)] += line[d, h, z].astype(jnp.float32)
            when(ok, fin)
    for zb in order:
        for yb, xb in combos:
            core_copy(zb, yb, xb).wait_send()
        for h in (0, 1):
            for j in (0, 1):
                one_copy(h, zb, j).wait_send()
            two_copy(h, zb).wait_send()
            when(zb > z, lambda: line_copy(h, zb, True).wait_send())
            when(zb < z, lambda: line_copy(h, zb, False).wait_send())

def reduce_scatter(x, nz, cid):
    N, T, D = x.shape
    sem = pltpu.SemaphoreType.DMA
    bf = x.dtype
    parts = max(1, N // 32)
    W = D // parts
    outs = [
        pl.pallas_call(
            functools.partial(scatter_kernel, nz, i * W),
            out_shape=jax.ShapeDtypeStruct((T, W), jnp.float32),
            in_specs=[pl.BlockSpec(memory_space=pl.ANY)],
            out_specs=pl.BlockSpec(memory_space=pltpu.VMEM),
            scratch_shapes=[
                pltpu.VMEM((N // 2, T, W), bf), pltpu.VMEM((N // 2, T, W), bf),
                pltpu.VMEM((2, 2 * nz, T // 2, W), bf), pltpu.VMEM((2, nz, T // 2, W), bf),
                pltpu.VMEM((2, 2, nz, T // 2, W), bf),
                sem((N // 2,)), sem((N // 2,)), sem((N // 2,)), sem((2, 2 * nz)), sem((2, 2 * nz)),
                sem((2, nz)), sem((2, nz)), sem((2, nz)), sem((2, 2, nz))],
            cost_estimate=lasting(85),
        compiler_params=pltpu.CompilerParams(
                collective_id=cid + i, has_side_effects=True, vmem_limit_bytes=48 << 20
            ),
        )(x)
        for i in range(parts)
    ]
    return outs[0] if parts == 1 else jnp.concatenate(outs, axis=1)


def lasting(us):
    return pl.CostEstimate(flops=0, bytes_accessed=int(us * 3.5e6), transcendentals=0)


def remote(src, dst, send_sem, recv_sem, dev):
    return pltpu.make_async_remote_copy(
        src_ref=src, dst_ref=dst, send_sem=send_sem, recv_sem=recv_sem, device_id=dev, device_id_type=MESH
    )


def quad_neighbours():
    z, y, c, x = place()
    return dict(x=(device(z, y, c, 1 - x), None), c=(device(z, y, 1 - c, x), None))


def open_kernel(nz, stream, wq, kv, lat, tiny, stream_all, wq_o, kv_o, lat_o, tiny_o, b0, b1, b2, b3, b4,
                load, store, send, recv, x_send, x_recv, zr_send, zl_send, y_send, p_recv):
    z, y, c, x = place()
    nbr = neighbours(nz)
    greet(nbr)
    quads = 2 * nz
    own, side, other = c * 2 + x, c * 2 + 1 - x, 1 - x
    rows = lat.shape[0] // 2
    xdev, cdev = nbr["x"][0], nbr["c"][0]

    def heads(ref, out, xx):
        n = out.shape[2]
        return ref.at[:, pl.ds(pl.multiple_of((xx * 2 + c) * n, 128), n)]

    def rows_of(a, j):
        n = (wq.shape[0] // quads, kv.shape[0] // quads, rows // quads)[a]
        return pl.ds(pl.multiple_of((c * rows if a == 2 else 0) + j * n, n), n)

    def piece(a, j):
        return (wq_o, kv_o, lat_o)[a].at[other, rows_of(a, j)]

    mine = z * 2 + y

    def first(a):
        r = rows_of(a, mine)
        if a == 2:
            src, dst = lat.at[r], lat_o.at[x, r]
        else:
            ref, out = ((wq, wq_o), (kv, kv_o))[a]
            n = out.shape[2]
            src, dst = ref.at[r, pl.ds(pl.multiple_of((other * 2 + c) * n, 128), n)], out.at[x, r]
        return remote(src, dst, x_send.at[a], x_recv.at[a], xdev)

    def along(a, j, kind):
        sems = dict(zr=zr_send, zl=zl_send, y=y_send)[kind]
        return remote(piece(a, j), piece(a, j), sems.at[a, j], p_recv.at[a, j], nbr[kind][0])

    kinds = (2, 1, 0)
    for a in kinds:
        first(a).start()
    xs = [
        remote(stream, stream_all.at[own], send.at[0], recv.at[0], xdev),
        remote(tiny, tiny_o.at[x], send.at[1], recv.at[1], xdev),
    ]
    for d in xs:
        d.start()
    cs = [remote(stream, stream_all.at[own], send.at[2], recv.at[2], cdev)]
    cs[0].start()
    here = [
        (stream, b0, stream_all.at[own]), (tiny, b4, tiny_o.at[x]), (lat, b3, lat_o.at[x]),
        (heads(kv, kv_o, x), b2, kv_o.at[x]), (heads(wq, wq_o, x), b1, wq_o.at[x]),
    ]
    for i, (a, b, o) in enumerate(here):
        pltpu.make_async_copy(a, b, load.at[i]).start()
    for i, (a, b, o) in enumerate(here):
        pltpu.make_async_copy(a, b, load.at[i]).wait()
        pltpu.make_async_copy(b, o, store.at[i]).start()

    def spread(go):
        def send(a, j, kind):
            d = along(a, j, kind)
            ok = nbr[kind][1]
            when(ok, (lambda: d.start()) if go else (lambda: d.wait_send()))

        for a in kinds:
            if go:
                first(a).wait_recv()
            for kind in ("zr", "zl", "y"):
                send(a, mine, kind)
        for s in range(nz - 1):
            for kind, zb, ok in (("zr", z - 1 - s, z - 1 - s >= 0), ("zl", z + 1 + s, z + 1 + s < nz)):

                def f(kind=kind, zb=zb):
                    j = zb * 2 + y
                    for a in kinds:
                        if go:
                            along(a, j, "y").wait_recv()
                        send(a, j, kind)
                        send(a, j, "y")

                pl.when(ok)(f)

    spread(True)
    xs[0].wait_recv()
    cs.append(remote(stream_all.at[side], stream_all.at[side], send.at[3], recv.at[3], cdev))
    cs[1].start()
    xs[1].wait_recv()
    for zb in range(nz):
        for a in kinds:
            along(a, zb * 2 + 1 - y, "y").wait_recv()
    half = pl.ds(pl.multiple_of(c * rows, rows), rows)
    cs.append(remote(lat_o.at[other, half], lat_o.at[other, half], send.at[4], recv.at[4], cdev))
    cs[2].start()
    for d in cs:
        d.wait_recv()
    for i, (a, b, o) in enumerate(here):
        pltpu.make_async_copy(b, o, store.at[i]).wait()
    for d in xs + cs:
        d.wait_send()
    for a in kinds:
        first(a).wait_send()
    spread(False)


def open_quad(stream, wq, kv, lat, tiny, nz, cid):
    sd = jax.ShapeDtypeStruct
    ins = (stream, wq, kv, lat, tiny)
    shapes = [(4,) + stream.shape, (2, wq.shape[0], wq.shape[1] // 4), (2, kv.shape[0], kv.shape[1] // 4), (2,) + lat.shape, (2,) + tiny.shape]
    pieces = SEM((3, 2 * nz))
    return pl.pallas_call(
        functools.partial(open_kernel, nz),
        out_shape=[sd(shape, v.dtype) for shape, v in zip(shapes, ins)],
        in_specs=[HBM] * 5,
        out_specs=[HBM] * 5,
        scratch_shapes=[pltpu.VMEM(shape[1:], v.dtype) for shape, v in zip(shapes, ins)]
        + [SEM((5,)), SEM((5,)), SEM((5,)), SEM((5,)), SEM((3,)), SEM((3,)), pieces, pieces, pieces, pieces],
        cost_estimate=lasting(50),
        compiler_params=pltpu.CompilerParams(collective_id=cid, has_side_effects=True, vmem_limit_bytes=16 << 20),
    )(*ins)


def split_kernel(units, gate, up, out):
    lanes = out.shape[2] // 2
    for j in range(out.shape[0]):
        lo = min(units * j // 128 * 128, gate.shape[1] - 2 * lanes)
        row = lax.broadcasted_iota(jnp.int32, (2 * lanes, lanes), 0)
        lane = lax.broadcasted_iota(jnp.int32, (2 * lanes, lanes), 1)
        pick = ((row == lane + (units * j - lo)) & (lane < units)).astype(jnp.float32).astype(gate.dtype)
        for k, ref in enumerate((gate, up)):
            out[j, :, k * lanes : (k + 1) * lanes] = wide_product(ref[:, lo : lo + 2 * lanes], pick).astype(out.dtype)


def split_units(gate, up, n_dev, units):
    vmem = pl.BlockSpec(memory_space=pltpu.VMEM)
    return pl.pallas_call(
        functools.partial(split_kernel, units),
        out_shape=jax.ShapeDtypeStruct((n_dev, gate.shape[0], 256), gate.dtype),
        in_specs=[vmem, vmem],
        out_specs=vmem,
        cost_estimate=lasting(4),
        compiler_params=pltpu.CompilerParams(vmem_limit_bytes=16 << 20),
    )(gate, up)


def join_kernel(units, blocks, gate, up):
    lanes = blocks.shape[2] // 2
    row = lax.broadcasted_iota(jnp.int32, (lanes, lanes), 0)
    lane = lax.broadcasted_iota(jnp.int32, (lanes, lanes), 1)
    for t in range(gate.shape[1] // lanes):
        totals = [None, None]
        for j in range(lanes * t // units, (lanes * t + lanes - 1) // units + 1):
            pick = ((row + (units * j - lanes * t) == lane) & (row < units)).astype(jnp.float32).astype(blocks.dtype)
            for k in (0, 1):
                v = wide_product(blocks[j, :, k * lanes : (k + 1) * lanes], pick)
                totals[k] = v if totals[k] is None else totals[k] + v
        for k, ref in enumerate((gate, up)):
            ref[:, t * lanes : (t + 1) * lanes] = totals[k]


def join_units(blocks, total, units):
    vmem = pl.BlockSpec(memory_space=pltpu.VMEM)
    out = jax.ShapeDtypeStruct((blocks.shape[1], total), jnp.float32)
    return pl.pallas_call(
        functools.partial(join_kernel, units),
        out_shape=[out, out],
        in_specs=[vmem],
        out_specs=[vmem, vmem],
        cost_estimate=lasting(4),
        compiler_params=pltpu.CompilerParams(vmem_limit_bytes=16 << 20),
    )(blocks)


def quad_gather_kernel(x_ref, o_ref, local, send, recv):
    z, y, c, x = place()
    nbr = quad_neighbours()
    greet(nbr)
    own, side = c * 2 + x, c * 2 + 1 - x
    half = x_ref.shape[0] // 2
    copies = []
    for h in (0, 1):
        r = pl.ds(h * half, half)
        a = remote(x_ref.at[r], o_ref.at[own, r], send.at[0, h], recv.at[0, h], nbr["x"][0])
        b = remote(x_ref.at[r], o_ref.at[own, r], send.at[1, h], recv.at[1, h], nbr["c"][0])
        d = remote(o_ref.at[side, r], o_ref.at[side, r], send.at[2, h], recv.at[2, h], nbr["c"][0])
        a.start()
        b.start()
        copies.append((a, b, d))
    here = pltpu.make_async_copy(x_ref, o_ref.at[own], local)
    here.start()
    for a, b, d in copies:
        a.wait_recv()
        d.start()
    for a, b, d in copies:
        b.wait_recv()
        d.wait_recv()
        a.wait_send()
        b.wait_send()
        d.wait_send()
    here.wait()


def quad_gather(v, cid):
    return pl.pallas_call(
        quad_gather_kernel,
        out_shape=jax.ShapeDtypeStruct((4,) + v.shape, v.dtype),
        in_specs=[HBM],
        out_specs=HBM,
        scratch_shapes=[SEM, SEM((3, 2)), SEM((3, 2))],
        cost_estimate=lasting(18),
        compiler_params=pltpu.CompilerParams(collective_id=cid, has_side_effects=True),
    )(v)


def quad_scatter_kernel(v_ref, o_ref, mine, core, far, load, send, recv):
    z, y, c, x = place()
    nbr = quad_neighbours()
    greet(nbr)
    half = o_ref.shape[0] // 2
    steps = []
    for h in (0, 1):
        r = pl.ds(h * half, half)
        for j, xb in ((0, 1 - x), (1, x)):
            a = remote(v_ref.at[(1 - c) * 2 + xb, r], core.at[j, r], send.at[j, h], recv.at[j, h], nbr["c"][0])
            b = pltpu.make_async_copy(v_ref.at[c * 2 + xb, r], mine.at[j, r], load.at[j, h])
            a.start()
            b.start()
            steps.append((a, b))
    outs = []
    for h in (0, 1):
        r = pl.ds(h * half, half)
        a, b = steps[2 * h]
        a.wait_recv()
        b.wait()
        add_rows(mine.at[0], core.at[0], h * half, h * half, half)
        f = remote(mine.at[0, r], far.at[r], send.at[2, h], recv.at[2, h], nbr["x"][0])
        f.start()
        outs.append(f)
    for h in (0, 1):
        a, b = steps[2 * h + 1]
        a.wait_recv()
        b.wait()
        outs[h].wait_recv()
        def body(i, carry, h=h):
            r = pl.ds(pl.multiple_of(h * half + i * 16, 16), 16)
            o_ref[r] = (mine[1, r].astype(jnp.float32) + core[1, r].astype(jnp.float32)) + far[r].astype(jnp.float32)
            return carry
        lax.fori_loop(0, half // 16, body, 0)
    for a, b in steps:
        a.wait_send()
    for f in outs:
        f.wait_send()


def quad_scatter(v, cid):
    _, rows, cols = v.shape
    buf = pltpu.VMEM((2, rows, cols), v.dtype)
    return pl.pallas_call(
        quad_scatter_kernel,
        out_shape=jax.ShapeDtypeStruct((rows, cols), jnp.float32),
        in_specs=[HBM],
        out_specs=pl.BlockSpec(memory_space=pltpu.VMEM),
        scratch_shapes=[buf, buf, pltpu.VMEM((rows, cols), v.dtype), SEM((2, 2)), SEM((3, 2)), SEM((3, 2))],
        cost_estimate=lasting(16),
        compiler_params=pltpu.CompilerParams(
            collective_id=cid, has_side_effects=True, vmem_limit_bytes=24 << 20
        ),
    )(v)


def finish_kernel(nz, na, own, far, stream, attn, mid, *refs):
    ins, refs = refs[:na], refs[na:]
    (res_o, q_o, kv_o, out_o, lat_o, router_o, side_o, stat_o), refs = refs[:8], refs[8:]
    (t_mine, t_core, t_one, t_two, t_line, ffn), refs = refs[:6], refs[6:]
    mine, refs = refs[:na], refs[na:]
    one, refs = refs[:na], refs[na:]
    line, refs = refs[:na], refs[na:]
    (q_all, kv_all, out_all, side_all, stat, stat_in), refs = refs[:6], refs[6:]
    (t_load, core_send, core_recv, tx_send, tx_recv, ty_send, ty_recv, tz_send, tz_recv,
     load, y_send, y_recv, z_send, z_recv, own_sem, q_send, q_recv, out_send, out_recv, st_send, st_recv) = refs
    z, y, c, x = place()
    nbr = neighbours(nz)
    nbr["d"] = (device(z, y, 1 - c, 1 - x), None)
    quads = 2 * nz
    linear = slot(z, y, c, x)
    target = (x * 2 + c) * quads + z * 2 + y
    group, q = linear // quads, lax.rem(linear, quads)
    source = device(q // 2, lax.rem(q, 2), lax.rem(group, 2), group // 2)
    away = target != linear
    nbr["to"] = ((target // 2, lax.rem(target, 2)), away)
    nbr["from"] = (source, away)
    bits = [b for b in range(8) if 1 << b < nz]
    for b in bits:
        low = lax.rem(z // (1 << b), 2)
        nbr["z%d" % b] = (device(z + (1 - 2 * low) * (1 << b), y, c, x), None)
    greet(nbr)
    order = far_first(nz, z)
    xdev, cdev, ddev, ydev = (nbr[k][0] for k in ("x", "c", "d", "y"))
    zdev = lambda right: nbr["zr" if right else "zl"][0]
    add = lambda total, other: add_rows(total, other, 0, 0, total.shape[0])
    place_of = lambda zb, yb, xb: (zb * 2 + yb) * 2 + xb
    combos = [(1 - y, 1 - x), (y, 1 - x), (1 - y, x), (y, x)]

    def t_core_copy(k):
        return remote(far.at[k], t_core.at[k], core_send.at[k], core_recv.at[k], cdev)

    def t_load_copy(k):
        return pltpu.make_async_copy(own.at[k], t_mine.at[k], t_load.at[k])

    def tx_copy(zb, yb):
        i = zb * 2 + yb
        return remote(t_mine.at[place_of(zb, yb, 1 - x)], t_one.at[i], tx_send.at[i], tx_recv.at[i], xdev)

    def ty_copy(zb):
        return remote(t_mine.at[place_of(zb, 1 - y, x)], t_two.at[zb], ty_send.at[zb], ty_recv.at[zb], ydev)

    def tz_copy(zb, right):
        d = 0 if right else 1
        return remote(t_mine.at[place_of(zb, y, x)], t_line.at[d, zb], tz_send.at[zb], tz_recv.at[d, zb], zdev(right))

    def t_stage0(zb):
        for i, (yb, xb) in enumerate(combos):
            k = place_of(zb, yb, xb)
            t_core_copy(k).wait_recv()
            t_load_copy(k).wait()
            add(t_mine.at[k], t_core.at[k])
            if i < 2:
                tx_copy(zb, yb).start()

    def t_stage1(zb):
        for yb in (1 - y, y):
            tx_copy(zb, yb).wait_recv()
            add(t_mine.at[place_of(zb, yb, x)], t_one.at[zb * 2 + yb])
            if yb is not y:
                ty_copy(zb).start()

    def on_line(zb, arrive, leave):
        when(jnp.logical_and(zb > z, z >= 1), lambda: arrive(True))
        when(jnp.logical_and(zb < z, z + 1 < nz), lambda: arrive(False))
        when(zb > z, lambda: leave(True))
        when(zb < z, lambda: leave(False))

    def t_stage2(zb):
        total = t_mine.at[place_of(zb, y, x)]
        ty_copy(zb).wait_recv()
        add(total, t_two.at[zb])

        def arrive(right):
            tz_copy(zb, right).wait_recv()
            add(total, t_line.at[0 if right else 1, zb])

        on_line(zb, arrive, lambda right: tz_copy(zb, right).start())

    def w_load(a, k):
        src = ins[a].at[k, c * 2 + x] if len(ins[a].shape) == 4 else ins[a].at[k]
        return pltpu.make_async_copy(src, mine[a].at[k], load.at[a, k])

    def wy_copy(a, zb):
        return remote(mine[a].at[zb * 2 + 1 - y], one[a].at[zb], y_send.at[a, zb], y_recv.at[a, zb], ydev)

    def wz_copy(a, zb, right):
        d = 0 if right else 1
        return remote(mine[a].at[zb * 2 + y], line[a].at[d, zb], z_send.at[a, zb], z_recv.at[d, a, zb], zdev(right))

    def w_stage0(zb):
        for a in range(na):
            w_load(a, zb * 2 + 1 - y).wait()
            wy_copy(a, zb).start()

    def w_stage1(zb):
        for a in range(na):
            total = mine[a].at[zb * 2 + y]
            w_load(a, zb * 2 + y).wait()
            wy_copy(a, zb).wait_recv()
            add(total, one[a].at[zb])

            def arrive(right):
                wz_copy(a, zb, right).wait_recv()
                add(total, line[a].at[0 if right else 1, zb])

            on_line(zb, arrive, lambda right: wz_copy(a, zb, right).start())

    for zb in order:
        for yb, xb in combos:
            k = place_of(zb, yb, xb)
            t_core_copy(k).start()
            t_load_copy(k).start()
        for yb in (1 - y, y):
            for a in range(na):
                w_load(a, zb * 2 + yb).start()
    for i in range(nz):
        if i < 2:
            w_stage0(order[i])
        t_stage0(order[i])
    for i in range(nz):
        t_stage1(order[i])
        if i + 2 < nz:
            w_stage0(order[i + 2])
        w_stage1(order[i])
        t_stage2(order[i])

    here = t_mine.at[place_of(z, y, x)]
    for right, ok in ((True, z >= 1), (False, z + 1 < nz)):

        def last(right=right):
            tz_copy(z, right).wait_recv()

        when(ok, last)
    rows = 16

    def body(i, sums):
        r = pl.ds(pl.multiple_of(i * rows, rows), rows)
        left = jnp.where(z >= 1, t_line[0, z, r].astype(jnp.float32), 0.0)
        right = jnp.where(z + 1 < nz, t_line[1, z, r].astype(jnp.float32), 0.0)
        v = here[r].astype(jnp.float32) + left + right
        total = mid[r] + v
        res_o[r] = total.astype(res_o.dtype)
        fold = lambda u: jnp.sum((u * u).reshape(rows, -1, 128), axis=(0, 1))[None]
        terms = (stream[r].astype(jnp.float32), attn[r], mid[r], v, total)
        return tuple(s + fold(u) for s, u in zip(sums, terms))

    sums = lax.fori_loop(0, mid.shape[0] // rows, body, (jnp.zeros((1, 128), jnp.float32),) * 5)
    stat[...] = jnp.concatenate(sums + (jnp.zeros((3, 128), jnp.float32),), axis=0)
    rounds = ["c", "x", "y"] + ["z%d" % b for b in bits]

    def stat_copy(i):
        return remote(stat, stat_in.at[i], st_send.at[i], st_recv.at[i], nbr[rounds[i]][0])

    def stat_next(i):
        if 0 < i <= len(rounds):
            stat_copy(i - 1).wait()
            stat[...] = stat[...] + stat_in[i - 1]
        if i < len(rounds):
            stat_copy(i).start()

    stat_next(0)

    k = z * 2 + y
    member, group = c * 2 + x, x * 2 + c
    waits = []
    spread = {0: q_all, 1: kv_all, na - 1: side_all}
    for n_done, a in enumerate((2, 0, 1, 3, 4, na - 1)):
        total = mine[a].at[k]

        def fin(right):
            wz_copy(a, z, right).wait_recv()
            add(total, line[a].at[0 if right else 1, z])

        when(z >= 1, lambda: fin(True))
        when(z + 1 < nz, lambda: fin(False))
        if a in spread:
            dst = spread[a]
            part = dst.shape[1]
            piece = lambda m: total if a == na - 1 else total.at[pl.ds(pl.multiple_of(m * part, part), part)]
            d = pltpu.make_async_copy(piece(member), dst.at[group], own_sem.at[a])
            d.start()
            waits.append(d)
            for i, (dev, cc, xx) in enumerate(((xdev, c, 1 - x), (cdev, 1 - c, x), (ddev, 1 - c, 1 - x))):
                d = remote(piece(cc * 2 + xx), dst.at[group], q_send.at[a, i], q_recv.at[a, i], dev)
                d.start()
                waits.append(d)
        elif a == 2:
            to = remote(total, out_all, out_send, out_recv, nbr["to"][0])
            stay = pltpu.make_async_copy(total, out_all, own_sem.at[a])
            when(away, lambda: to.start())
            when(jnp.logical_not(away), lambda: stay.start())

        stat_next(n_done + 1)
    for i in range(na + 1, len(rounds) + 1):
        stat_next(i)
    stat_o[...] = stat[...]
    router_o[...] = mine[4][k].astype(jnp.float32)
    lat_o[...] = mine[3][k].astype(jnp.float32)
    when(away, lambda: to.wait())
    when(jnp.logical_not(away), lambda: stay.wait())
    out_o[...] = out_all[...].astype(jnp.float32)
    for d in waits:
        d.wait()
    for g in range(4):
        for dst, src in ((q_o, q_all), (kv_o, kv_all)):
            n = src.shape[2]
            dst[:, g * n : (g + 1) * n] = src[g].astype(jnp.float32)
    side_o[...] = side_all[0] + side_all[1] + side_all[2] + side_all[3]

    for zb in order:
        for yb, xb in combos:
            t_core_copy(place_of(zb, yb, xb)).wait_send()
        for yb in (1 - y, y):
            tx_copy(zb, yb).wait_send()
        ty_copy(zb).wait_send()
        on_line(zb, lambda right: None, lambda right: tz_copy(zb, right).wait_send())
        for a in range(na):
            wy_copy(a, zb).wait_send()
            on_line(zb, lambda right: None, lambda right: wz_copy(a, zb, right).wait_send())


def finish(own, far, stream, attn, mid, arrays, nz, cid):
    na = len(arrays)
    tok, width = mid.shape
    n, quads = 4 * nz, 2 * nz
    f32, b16, sd = jnp.float32, own.dtype, jax.ShapeDtypeStruct
    q, kv, out, lat, router, side = arrays
    vmem = pl.BlockSpec(memory_space=pltpu.VMEM)
    shapes = [
        sd((tok, width), b16), sd((q.shape[1] // 4, 4 * q.shape[2]), f32), sd((kv.shape[1] // 4, 4 * kv.shape[2]), f32),
        sd(out.shape[1:], f32), sd(lat.shape[2:], f32), sd(router.shape[2:], f32), sd(side.shape[1:], f32), sd((8, 128), f32),
    ]
    buf = lambda *shape: pltpu.VMEM(shape, b16)
    return pl.pallas_call(
        functools.partial(finish_kernel, nz, na),
        out_shape=shapes,
        in_specs=[HBM, HBM, vmem, vmem, vmem] + [HBM] * na,
        out_specs=[vmem] * 8,
        scratch_shapes=[buf(n, tok, width), buf(n, tok, width), buf(quads, tok, width), buf(nz, tok, width),
                        buf(2, nz, tok, width), pltpu.VMEM((8, 128), f32)]
        + [pltpu.VMEM((quads,) + v.shape[-2:], v.dtype) for v in arrays]
        + [pltpu.VMEM((nz,) + v.shape[-2:], v.dtype) for v in arrays]
        + [pltpu.VMEM((2, nz) + v.shape[-2:], v.dtype) for v in arrays]
        + [buf(4, q.shape[1] // 4, q.shape[2]), buf(4, kv.shape[1] // 4, kv.shape[2]), buf(*out.shape[1:]),
           pltpu.VMEM((4,) + side.shape[1:], f32), pltpu.VMEM((8, 128), f32), pltpu.VMEM((8, 8, 128), f32)]
        + [SEM((n,)), SEM((n,)), SEM((n,)), SEM((quads,)), SEM((quads,)), SEM((nz,)), SEM((nz,)), SEM((nz,)), SEM((2, nz)),
           SEM((na, quads)), SEM((na, nz)), SEM((na, nz)), SEM((na, nz)), SEM((2, na, nz)), SEM((na,)), SEM((na, 3)),
           SEM((na, 3)), SEM, SEM, SEM((8,)), SEM((8,))],
        cost_estimate=lasting(130),
        compiler_params=pltpu.CompilerParams(collective_id=cid, has_side_effects=True, vmem_limit_bytes=58 << 20),
    )(own, far, stream, attn, mid, *arrays)


def silu_parts(values):
    sigmoid = jax.nn.sigmoid(values)
    return values * sigmoid, sigmoid * (1.0 + values * (1.0 - sigmoid))


def experts_kernel(nt_ref, sg_ref, tail_ref, wg_ref, wu_ref, wd_ref, ws_ref, wsd_ref,
                   own_ref, far_ref, ng_ref, dwg_hbm, dwu_hbm, dwd_hbm, dws_out, dsd_ref,
                   dwg, dwu, dwd, dws_ref, sem, *, slots):
    f32, b16 = jnp.float32, jnp.bfloat16
    i = pl.program_id(0)
    @pl.when(i == 0)
    def _():
        for r in (dwg, dwu, dwd, dws_ref, dsd_ref):
            r[...] = jnp.zeros_like(r)
    tokens = nt_ref.shape[0] * nt_ref.shape[1]
    width = nt_ref.shape[2]
    nt = nt_ref[...].reshape(tokens, width)
    sg = sg_ref[...].reshape(tokens, width)
    blocks, tok = nt_ref.shape[:2]
    lines = tail_ref.shape[1] // 2
    me = lax.axis_index("rep")
    gate_row = tail_ref[:, pl.ds(me, 1), :].reshape(blocks, tok)
    named = tail_ref[:, pl.ds(lines + me, 1), :].reshape(blocks, tok)
    before = lax.broadcasted_iota(jnp.int32, (tok, tok), 0) < lax.broadcasted_iota(jnp.int32, (tok, tok), 1)
    rank = wide_product(named.astype(b16), before.astype(f32).astype(b16)).astype(jnp.int32)
    rank = rank + lax.broadcasted_iota(jnp.int32, (blocks, tok), 0) * (slots // blocks)
    place_of = jnp.where(named > 0, rank, -1)
    in_row = lambda v: jnp.concatenate([v[j : j + 1] for j in range(blocks)], axis=1)
    hit = lax.broadcasted_iota(jnp.int32, (slots, tokens), 0) == in_row(place_of)
    pick = hit.astype(f32).astype(b16)
    x = wide_product(pick, nt).astype(b16)
    g0 = wide_product(pick, sg)
    gate = jnp.sum(jnp.where(hit, in_row(gate_row), 0.0), axis=1, keepdims=True)
    g = (gate * g0).astype(b16)
    gv = dot_nt(x, wg_ref[...])
    uv = dot_nt(x, wu_ref[...])
    act, slope = silu_parts(gv)
    hid = (act * uv).astype(b16)
    part = wide_product(hid, wd_ref[...])
    gg = jnp.sum(g0 * part, axis=1, keepdims=True)
    gg_high = gg.astype(b16).astype(f32)
    column = lax.axis_index("rep") * 4 + lax.axis_index("shard") * 2
    lane = lax.broadcasted_iota(jnp.int32, (slots, 128), 1)
    gg = jnp.where(lane == column, gg_high, jnp.where(lane == column + 1, gg - gg_high, 0.0)).astype(b16)
    e_out = (gate * part).astype(b16)
    dwd[...] += dot_tn(hid, g)
    hg = dot_nt(g, wd_ref[...])
    dg = (hg * uv * slope).astype(b16)
    du = (hg * act).astype(b16)
    dwg[...] += dot_tn(dg, x)
    dwu[...] += dot_tn(du, x)
    ing = (wide_product(dg, wg_ref[...]) + wide_product(du, wu_ref[...])).astype(b16)
    fs = wsd_ref.shape[0]
    s = wide_product(nt, ws_ref[...])
    sgv, suv = s[:, :fs], s[:, fs:]
    sact, sslope = silu_parts(sgv)
    sh = (sact * suv).astype(b16)
    shg = dot_nt(sg, wsd_ref[...])
    ds = jnp.concatenate([shg * suv * sslope, shg * sact], axis=1).astype(b16)
    dsd_ref[...] += dot_tn(sh, sg)
    dws_ref[...] += dot_tn(ds, nt)
    out = wide_product(sh, wsd_ref[...]) + dot_tn(pick, e_out)
    out = out.astype(b16).reshape(nt_ref.shape)
    c = lax.rem(lax.axis_index("rep"), 2)
    for j in (0, 1):

        @pl.when(c == j)
        def _(j=j):
            own_ref[...] = out[2 * j : 2 * j + 2]
            far_ref[...] = out[2 - 2 * j : 4 - 2 * j]

    ng = dot_nt(ds, ws_ref[...]) + dot_tn(pick, ing)
    ng_ref[:, :, :width] = ng.astype(b16).reshape(nt_ref.shape)
    ng_ref[:, :, width:] = dot_tn(pick, gg).astype(b16).reshape(ng_ref.shape[:2] + (128,))
    @pl.when(i == pl.num_programs(0) - 1)
    def _():
        cs = [pltpu.make_async_copy(a, b, sem.at[j]) for j, (a, b) in enumerate(((dwg, dwg_hbm), (dwu, dwu_hbm), (dwd, dwd_hbm)))]
        for c in cs: c.start()
        dws_out[...] = dws_ref[...].T.astype(b16)
        for c in cs: c.wait()

def experts_both(nt, sg, tails, wg, wu, wd, ws, wsd, capacity, blocks=4):
    n, tok, width = nt.shape
    steps = n // blocks
    f = wg.shape[0]; fs = wsd.shape[0]
    f32 = jnp.float32
    one = lambda a: pl.BlockSpec(a.shape, lambda i: (0,) * a.ndim, pipeline_mode=pl.Buffered(1))
    blk = pl.BlockSpec((blocks, tok, width), lambda i: (i, 0, 0))
    half = pl.BlockSpec((blocks // 2, tok, width), lambda i: (i, 0, 0))
    row = pl.BlockSpec((blocks,) + tails.shape[1:], lambda i: (i, 0, 0))
    sd = jax.ShapeDtypeStruct
    anyspec = HBM
    acc = pltpu.VMEM((f, width), f32)
    return pl.pallas_call(
        functools.partial(experts_kernel, slots=blocks * capacity),
        grid=(steps,),
        in_specs=[blk, blk, row] + [one(w) for w in (wg, wu, wd, ws, wsd)],
        out_specs=[half, half, pl.BlockSpec((blocks, tok, width + 128), lambda i: (i, 0, 0)), anyspec, anyspec, anyspec,
                   pl.BlockSpec((width, 2 * fs), lambda i: (0, 0)), pl.BlockSpec((fs, width), lambda i: (0, 0))],
        out_shape=[sd((n // 2, tok, width), nt.dtype)] * 2 + [sd((n, tok, width + 128), nt.dtype),
                   sd((f, width), f32), sd((f, width), f32), sd((f, width), f32),
                   sd((width, 2 * fs), nt.dtype), sd((fs, width), f32)],
        scratch_shapes=[acc, acc, acc, pltpu.VMEM((2 * fs, width), f32), SEM((3,))],
        compiler_params=pltpu.CompilerParams(vmem_limit_bytes=64 << 20, dimension_semantics=("arbitrary",)),
        cost_estimate=lasting(110),
    )(nt, sg, tails, wg, wu, wd, ws, wsd)


def swap(v, nz, f):
    pairs = [
        (slot(*f(z, y, c, x)), slot(z, y, c, x))
        for z in range(nz) for y in range(2) for c in range(2) for x in range(2)
    ]
    return lax.ppermute(v, ("rep", "shard"), pairs)


def on_device(
    stream_in, stream_grad, prefix_len, routes, route_weight, attn_gain, query_proj, latent_proj, rope_key_proj,
    latent_gain, kv_up_proj, out_proj, ffn_gain, router_proj, shared_gate, shared_up, shared_down, expert_gate,
    expert_up, expert_down,
):
    f32, b16 = jnp.float32, jnp.bfloat16
    both = ("rep", "shard")
    n_shard, n_rep = lax.axis_size("shard"), lax.axis_size("rep")
    n_dev = n_rep * n_shard
    nz = n_rep // 4
    quads = n_rep // 2
    rep, x = lax.axis_index("rep"), lax.axis_index("shard")
    c = lax.rem(rep, 2)
    member, group = c * 2 + x, x * 2 + c
    tok, width = stream_in.shape
    experts = router_proj.shape[1]
    capacity = max(2, tok * TOP_K * 7 // (6 * experts))
    seq = n_shard * tok
    scale = (DN + DR) ** (-0.5)
    heads = H // 4
    qcols, kcols = heads * (DN + DR), heads * (DN + DV)
    kvr = latent_proj.shape[1]
    lanes = kvr + DR

    dh = width // n_shard
    gl = jnp.pad(latent_gain, (0, dh - kvr // n_shard))
    tiny = jnp.concatenate([rope_key_proj.T, router_proj.T, attn_gain[None], ffn_gain[None], gl[None]], axis=0)
    tiny = jnp.pad(tiny, ((0, -tiny.shape[0] % 16), (0, 0)))
    stream_all, mat_q, mat_kv, mat_lat, tiny = open_quad(stream_in, query_proj, kv_up_proj, latent_proj, tiny, nz, 1)
    mat_q = mat_q.reshape(width, qcols)
    mat_kv = mat_kv.reshape(kvr, kcols)
    mat_lat = mat_lat.reshape(width, kvr)
    joined = jnp.concatenate([tiny[0], tiny[1]], axis=1)
    rope_t, router_t = joined[:DR], joined[DR : DR + experts]
    gain_attn = joined[DR + experts].astype(f32)
    gain_ffn = joined[DR + experts + 1].astype(f32)
    gain_latent = tiny[:, DR + experts + 2, : kvr // n_shard].reshape(kvr).astype(f32)
    mat_out = lax.dynamic_slice_in_dim(out_proj, c * heads * DV, heads * DV, 0)

    late_grad, stream_all = lax.optimization_barrier((stream_grad, stream_all))
    grad_all = lax.all_gather(late_grad, both, axis=0)
    one_hot = (routes[:, :, None] == jnp.arange(experts)[None, None, :]).astype(f32)
    mask = jnp.sum(one_hot, axis=1)
    weight = jnp.sum(one_hot * route_weight[:, :, None], axis=1)
    fs = shared_down.shape[0]
    lanes_s = -(-fs // 128) * 128
    own_w = width // n_dev
    split = split_units(shared_gate, shared_up, n_dev, fs)
    w_s = lax.all_to_all(split, both, split_axis=0, concat_axis=0, tiled=True).reshape(width, 2 * lanes_s)
    w_sd = jnp.pad(shared_down, ((0, lanes_s - fs), (0, 0)))

    stream4 = stream_all.reshape(4 * tok, width).astype(f32)
    normed = (stream4 * rms_scale(stream4) * gain_attn).astype(b16)
    positions = jnp.arange(seq)
    cosine, sine = rope_tables(positions, DR)
    q_raw = wide_product(normed, mat_q).reshape(2, seq, heads, DN + DR)
    q_nope = q_raw[..., :DN].astype(b16)
    q_rot = rotate(q_raw[..., DN:], cosine[:, None], sine[:, None]).astype(b16)
    latent = wide_product(normed, mat_lat)
    scale_lat = rms_scale(latent)
    latent_normed = (latent * scale_lat * gain_latent).astype(b16)
    k_rot = rotate(dot_nt(normed, rope_t).reshape(2, seq, DR), cosine, sine).astype(b16)
    keyval = wide_product(latent_normed, mat_kv).astype(b16).reshape(2, seq, heads, DN + DV)
    k_nope, values = keyval[..., :DN], keyval[..., DN:]
    prefix = lax.dynamic_slice_in_dim(prefix_len, rep - c, 2)
    allowed = (positions[None, None, :] <= positions[None, :, None]) | (positions[None, None, :] < prefix[:, None, None])
    allowed = allowed[:, None]
    raw = contract(q_nope, k_nope, ((3,), (3,)), ((0, 2), (0, 2)))
    raw = raw + jnp.swapaxes(contract(q_rot, k_rot, ((3,), (2,)), ((0,), (0,))), 1, 2)
    scores = jnp.where(allowed, raw * scale, MASKED)
    expo = jnp.exp(scores - jnp.max(scores, axis=-1, keepdims=True))
    probs = expo / jnp.sum(expo, axis=-1, keepdims=True)
    probs_low = probs.astype(b16)
    attended = jnp.swapaxes(contract(probs_low, values, ((3,), (1,)), ((0, 1), (0, 2))), 1, 2)
    attended = attended.astype(b16).reshape(4 * tok, heads * DV)
    part = wide_product(attended, mat_out).astype(b16).reshape(4, tok, width)
    attn_out = quad_scatter(part, 3)
    stream = stream_in.astype(f32)
    mid = stream + attn_out
    scale_two = rms_scale(mid)
    normed_two = (mid * scale_two * gain_ffn).astype(b16)

    router_prob = jax.nn.softmax(dot_nt(normed_two, router_t), axis=-1)
    picked = mask * router_prob
    picked_sum = jnp.sum(picked, axis=-1, keepdims=True)
    gates = weight * picked / picked_sum
    nt_all, tails = all_gather(normed_two, jnp.concatenate([gates.T, mask.T], axis=0), n_dev, nz, 4)

    mats = (jnp.swapaxes(expert_gate, 1, 2)[0], jnp.swapaxes(expert_up, 1, 2)[0], expert_down[0], w_s, w_sd)
    out_own, out_far, n_grad, grad_eg, grad_eu, grad_ed, grad_s, grad_sd = experts_both(
        nt_all, grad_all, tails, *mats, capacity, 4)
    n_grad = reduce_scatter(n_grad, nz, 16)
    back = lax.all_to_all(grad_s.reshape(n_dev, own_w, 2 * lanes_s), both, split_axis=0, concat_axis=0, tiled=True)
    back = join_units(back, n_dev * fs, fs)
    gate_grad = jnp.sum(n_grad[:, width : width + 4 * experts].reshape(tok, experts, 4), axis=-1)
    n_grad = n_grad[:, :width]

    weighted = weight * gate_grad
    picked_grad = weighted / picked_sum - jnp.sum(weighted * picked, axis=-1, keepdims=True) / (picked_sum * picked_sum)
    prob_grad = mask * picked_grad
    logit_grad = (router_prob * (prob_grad - jnp.sum(router_prob * prob_grad, axis=-1, keepdims=True))).astype(b16)
    n_grad = n_grad + wide_product(logit_grad, router_t)
    norm_part, ffn_gain_grad = norm_back(n_grad, mid, scale_two, gain_ffn)
    mid_grad = stream_grad.astype(f32) + norm_part
    aog = mid_grad.astype(b16)
    tail = jnp.pad(logit_grad, ((0, 0), (0, 128 - experts)))
    aog_all = quad_gather(jnp.concatenate([aog, tail], axis=1), 7).reshape(4 * tok, width + 128)
    logit_all = aog_all[:, width:]
    aog_all = aog_all[:, :width]

    att_grad = dot_nt(aog_all, mat_out).astype(b16)
    grad_out = dot_tn(attended, aog_all)
    att_grad = att_grad.reshape(2, seq, heads, DV)
    value_grad = jnp.swapaxes(contract(probs_low, att_grad, ((2,), (1,)), ((0, 1), (0, 2))), 1, 2)
    prob_grad_a = contract(att_grad, values, ((3,), (3,)), ((0, 2), (0, 2)))
    s_grad = probs * (prob_grad_a - jnp.sum(probs * prob_grad_a, axis=-1, keepdims=True))
    s_grad = s_grad.astype(b16)
    qn_grad = scale * jnp.swapaxes(contract(s_grad, k_nope, ((3,), (1,)), ((0, 1), (0, 2))), 1, 2)
    qr_grad = scale * jnp.swapaxes(contract(s_grad, k_rot, ((3,), (1,)), ((0,), (0,))), 1, 2)
    kn_grad = scale * jnp.swapaxes(contract(s_grad, q_nope, ((2,), (1,)), ((0, 1), (0, 2))), 1, 2)
    kr_grad = scale * contract(s_grad, q_rot, ((1, 2), (2, 1)), ((0,), (0,)))
    keyval_grad = jnp.concatenate([kn_grad, value_grad], axis=-1).astype(b16).reshape(4 * tok, kcols)
    qr_grad = rotate(qr_grad, cosine[:, None], -sine[:, None])
    query_grad = jnp.concatenate([qn_grad, qr_grad], axis=-1).astype(b16).reshape(4 * tok, qcols)
    lat_part = dot_nt(keyval_grad, mat_kv)
    lat_part = jnp.concatenate([lat_part, kr_grad.reshape(4 * tok, DR)], axis=1).astype(b16)
    lat_part = lat_part.astype(f32) + swap(lat_part, nz, lambda z, y, c, x: (z, y, c, 1 - x)).astype(f32)
    lat_part = lat_part.astype(b16)
    lat_sum = lat_part.astype(f32) + swap(lat_part, nz, lambda z, y, c, x: (z, y, 1 - c, x)).astype(f32)
    lat_sum, kr_sum = lat_sum[:, :kvr], lat_sum[:, kvr:lanes].reshape(2, seq, DR)
    key_pre = rotate(kr_sum, cosine, -sine).reshape(4 * tok, DR).astype(b16)
    weighted_l = lat_sum * gain_latent
    inner = jnp.mean(weighted_l * latent, axis=-1, keepdims=True)
    latent_pre = scale_lat * weighted_l - latent * (scale_lat * scale_lat * scale_lat) * inner
    lat_gain_rows = lat_sum * latent * scale_lat
    lat_gain_grad = jnp.sum(lax.dynamic_slice_in_dim(lat_gain_rows, member * tok, tok, 0), axis=0)
    lat_grad = jnp.concatenate([latent_pre.astype(b16), key_pre], axis=1)
    part = dot_nt(query_grad, mat_q)
    normed_grad = quad_scatter(part.astype(b16).reshape(4, tok, width), 9)
    lat_own = lax.dynamic_slice_in_dim(lat_grad, member * tok, tok, 0)
    normed_grad = normed_grad + dot_nt(lat_own[:, :kvr], mat_lat) + wide_product(lat_own[:, kvr:], rope_t)
    attn_part, attn_gain_grad = norm_back(normed_grad, stream, rms_scale(stream), gain_attn)
    grad_stream = (mid_grad + attn_part).astype(b16)

    gq = dot_tn(normed, query_grad).astype(b16)
    gkv = dot_tn(latent_normed, keyval_grad).astype(b16)
    nt_quad = lax.dynamic_slice_in_dim(nt_all, (rep // 2) * 4, 4, 0).reshape(4 * tok, width)
    lat_grad = jnp.pad(lat_grad, ((0, 0), (0, -lanes % 128)))
    glat = dot_tn(normed, lat_grad).astype(b16).reshape(quads, 4, own_w, -1)
    grouter = dot_tn(nt_quad, logit_all).astype(b16).reshape(quads, 4, own_w, -1)
    side = jnp.concatenate([v.reshape(quads, -1) for v in (attn_gain_grad, ffn_gain_grad, lat_gain_grad)], axis=1)
    side = jnp.pad(side, ((0, 0), (0, 1024 - side.shape[1]))).reshape(quads, 8, 128)
    stream_out, o_q, o_kv, o_out, o_lat, o_router, o_side, o_stat = finish(
        out_own, out_far, stream_in, attn_out, mid,
        [gq.reshape(quads, -1, qcols), gkv.reshape(quads, -1, kcols), grad_out.astype(b16).reshape(quads, -1, width), glat, grouter, side],
        nz, 10)
    o_side = o_side.reshape(-1)
    per = width // quads
    perl = kvr // quads
    ga = lax.dynamic_slice_in_dim(o_side, member * own_w, own_w)
    gf = lax.dynamic_slice_in_dim(o_side, per + member * own_w, own_w)
    gla = lax.dynamic_slice_in_dim(o_side, 2 * per + member * (perl // 4), perl // 4)
    stats = jnp.sqrt(jnp.sum(o_stat[:5], axis=1) / (tok * n_dev * width))
    return (
        stream_out, grad_stream, stats, ga, o_q, o_lat[:, :kvr], o_lat[:, kvr:lanes], gla, o_kv, o_out, gf,
        o_router[:, :experts], back[0], back[1], grad_sd[:fs], jnp.swapaxes(grad_eg[None], 1, 2), jnp.swapaxes(grad_eu[None], 1, 2), grad_ed[None],
    )


def on_device_weights(
    stream_in,
    stream_grad,
    prefix_len,
    routes,
    route_weight,
    attn_gain,
    query_proj,
    latent_proj,
    rope_key_proj,
    latent_gain,
    kv_up_proj,
    out_proj,
    ffn_gain,
    router_proj,
    shared_gate,
    shared_up,
    shared_down,
    expert_gate,
    expert_up,
    expert_down,
):
    n_shard = lax.axis_size("shard")
    n_rep = lax.axis_size("rep")
    rep_index = lax.axis_index("rep")
    shard_index = lax.axis_index("shard")
    tok_rows = stream_in.shape[0]
    seq_len = n_shard * tok_rows
    experts = router_proj.shape[1]
    capacity = max(2, tok_rows * TOP_K * 7 // (6 * experts))
    head_width = H * (DN + DV)
    kv_rows = tok_rows * head_width // 128
    rope_rows = tok_rows * DR // 128
    piece_rows = kv_rows + rope_rows
    score_scale = (DN + DR) ** (-0.5)
    weights = (
        attn_gain,
        query_proj,
        latent_proj,
        rope_key_proj,
        latent_gain,
        kv_up_proj,
        out_proj,
        ffn_gain,
        router_proj,
    )
    shared_mats = (shared_gate, shared_up, shared_down)
    (
        gain_attn,
        mat_query,
        mat_latent,
        mat_rope,
        gain_latent,
        mat_kv,
        mat_out,
        gain_ffn,
        mat_router,
    ) = (
        lax.all_gather(weights[0], "shard", axis=0, tiled=True),
        lax.all_gather(weights[1], "shard", axis=0, tiled=True),
        lax.all_gather(weights[2], "shard", axis=0, tiled=True),
        lax.all_gather(weights[3], "shard", axis=0, tiled=True),
        lax.all_gather(weights[4], "shard", axis=0, tiled=True),
        lax.all_gather(weights[5], "shard", axis=0, tiled=True),
        lax.all_gather(weights[6], "shard", axis=0, tiled=True),
        lax.all_gather(weights[7], "shard", axis=0, tiled=True),
        lax.all_gather(weights[8], "shard", axis=0, tiled=True),
    )
    mat_sgate, mat_sup, mat_sdown = (
        lax.all_gather(shared_mats[0], ("rep", "shard"), axis=0, tiled=True),
        lax.all_gather(shared_mats[1], ("rep", "shard"), axis=0, tiled=True),
        lax.all_gather(shared_mats[2], ("rep", "shard"), axis=0, tiled=True),
    )
    gain_attn = gain_attn.astype(jnp.float32)
    gain_latent = gain_latent.astype(jnp.float32)
    gain_ffn = gain_ffn.astype(jnp.float32)
    stream = stream_in.astype(jnp.float32)
    scale_one = rms_scale(stream)
    normed = (stream * scale_one * gain_attn).astype(jnp.bfloat16)
    positions = shard_index * tok_rows + jnp.arange(tok_rows)
    cosine, sine_vals = rope_tables(positions, DR)
    query_raw = wide_product(normed, mat_query).reshape(tok_rows, H, DN + DR)
    query_nope = query_raw[:, :, :DN].astype(jnp.bfloat16)
    query_rot = rotate(query_raw[:, :, DN:], cosine[:, None], sine_vals[:, None]).astype(
        jnp.bfloat16
    )
    latent = wide_product(normed, mat_latent)
    scale_lat = rms_scale(latent)
    latent_normed = (latent * scale_lat * gain_latent).astype(jnp.bfloat16)
    keyval_own = wide_product(latent_normed, mat_kv).astype(jnp.bfloat16)
    key_rot_own = rotate(wide_product(normed, mat_rope), cosine, sine_vals).astype(jnp.bfloat16)
    packed = jnp.concatenate(
        [keyval_own.reshape(kv_rows, 128), key_rot_own.reshape(rope_rows, 128)], axis=0
    )
    seq_keys = lax.all_gather(packed, "shard", axis=0, tiled=True).reshape(n_shard, piece_rows, 128)
    keyval = seq_keys[:, :kv_rows].reshape(seq_len, H, DN + DV)
    key_rot = seq_keys[:, kv_rows:].reshape(seq_len, DR)
    key_nope = keyval[:, :, :DN]
    values = keyval[:, :, DN:]
    prefix = lax.dynamic_index_in_dim(prefix_len, rep_index, keepdims=False)
    key_pos = jnp.arange(seq_len)
    allowed = (key_pos[None, :] <= positions[:, None]) | (key_pos[None, :] < prefix)

    def score_block():
        raw = contract(query_nope, key_nope, ((2,), (2,)), ((1,), (1,)))
        raw = raw + jnp.transpose(contract(query_rot, key_rot, ((2,), (1,)), ((), ())), (1, 0, 2))
        return jnp.where(allowed[None], raw * score_scale, MASKED)

    scores = score_block()
    top_score = jnp.max(scores, axis=-1, keepdims=True)
    expo = jnp.exp(scores - top_score)
    total_exp = jnp.sum(expo, axis=-1, keepdims=True)
    log_total = top_score + jnp.log(total_exp)
    probs_low = (expo / total_exp).astype(jnp.bfloat16)
    attended = jnp.transpose(contract(probs_low, values, ((2,), (0,)), ((0,), (1,))), (1, 0, 2))
    attended = attended.reshape(tok_rows, H * DV).astype(jnp.bfloat16)
    attn_out = wide_product(attended, mat_out)
    mid = stream + attn_out
    scale_two = rms_scale(mid)
    normed_two = (mid * scale_two * gain_ffn).astype(jnp.bfloat16)
    router_prob = jax.nn.softmax(wide_product(normed_two, mat_router), axis=-1)
    one_hot = (routes[:, :, None] == jnp.arange(experts)[None, None, :]).astype(jnp.float32)
    picked = jnp.sum(one_hot * router_prob[:, None, :], axis=-1)
    picked_sum = jnp.sum(picked, axis=-1, keepdims=True)
    gates = route_weight * picked / picked_sum
    sgate_val = wide_product(normed_two, mat_sgate)
    sup_val = wide_product(normed_two, mat_sup)
    shared_hidden = (jax.nn.silu(sgate_val) * sup_val).astype(jnp.bfloat16)
    shared_out = wide_product(shared_hidden, mat_sdown)
    flat_routes = routes.reshape(-1)
    route_hot = (flat_routes[:, None] == jnp.arange(experts)[None, :]).astype(jnp.int32)
    route_rank = jnp.sum((jnp.cumsum(route_hot, axis=0) - route_hot) * route_hot, axis=1)
    slot_index = flat_routes * capacity + route_rank
    send_rows = (
        jnp.zeros((experts * capacity, D), jnp.bfloat16)
        .at[slot_index]
        .set(jnp.repeat(normed_two, TOP_K, axis=0))
    )
    doubled = jnp.broadcast_to(
        send_rows.reshape(experts, 1, capacity, D), (experts, n_shard, capacity, D)
    ).reshape(-1, D)
    incoming_rows = lax.all_to_all(
        doubled, ("rep", "shard"), split_axis=0, concat_axis=0, tiled=True
    )
    gate_local = expert_gate[0]
    local_up_weight = expert_up[0]
    down_local = expert_down[0]
    expert_gate_value = wide_product(incoming_rows, gate_local)
    expert_up_value = wide_product(incoming_rows, local_up_weight)
    expert_inner_state = (jax.nn.silu(expert_gate_value) * expert_up_value).astype(jnp.bfloat16)
    expert_part = wide_product(expert_inner_state, down_local).astype(jnp.bfloat16)
    returned = lax.all_to_all(
        expert_part, ("rep", "shard"), split_axis=0, concat_axis=0, tiled=True
    )
    expert_sum = jnp.sum(
        returned.reshape(experts, n_shard, capacity, D).astype(jnp.float32), axis=1
    ).reshape(experts * capacity, D)
    picked_rows = expert_sum[slot_index].reshape(tok_rows, TOP_K, D)
    ffn_out = shared_out + jnp.sum(gates[:, :, None] * picked_rows, axis=1)
    residual = mid + ffn_out
    squares = jnp.stack(
        [
            jnp.sum(stream * stream),
            jnp.sum(attn_out * attn_out),
            jnp.sum(mid * mid),
            jnp.sum(ffn_out * ffn_out),
            jnp.sum(residual * residual),
        ]
    )
    totals = lax.psum(squares, ("rep", "shard"))
    stats = jnp.sqrt(totals / (tok_rows * n_rep * n_shard * D))
    (
        gain_attn,
        mat_query,
        mat_latent,
        mat_rope,
        gain_latent,
        mat_kv,
        mat_out,
        gain_ffn,
        mat_router,
    ) = (
        lax.all_gather(weights[0], "shard", axis=0, tiled=True),
        lax.all_gather(weights[1], "shard", axis=0, tiled=True),
        lax.all_gather(weights[2], "shard", axis=0, tiled=True),
        lax.all_gather(weights[3], "shard", axis=0, tiled=True),
        lax.all_gather(weights[4], "shard", axis=0, tiled=True),
        lax.all_gather(weights[5], "shard", axis=0, tiled=True),
        lax.all_gather(weights[6], "shard", axis=0, tiled=True),
        lax.all_gather(weights[7], "shard", axis=0, tiled=True),
        lax.all_gather(weights[8], "shard", axis=0, tiled=True),
    )
    mat_sgate, mat_sup, mat_sdown = (
        lax.all_gather(shared_mats[0], ("rep", "shard"), axis=0, tiled=True),
        lax.all_gather(shared_mats[1], ("rep", "shard"), axis=0, tiled=True),
        lax.all_gather(shared_mats[2], ("rep", "shard"), axis=0, tiled=True),
    )
    gain_attn = gain_attn.astype(jnp.float32)
    gain_latent = gain_latent.astype(jnp.float32)
    gain_ffn = gain_ffn.astype(jnp.float32)
    grad_top = stream_grad.astype(jnp.float32)
    gate_grad = jnp.sum(grad_top[:, None, :] * picked_rows, axis=-1)
    expert_grad = (gates[:, :, None] * grad_top[:, None, :]).astype(jnp.bfloat16).reshape(-1, D)
    send_grad = jnp.zeros((experts * capacity, D), jnp.bfloat16).at[slot_index].set(expert_grad)
    doubled_grad = jnp.broadcast_to(
        send_grad.reshape(experts, 1, capacity, D), (experts, n_shard, capacity, D)
    ).reshape(-1, D)
    received_grad = lax.all_to_all(
        doubled_grad, ("rep", "shard"), split_axis=0, concat_axis=0, tiled=True
    )
    grad_edown = contract(expert_inner_state, received_grad, ((0,), (0,)), ((), ()))
    inner_state_gradient = contract(received_grad, down_local, ((1,), (1,)), ((), ()))
    gate_value_gradient = (
        inner_state_gradient * expert_up_value * swish_derivative(expert_gate_value)
    ).astype(jnp.bfloat16)
    up_value_gradient = (inner_state_gradient * jax.nn.silu(expert_gate_value)).astype(jnp.bfloat16)
    grad_egate = contract(incoming_rows, gate_value_gradient, ((0,), (0,)), ((), ()))
    expert_up_gradient = contract(incoming_rows, up_value_gradient, ((0,), (0,)), ((), ()))
    part_in_grad = contract(gate_value_gradient, gate_local, ((1,), (1,)), ((), ()))
    part_in_grad = (
        part_in_grad
        + contract(up_value_gradient, local_up_weight, ((1,), (1,)), ((), ()))
    ).astype(jnp.bfloat16)
    returned_grad = lax.all_to_all(
        part_in_grad, ("rep", "shard"), split_axis=0, concat_axis=0, tiled=True
    )
    slot_grad = jnp.sum(
        returned_grad.reshape(experts, n_shard, capacity, D).astype(jnp.float32), axis=1
    ).reshape(experts * capacity, D)
    routed_grad = jnp.sum(slot_grad[slot_index].reshape(tok_rows, TOP_K, D), axis=1)
    shared_hidden_grad = contract(stream_grad, mat_sdown, ((1,), (1,)), ((), ()))
    dshared_gate = (shared_hidden_grad * sup_val * swish_derivative(sgate_val)).astype(jnp.bfloat16)
    dshared_up = (shared_hidden_grad * jax.nn.silu(sgate_val)).astype(jnp.bfloat16)
    weighted_grad = route_weight * gate_grad
    picked_grad = weighted_grad / picked_sum - jnp.sum(
        weighted_grad * picked, axis=-1, keepdims=True
    ) / (picked_sum * picked_sum)
    prob_grad = jnp.sum(one_hot * picked_grad[:, :, None], axis=1)
    logit_grad = (
        router_prob * (prob_grad - jnp.sum(router_prob * prob_grad, axis=-1, keepdims=True))
    ).astype(jnp.bfloat16)
    normed_two_grad = contract(dshared_gate, mat_sgate, ((1,), (1,)), ((), ()))
    normed_two_grad = normed_two_grad + contract(dshared_up, mat_sup, ((1,), (1,)), ((), ()))
    normed_two_grad = normed_two_grad + contract(logit_grad, mat_router, ((1,), (1,)), ((), ()))
    normed_two_grad = normed_two_grad + routed_grad
    norm_part, grad_gain_ffn = norm_back(normed_two_grad, mid, scale_two, gain_ffn)
    mid_grad = grad_top + norm_part
    attn_out_grad = mid_grad.astype(jnp.bfloat16)
    attended_grad = contract(attn_out_grad, mat_out, ((1,), (1,)), ((), ()))
    attended_grad = attended_grad.astype(jnp.bfloat16).reshape(tok_rows, H, DV)
    probs_full = jnp.where(allowed[None], jnp.exp(score_block() - log_total), 0.0)
    value_grad = jnp.transpose(contract(probs_full.astype(jnp.bfloat16), attended_grad, ((1,), (0,)), ((0,), (1,))), (1, 0, 2))
    prob_att_grad = contract(attended_grad, values, ((2,), (2,)), ((1,), (1,)))
    scores_grad = probs_full * (
        prob_att_grad - jnp.sum(probs_full * prob_att_grad, axis=-1, keepdims=True)
    )
    scores_grad = scores_grad.astype(jnp.bfloat16)
    query_nope_grad = score_scale * jnp.transpose(contract(scores_grad, key_nope, ((2,), (0,)), ((0,), (1,))), (1, 0, 2))
    query_rot_grad = score_scale * jnp.transpose(contract(scores_grad, key_rot, ((2,), (0,)), ((), ())), (1, 0, 2))
    key_nope_grad = score_scale * jnp.transpose(contract(scores_grad, query_nope, ((1,), (0,)), ((0,), (1,))), (1, 0, 2))
    key_rot_grad = score_scale * contract(scores_grad, query_rot, ((0, 1,), (1, 0,)), ((), ()))
    keyval_grad_all = jnp.concatenate([key_nope_grad, value_grad], axis=-1).reshape(
        n_shard, kv_rows, 128
    )
    key_grad_pieces = jnp.concatenate(
        [keyval_grad_all, key_rot_grad.reshape(n_shard, rope_rows, 128)], axis=1
    )
    own_keys = lax.psum_scatter(
        key_grad_pieces.reshape(-1, 128).astype(jnp.bfloat16),
        "shard",
        scatter_dimension=0,
        tiled=True,
    ).astype(jnp.float32)
    keyval_grad = own_keys[:kv_rows].reshape(tok_rows, head_width).astype(jnp.bfloat16)
    key_pre_grad = rotate(own_keys[kv_rows:].reshape(tok_rows, DR), cosine, -sine_vals).astype(
        jnp.bfloat16
    )
    query_rot_back = rotate(query_rot_grad, cosine[:, None], -sine_vals[:, None])
    query_grad = (
        jnp.concatenate([query_nope_grad, query_rot_back], axis=-1)
        .reshape(tok_rows, H * (DN + DR))
        .astype(jnp.bfloat16)
    )
    latent_normed_grad = contract(keyval_grad, mat_kv, ((1,), (1,)), ((), ()))
    latent_pre, grad_gain_latent = norm_back(latent_normed_grad, latent, scale_lat, gain_latent)
    latent_grad = latent_pre.astype(jnp.bfloat16)
    normed_grad = contract(query_grad, mat_query, ((1,), (1,)), ((), ()))
    normed_grad = normed_grad + contract(key_pre_grad, mat_rope, ((1,), (1,)), ((), ()))
    normed_grad = normed_grad + contract(latent_grad, mat_latent, ((1,), (1,)), ((), ()))
    attn_part, grad_gain_attn = norm_back(normed_grad, stream, scale_one, gain_attn)
    grad_stream = (mid_grad + attn_part).astype(jnp.bfloat16)
    owned = (
        lax.psum_scatter(
            grad_gain_attn[None][0], ("rep", "shard"), scatter_dimension=0, tiled=True
        ),
        lax.psum_scatter(
            contract(normed, query_grad, ((0,), (0,)), ((), ())),
            ("rep", "shard"),
            scatter_dimension=0,
            tiled=True,
        ),
        lax.psum_scatter(
            contract(normed, latent_grad, ((0,), (0,)), ((), ())),
            ("rep", "shard"),
            scatter_dimension=0,
            tiled=True,
        ),
        lax.psum_scatter(
            contract(normed, key_pre_grad, ((0,), (0,)), ((), ())),
            ("rep", "shard"),
            scatter_dimension=0,
            tiled=True,
        ),
        lax.psum_scatter(
            grad_gain_latent[None][0], ("rep", "shard"), scatter_dimension=0, tiled=True
        ),
        lax.psum_scatter(
            contract(latent_normed, keyval_grad, ((0,), (0,)), ((), ())),
            ("rep", "shard"),
            scatter_dimension=0,
            tiled=True,
        ),
        lax.psum_scatter(
            contract(attended, attn_out_grad, ((0,), (0,)), ((), ())),
            ("rep", "shard"),
            scatter_dimension=0,
            tiled=True,
        ),
        lax.psum_scatter(grad_gain_ffn[None][0], ("rep", "shard"), scatter_dimension=0, tiled=True),
        lax.psum_scatter(
            contract(normed_two, logit_grad, ((0,), (0,)), ((), ())),
            ("rep", "shard"),
            scatter_dimension=0,
            tiled=True,
        ),
        lax.psum_scatter(
            contract(normed_two, dshared_gate, ((0,), (0,)), ((), ())),
            ("rep", "shard"),
            scatter_dimension=0,
            tiled=True,
        ),
        lax.psum_scatter(
            contract(normed_two, dshared_up, ((0,), (0,)), ((), ())),
            ("rep", "shard"),
            scatter_dimension=0,
            tiled=True,
        ),
        lax.psum_scatter(
            contract(shared_hidden, stream_grad, ((0,), (0,)), ((), ())),
            ("rep", "shard"),
            scatter_dimension=0,
            tiled=True,
        ),
    )
    return (
        residual.astype(jnp.bfloat16),
        grad_stream,
        stats,
        owned[0],
        owned[1],
        owned[2],
        owned[3],
        owned[4],
        owned[5],
        owned[6],
        owned[7],
        owned[8],
        owned[9],
        owned[10],
        owned[11],
        grad_egate[None],
        expert_up_gradient[None],
        grad_edown[None],
    )


def by_size(*args):
    tokens = lax.axis_size("rep") * lax.axis_size("shard") * args[0].shape[0]
    return (on_device if tokens * args[0].shape[1] <= 1 << 23 else on_device_weights)(*args)


def solution(mesh):
    placed = (
        P(("rep", "shard"), None),
        P(("rep", "shard"), None),
        P(),
        P(("rep", "shard"), None),
        P(("rep", "shard"), None),
        P("shard"),
        P("shard", None),
        P("shard", None),
        P("shard", None),
        P("shard"),
        P("shard", None),
        P("shard", None),
        P("shard"),
        P("shard", None),
        P(("rep", "shard"), None),
        P(("rep", "shard"), None),
        P(("rep", "shard"), None),
        P("rep", None, "shard"),
        P("rep", None, "shard"),
        P("rep", "shard", None),
    )
    return jax.shard_map(
        by_size,
        mesh=mesh,
        in_specs=placed,
        out_specs=(
            P(("rep", "shard"), None),
            P(("rep", "shard"), None),
            P(),
            P(("rep", "shard")),
            P(("rep", "shard"), None),
            P(("rep", "shard"), None),
            P(("rep", "shard"), None),
            P(("rep", "shard")),
            P(("rep", "shard"), None),
            P(("rep", "shard"), None),
            P(("rep", "shard")),
            P(("rep", "shard"), None),
            P(("rep", "shard"), None),
            P(("rep", "shard"), None),
            P(("rep", "shard"), None),
            P("rep", None, "shard"),
            P("rep", None, "shard"),
            P("rep", "shard", None),
        ),
        check_vma=False,
    )
```

```python
import functools
import jax
import jax.numpy as jnp
from jax import lax
from jax.experimental import pallas as pl
from jax.experimental.pallas import tpu as pltpu
from jax.sharding import PartitionSpec as P

D = 2048
H = 16
DN = 128
DR = 64
DV = 128
TOP_K = 6


EPS = 1e-06
ROPE_BASE = 10000.0
MASKED = -1e30


def wide_product(left, right):
    return jnp.dot(left, right, preferred_element_type=jnp.float32)


def contract(left, right, over, batch=((), ())):
    return lax.dot_general(left, right, (over, batch), preferred_element_type=jnp.float32)


def dot_nt(left, right):
    return contract(left, right, ((1,), (1,)))


def dot_tn(left, right):
    return contract(left, right, ((0,), (0,)))


def rms_scale(values):
    return lax.rsqrt(jnp.mean(values * values, axis=-1, keepdims=True) + EPS)


def norm_back(grad_out, inputs, row_scale, gain_vec):
    weighted = grad_out * gain_vec
    inner_mean = jnp.mean(weighted * inputs, axis=-1, keepdims=True)
    grad_in = row_scale * weighted - inputs * (row_scale * row_scale * row_scale) * inner_mean
    grad_gain = jnp.sum(grad_out * inputs * row_scale, axis=0)
    return (grad_in, grad_gain)


def rope_tables(positions, rope_width):
    frequency = ROPE_BASE ** (-2.0 * jnp.arange(rope_width // 2, dtype=jnp.float32) / rope_width)
    angles = positions.astype(jnp.float32)[:, None] * frequency[None, :]
    return (jnp.cos(angles), jnp.sin(angles))


def rotate(values, cosine, sine_vals):
    half_dim = values.shape[-1] // 2
    low_half = values[..., :half_dim]
    high_half = values[..., half_dim:]
    return jnp.concatenate(
        [low_half * cosine - high_half * sine_vals, high_half * cosine + low_half * sine_vals],
        axis=-1,
    )


def swish_derivative(values):
    sigmoid = jax.nn.sigmoid(values)
    return sigmoid * (1.0 + values * (1.0 - sigmoid))


MESH = pl.DeviceIdType.MESH
SEM = pltpu.SemaphoreType.DMA
HBM = pl.BlockSpec(memory_space=pl.ANY)

def when(ok, f):
    if ok is None: f()
    else: pl.when(ok)(f)

def place():
    rep, x = lax.axis_index("rep"), lax.axis_index("shard")
    return rep // 4, lax.rem(rep // 2, 2), lax.rem(rep, 2), x

def device(z, y, c, x):
    return ((z * 2 + y) * 2 + c, x)

def slot(z, y, c, x):
    return ((z * 2 + y) * 2 + c) * 2 + x

def neighbours(nz):
    z, y, c, x = place()
    return dict(
        zr=(device(z + 1, y, c, x), z + 1 < nz),
        zl=(device(z - 1, y, c, x), z >= 1),
        y=(device(z, 1 - y, c, x), None),
        x=(device(z, y, c, 1 - x), None),
        c=(device(z, y, 1 - c, x), None),
    )

def greet(nbr):
    bar = pltpu.get_barrier_semaphore()
    count = 0
    for dev, ok in nbr.values():
        when(ok, lambda dev=dev: pl.semaphore_signal(bar, inc=1, device_id=dev, device_id_type=MESH))
        count = count + (1 if ok is None else jnp.where(ok, 1, 0))
    pl.semaphore_wait(bar, count)

def gather_kernel(nz, x_ref, t_ref, o_ref, ot_ref, own_sem, z_send, y_send, x_send, c_send, recv, crecv):
    z, y, c, x = place()
    nbr = neighbours(nz)
    greet(nbr)
    half = x_ref.shape[0] // 2
    own = slot(z, y, c, x)
    sems = dict(zr=z_send.at[0], zl=z_send.at[1], y=y_send, x=x_send, c=c_send)

    def move(kind, h, b, mine=False):
        if h == 2:
            src, dst = t_ref if mine else ot_ref.at[b], ot_ref.at[b]
        else:
            rows = pl.ds(h * half, half)
            src, dst = x_ref.at[rows] if mine else o_ref.at[b, rows], o_ref.at[b, rows]
        return pltpu.make_async_remote_copy(
            src_ref=src, dst_ref=dst, send_sem=sems[kind].at[h, b],
            recv_sem=(crecv if kind == "c" else recv).at[h, b], device_id=nbr[kind][0], device_id_type=MESH)

    def schedule(go):
        def send(kind, h, b, mine=False):
            def f():
                for hh in (2, 0) if h == 0 else (1,):
                    d = move(kind, hh, b, mine)
                    d.start() if go else d.wait_send()

            when(nbr[kind][1], f)

        def arrive(h, b):
            if go:
                for hh in (2, 0) if h == 0 else (1,):
                    move("x", hh, b).wait_recv()

        second, third = ("y", "x"), ("x", "y")
        for h in (0, 1):
            send("zr", h, own, True)
            send("zl", h, own, True)
            send(second[h], h, own, True)
        for h in (0, 1):
            send(third[h], h, own, True)
            send("c", h, own, True)
        rounds = [[(z, None)]]
        for s in range(nz - 1):
            rounds.append([(z - 1 - s, z - 1 - s >= 0), (z + 1 + s, z + 1 + s < nz)])

        def drain1(rnd):
            for i, (zb, ok) in enumerate(rnd):
                for h in (0, 1):
                    def f(zb=zb, h=h, i=i):
                        b = slot(zb, y, c, x)
                        arrive(h, b)
                        send("zr" if i == 0 else "zl", h, b)
                        send(second[h], h, b)
                        send(third[h], h, b)
                        send("c", h, b)
                    when(ok, f)

        def drain2(rnd):
            for zb, ok in rnd:
                for h in (0, 1):
                    def f(zb=zb, h=h):
                        b = slot(zb, 1 - y, c, x) if h == 0 else slot(zb, y, c, 1 - x)
                        arrive(h, b)
                        send(third[h], h, b)
                        send("c", h, b)
                    when(ok, f)

        def drain3(rnd):
            for zb, ok in rnd:
                for h in (0, 1):
                    def f(zb=zb, h=h):
                        b = slot(zb, y, c, 1 - x) if h == 0 else slot(zb, 1 - y, c, x)
                        arrive(h, b)
                        send("c", h, b)
                        b = slot(zb, 1 - y, c, 1 - x)
                        arrive(h, b)
                        send("c", h, b)
                    when(ok, f)

        for s in range(nz - 1):
            drain1(rounds[s + 1])
            drain2(rounds[s])
            if s >= 1:
                drain3(rounds[s - 1])
        drain2(rounds[nz - 1])
        drain3(rounds[nz - 2])
        drain3(rounds[nz - 1])

    local = [
        pltpu.make_async_copy(x_ref, o_ref.at[own], own_sem.at[0]),
        pltpu.make_async_copy(t_ref, ot_ref.at[own], own_sem.at[1]),
    ]
    for d in local:
        d.start()
    schedule(True)
    for zb in range(nz):
        for yb in range(2):
            for xb in range(2):
                for h in (2, 0, 1):
                    move("c", h, slot(zb, yb, 1 - c, xb)).wait_recv()
    for d in local:
        d.wait()
    schedule(False)


def all_gather(x, t, n, nz, cid):
    return pl.pallas_call(
        functools.partial(gather_kernel, nz),
        out_shape=[jax.ShapeDtypeStruct((n,) + v.shape, v.dtype) for v in (x, t)],
        in_specs=[pl.BlockSpec(memory_space=pl.ANY)] * 2,
        out_specs=[pl.BlockSpec(memory_space=pl.ANY)] * 2,
        scratch_shapes=[SEM((2,)), SEM((2, 3, n)), SEM((3, n)), SEM((3, n)), SEM((3, n)), SEM((3, n)), SEM((3, n))],
        cost_estimate=lasting(85),
        compiler_params=pltpu.CompilerParams(collective_id=cid, has_side_effects=True),
    )(x, t)


def far_first(nz, z):
    def pick(i):
        total = 0
        for k in range(nz):
            ranked = sorted(range(nz), key=lambda d: (-abs(d - k), -d if k < nz // 2 else d))
            total = total + jnp.where(z == k, ranked[i], 0)
        return total
    return [pick(i) for i in range(nz)]

def add_rows(total, other, lo, other_lo, count):
    step = next(k for k in (32, 16, 8) if count % k == 0)

    def body(i, carry):
        r = pl.ds(pl.multiple_of(lo + i * step, step), step)
        s = pl.ds(pl.multiple_of(other_lo + i * step, step), step)
        total[r] = total[r] + other[s]
        return carry

    lax.fori_loop(0, count // step, body, 0)


def scatter_kernel(nz, x_ref, rows_in, rows_grad, hid, dg, du, o_ref, dwg_o, dwu_o, dwd_o, mine, core, one, two, line,
                   dwg, dwu, dwd, b_in, b_grad, b_hid, b_dg, b_du, load_sem, core_send, core_recv, one_send, one_recv,
                   two_send, two_recv, line_send, line_recv, chunk_sem, out_sem):
    z, y, c, x = place()
    nbr = neighbours(nz)
    greet(nbr)
    T = mine.shape[1]
    half = T // 2
    rows = lambda h: pl.ds(h * half, half)
    place_of = lambda zb, yb, xb: (zb * 2 + yb) * 2 + xb
    count = b_in.shape[1]
    chunks = rows_in.shape[0] // count

    def chunk_copies(i):
        r = pl.ds(i * count, count)
        pairs = ((rows_in, b_in), (rows_grad, b_grad), (hid, b_hid), (dg, b_dg), (du, b_du))
        return [pltpu.make_async_copy(a.at[r], b.at[i % 2], chunk_sem.at[i % 2, j]) for j, (a, b) in enumerate(pairs)]

    def result(j):
        out, b = ((dwg_o, b_in), (dwu_o, b_grad), (dwd_o, b_in))[j]
        spans = [(k, lo, min(count, out.shape[0] - lo)) for k, lo in enumerate(range(0, out.shape[0], count))]
        return spans, [
            pltpu.make_async_copy(b.at[k, pl.ds(0, n)], out.at[pl.ds(lo, n)], out_sem.at[j, k]) for k, lo, n in spans
        ]

    def write(j):
        total, b = ((dwg, b_in), (dwu, b_grad), (dwd, b_in))[j]
        spans, copies = result(j)
        for k, lo, n in spans:
            b[k, 0:n] = total[lo : lo + n].astype(b.dtype)
        for d in copies:
            d.start()

    def written(j):
        for d in result(j)[1]:
            d.wait()

    def chunk(i):
        if i >= chunks:
            return
        for d in chunk_copies(i):
            d.wait()
        k = i % 2
        terms = ((dwd, b_hid, b_grad), (dwg, b_dg, b_in), (dwu, b_du, b_in))
        for total, a, b in terms:
            v = dot_tn(a[k], b[k])
            total[...] = v if i == 0 else total[...] + v
        if i + 2 < chunks:
            for d in chunk_copies(i + 2):
                d.start()
        if i == chunks - 1:
            write(0)
            write(1)

    order = far_first(nz, z)
    combos = [(1 - y, 1 - x), (y, 1 - x), (1 - y, x), (y, x)]

    def core_copy(zb, yb, xb):
        k = place_of(zb, yb, xb)
        return remote(x_ref.at[slot(zb, yb, 1 - c, xb)], core.at[k], core_send.at[k], core_recv.at[k], nbr["c"][0])

    def load(zb, yb, xb):
        k = place_of(zb, yb, xb)
        return pltpu.make_async_copy(x_ref.at[slot(zb, yb, c, xb)], mine.at[k], load_sem.at[k])

    def one_copy(h, zb, j):
        k = place_of(zb, j, 1 - x) if h == 0 else place_of(zb, 1 - y, j)
        i = zb * 2 + j
        return remote(mine.at[k, rows(h)], one.at[h, i], one_send.at[h, i], one_recv.at[h, i], nbr["x" if h == 0 else "y"][0])

    def two_copy(h, zb):
        k = place_of(zb, 1 - y, x) if h == 0 else place_of(zb, y, 1 - x)
        return remote(mine.at[k, rows(h)], two.at[h, zb], two_send.at[h, zb], two_recv.at[h, zb], nbr["y" if h == 0 else "x"][0])

    def line_copy(h, zb, right):
        k = place_of(zb, y, x)
        d = 0 if right else 1
        return remote(mine.at[k, rows(h)], line.at[d, h, zb], line_send.at[h, zb], line_recv.at[d, h, zb], nbr["zr" if right else "zl"][0])

    for zb in order:
        for yb, xb in combos:
            core_copy(zb, yb, xb).start()
            load(zb, yb, xb).start()
    for i in range(min(2, chunks)):
        for d in chunk_copies(i):
            d.start()

    def stage0(zb):
        for n, (yb, xb) in enumerate(combos):
            k = place_of(zb, yb, xb)
            core_copy(zb, yb, xb).wait_recv()
            load(zb, yb, xb).wait()
            add_rows(mine.at[k], core.at[k], 0, 0, T)
            if n in (0, 1):
                one_copy(0, zb, yb).start()
            if n in (0, 2):
                one_copy(1, zb, xb).start()

    def stage1(zb):
        for far in (True, False):
            for h in (0, 1):
                j = (1 - y if far else y) if h == 0 else (1 - x if far else x)
                one_copy(h, zb, j).wait_recv()
                k = place_of(zb, j, x) if h == 0 else place_of(zb, y, j)
                add_rows(mine.at[k], one.at[h, zb * 2 + j], h * half, 0, half)
                if far:
                    two_copy(h, zb).start()

    def stage2(zb):
        k = place_of(zb, y, x)
        for h in (0, 1):
            two_copy(h, zb).wait_recv()
            add_rows(mine.at[k], two.at[h, zb], h * half, 0, half)
            def go(right, h=h):
                line_copy(h, zb, right).wait_recv()
                add_rows(mine.at[k], line.at[0 if right else 1, h, zb], h * half, 0, half)
            when(jnp.logical_and(zb > z, z >= 1), lambda: go(True))
            when(jnp.logical_and(zb < z, z + 1 < nz), lambda: go(False))
            when(zb > z, lambda: line_copy(h, zb, True).start())
            when(zb < z, lambda: line_copy(h, zb, False).start())

    for i in range(nz + 2):
        if i < nz:
            stage0(order[i])
        chunk(i)
        if 1 <= i < nz + 1:
            stage1(order[i - 1])
        if 2 <= i:
            stage2(order[i - 2])
    written(0)
    write(2)
    k = place_of(z, y, x)
    for h in (0, 1):
        lo = h * half
        o_ref[rows(h)] = mine[k, rows(h)].astype(jnp.float32)
        for d, ok in ((0, z >= 1), (1, z + 1 < nz)):
            def fin(d=d, h=h):
                line_copy(h, z, d == 0).wait_recv()
                o_ref[rows(h)] += line[d, h, z].astype(jnp.float32)
            when(ok, fin)
    written(1)
    written(2)
    for zb in order:
        for yb, xb in combos:
            core_copy(zb, yb, xb).wait_send()
        for h in (0, 1):
            for j in (0, 1):
                one_copy(h, zb, j).wait_send()
            two_copy(h, zb).wait_send()
            when(zb > z, lambda: line_copy(h, zb, True).wait_send())
            when(zb < z, lambda: line_copy(h, zb, False).wait_send())

def reduce_scatter(v, rows_in, rows_grad, hid, dg, du, nz, cid):
    n, tok, width = v.shape
    rows, wide = rows_in.shape
    f = hid.shape[1]
    parts = next(k for k in (4, 2, 1) if rows % (k * 16) == 0)
    b16, f32, sd = v.dtype, jnp.float32, jax.ShapeDtypeStruct
    buf = lambda *shape: pltpu.VMEM(shape, b16)
    grad = sd((f, wide), b16)
    return pl.pallas_call(
        functools.partial(scatter_kernel, nz),
        out_shape=[sd((tok, width), f32), grad, grad, grad],
        in_specs=[HBM] * 6,
        out_specs=[pl.BlockSpec(memory_space=pltpu.VMEM), HBM, HBM, HBM],
        scratch_shapes=[buf(n // 2, tok, width), buf(n // 2, tok, width), buf(2, 2 * nz, tok // 2, width),
                        buf(2, nz, tok // 2, width), buf(2, 2, nz, tok // 2, width)]
        + [pltpu.VMEM((f, wide), f32)] * 3
        + [buf(2, rows // parts, k) for k in (wide, wide, f, f, f)]
        + [SEM((n // 2,)), SEM((n // 2,)), SEM((n // 2,)), SEM((2, 2 * nz)), SEM((2, 2 * nz)), SEM((2, nz)), SEM((2, nz)),
           SEM((2, nz)), SEM((2, 2, nz)), SEM((2, 5)), SEM((3, 2))],
        cost_estimate=lasting(90),
        compiler_params=pltpu.CompilerParams(collective_id=cid, has_side_effects=True, vmem_limit_bytes=64 << 20),
    )(v, rows_in, rows_grad, hid, dg, du)


def lasting(us):
    return pl.CostEstimate(flops=0, bytes_accessed=int(us * 3.5e6), transcendentals=0)


def remote(src, dst, send_sem, recv_sem, dev):
    return pltpu.make_async_remote_copy(
        src_ref=src, dst_ref=dst, send_sem=send_sem, recv_sem=recv_sem, device_id=dev, device_id_type=MESH
    )


def quad_neighbours():
    z, y, c, x = place()
    return dict(x=(device(z, y, c, 1 - x), None), c=(device(z, y, 1 - c, x), None))


def open_kernel(nz, stream, wq, kv, lat, tiny, stream_all, wq_o, kv_o, lat_o, tiny_o, b0, b1, b2, b3, b4,
                load, store, send, recv, x_send, x_recv, zr_send, zl_send, y_send, p_recv):
    z, y, c, x = place()
    nbr = neighbours(nz)
    greet(nbr)
    quads = 2 * nz
    own, side, other = c * 2 + x, c * 2 + 1 - x, 1 - x
    rows = lat.shape[0] // 2
    xdev, cdev = nbr["x"][0], nbr["c"][0]

    def heads(ref, out, xx):
        n = out.shape[2]
        return ref.at[:, pl.ds(pl.multiple_of((xx * 2 + c) * n, 128), n)]

    def rows_of(a, j):
        n = (wq.shape[0] // quads, kv.shape[0] // quads, rows // quads)[a]
        return pl.ds(pl.multiple_of((c * rows if a == 2 else 0) + j * n, n), n)

    def piece(a, j):
        return (wq_o, kv_o, lat_o)[a].at[other, rows_of(a, j)]

    mine = z * 2 + y

    def first(a):
        r = rows_of(a, mine)
        if a == 2:
            src, dst = lat.at[r], lat_o.at[x, r]
        else:
            ref, out = ((wq, wq_o), (kv, kv_o))[a]
            n = out.shape[2]
            src, dst = ref.at[r, pl.ds(pl.multiple_of((other * 2 + c) * n, 128), n)], out.at[x, r]
        return remote(src, dst, x_send.at[a], x_recv.at[a], xdev)

    def along(a, j, kind):
        sems = dict(zr=zr_send, zl=zl_send, y=y_send)[kind]
        return remote(piece(a, j), piece(a, j), sems.at[a, j], p_recv.at[a, j], nbr[kind][0])

    kinds = (2, 1, 0)
    for a in kinds:
        first(a).start()
    xs = [
        remote(stream, stream_all.at[own], send.at[0], recv.at[0], xdev),
        remote(tiny, tiny_o.at[x], send.at[1], recv.at[1], xdev),
    ]
    for d in xs:
        d.start()
    cs = [remote(stream, stream_all.at[own], send.at[2], recv.at[2], cdev)]
    cs[0].start()
    here = [
        (stream, b0, stream_all.at[own]), (tiny, b4, tiny_o.at[x]), (lat, b3, lat_o.at[x]),
        (heads(kv, kv_o, x), b2, kv_o.at[x]), (heads(wq, wq_o, x), b1, wq_o.at[x]),
    ]
    for i, (a, b, o) in enumerate(here):
        pltpu.make_async_copy(a, b, load.at[i]).start()
    for i, (a, b, o) in enumerate(here):
        pltpu.make_async_copy(a, b, load.at[i]).wait()
        pltpu.make_async_copy(b, o, store.at[i]).start()

    def spread(go):
        def send(a, j, kind):
            d = along(a, j, kind)
            ok = nbr[kind][1]
            when(ok, (lambda: d.start()) if go else (lambda: d.wait_send()))

        for a in kinds:
            if go:
                first(a).wait_recv()
            for kind in ("zr", "zl", "y"):
                send(a, mine, kind)
        for s in range(nz - 1):
            for kind, zb, ok in (("zr", z - 1 - s, z - 1 - s >= 0), ("zl", z + 1 + s, z + 1 + s < nz)):

                def f(kind=kind, zb=zb):
                    j = zb * 2 + y
                    for a in kinds:
                        if go:
                            along(a, j, "y").wait_recv()
                        send(a, j, kind)
                        send(a, j, "y")

                pl.when(ok)(f)

    spread(True)
    xs[0].wait_recv()
    cs.append(remote(stream_all.at[side], stream_all.at[side], send.at[3], recv.at[3], cdev))
    cs[1].start()
    xs[1].wait_recv()
    for zb in range(nz):
        for a in kinds:
            along(a, zb * 2 + 1 - y, "y").wait_recv()
    half = pl.ds(pl.multiple_of(c * rows, rows), rows)
    cs.append(remote(lat_o.at[other, half], lat_o.at[other, half], send.at[4], recv.at[4], cdev))
    cs[2].start()
    for d in cs:
        d.wait_recv()
    for i, (a, b, o) in enumerate(here):
        pltpu.make_async_copy(b, o, store.at[i]).wait()
    for d in xs + cs:
        d.wait_send()
    for a in kinds:
        first(a).wait_send()
    spread(False)


def open_quad(stream, wq, kv, lat, tiny, nz, cid):
    sd = jax.ShapeDtypeStruct
    ins = (stream, wq, kv, lat, tiny)
    shapes = [(4,) + stream.shape, (2, wq.shape[0], wq.shape[1] // 4), (2, kv.shape[0], kv.shape[1] // 4), (2,) + lat.shape, (2,) + tiny.shape]
    pieces = SEM((3, 2 * nz))
    return pl.pallas_call(
        functools.partial(open_kernel, nz),
        out_shape=[sd(shape, v.dtype) for shape, v in zip(shapes, ins)],
        in_specs=[HBM] * 5,
        out_specs=[HBM] * 5,
        scratch_shapes=[pltpu.VMEM(shape[1:], v.dtype) for shape, v in zip(shapes, ins)]
        + [SEM((5,)), SEM((5,)), SEM((5,)), SEM((5,)), SEM((3,)), SEM((3,)), pieces, pieces, pieces, pieces],
        cost_estimate=lasting(50),
        compiler_params=pltpu.CompilerParams(collective_id=cid, has_side_effects=True, vmem_limit_bytes=16 << 20),
    )(*ins)


def split_kernel(units, gate, up, out):
    lanes = out.shape[2] // 2
    for j in range(out.shape[0]):
        lo = min(units * j // 128 * 128, gate.shape[1] - 2 * lanes)
        row = lax.broadcasted_iota(jnp.int32, (2 * lanes, lanes), 0)
        lane = lax.broadcasted_iota(jnp.int32, (2 * lanes, lanes), 1)
        pick = ((row == lane + (units * j - lo)) & (lane < units)).astype(jnp.float32).astype(gate.dtype)
        for k, ref in enumerate((gate, up)):
            out[j, :, k * lanes : (k + 1) * lanes] = wide_product(ref[:, lo : lo + 2 * lanes], pick).astype(out.dtype)


def split_units(gate, up, n_dev, units):
    vmem = pl.BlockSpec(memory_space=pltpu.VMEM)
    return pl.pallas_call(
        functools.partial(split_kernel, units),
        out_shape=jax.ShapeDtypeStruct((n_dev, gate.shape[0], 256), gate.dtype),
        in_specs=[vmem, vmem],
        out_specs=vmem,
        cost_estimate=lasting(4),
        compiler_params=pltpu.CompilerParams(vmem_limit_bytes=16 << 20),
    )(gate, up)


def join_kernel(units, blocks, gate, up):
    lanes = blocks.shape[2] // 2
    row = lax.broadcasted_iota(jnp.int32, (lanes, lanes), 0)
    lane = lax.broadcasted_iota(jnp.int32, (lanes, lanes), 1)
    for t in range(gate.shape[1] // lanes):
        totals = [None, None]
        for j in range(lanes * t // units, (lanes * t + lanes - 1) // units + 1):
            pick = ((row + (units * j - lanes * t) == lane) & (row < units)).astype(jnp.float32).astype(blocks.dtype)
            for k in (0, 1):
                v = wide_product(blocks[j, :, k * lanes : (k + 1) * lanes], pick)
                totals[k] = v if totals[k] is None else totals[k] + v
        for k, ref in enumerate((gate, up)):
            ref[:, t * lanes : (t + 1) * lanes] = totals[k]


def join_units(blocks, total, units):
    vmem = pl.BlockSpec(memory_space=pltpu.VMEM)
    out = jax.ShapeDtypeStruct((blocks.shape[1], total), jnp.float32)
    return pl.pallas_call(
        functools.partial(join_kernel, units),
        out_shape=[out, out],
        in_specs=[vmem],
        out_specs=[vmem, vmem],
        cost_estimate=lasting(4),
        compiler_params=pltpu.CompilerParams(vmem_limit_bytes=16 << 20),
    )(blocks)


def quad_gather_kernel(x_ref, o_ref, local, send, recv):
    z, y, c, x = place()
    nbr = quad_neighbours()
    greet(nbr)
    own, side = c * 2 + x, c * 2 + 1 - x
    half = x_ref.shape[0] // 2
    copies = []
    for h in (0, 1):
        r = pl.ds(h * half, half)
        a = remote(x_ref.at[r], o_ref.at[own, r], send.at[0, h], recv.at[0, h], nbr["x"][0])
        b = remote(x_ref.at[r], o_ref.at[own, r], send.at[1, h], recv.at[1, h], nbr["c"][0])
        d = remote(o_ref.at[side, r], o_ref.at[side, r], send.at[2, h], recv.at[2, h], nbr["c"][0])
        a.start()
        b.start()
        copies.append((a, b, d))
    here = pltpu.make_async_copy(x_ref, o_ref.at[own], local)
    here.start()
    for a, b, d in copies:
        a.wait_recv()
        d.start()
    for a, b, d in copies:
        b.wait_recv()
        d.wait_recv()
        a.wait_send()
        b.wait_send()
        d.wait_send()
    here.wait()


def quad_gather(v, cid):
    return pl.pallas_call(
        quad_gather_kernel,
        out_shape=jax.ShapeDtypeStruct((4,) + v.shape, v.dtype),
        in_specs=[HBM],
        out_specs=HBM,
        scratch_shapes=[SEM, SEM((3, 2)), SEM((3, 2))],
        cost_estimate=lasting(18),
        compiler_params=pltpu.CompilerParams(collective_id=cid, has_side_effects=True),
    )(v)


def quad_scatter_kernel(v_ref, o_ref, mine, core, far, load, send, recv):
    z, y, c, x = place()
    nbr = quad_neighbours()
    greet(nbr)
    half = o_ref.shape[0] // 2
    steps = []
    for h in (0, 1):
        r = pl.ds(h * half, half)
        for j, xb in ((0, 1 - x), (1, x)):
            a = remote(v_ref.at[(1 - c) * 2 + xb, r], core.at[j, r], send.at[j, h], recv.at[j, h], nbr["c"][0])
            b = pltpu.make_async_copy(v_ref.at[c * 2 + xb, r], mine.at[j, r], load.at[j, h])
            a.start()
            b.start()
            steps.append((a, b))
    outs = []
    for h in (0, 1):
        r = pl.ds(h * half, half)
        a, b = steps[2 * h]
        a.wait_recv()
        b.wait()
        add_rows(mine.at[0], core.at[0], h * half, h * half, half)
        f = remote(mine.at[0, r], far.at[r], send.at[2, h], recv.at[2, h], nbr["x"][0])
        f.start()
        outs.append(f)
    for h in (0, 1):
        a, b = steps[2 * h + 1]
        a.wait_recv()
        b.wait()
        outs[h].wait_recv()
        def body(i, carry, h=h):
            r = pl.ds(pl.multiple_of(h * half + i * 16, 16), 16)
            o_ref[r] = (mine[1, r].astype(jnp.float32) + core[1, r].astype(jnp.float32)) + far[r].astype(jnp.float32)
            return carry
        lax.fori_loop(0, half // 16, body, 0)
    for a, b in steps:
        a.wait_send()
    for f in outs:
        f.wait_send()


def quad_scatter(v, cid):
    _, rows, cols = v.shape
    buf = pltpu.VMEM((2, rows, cols), v.dtype)
    return pl.pallas_call(
        quad_scatter_kernel,
        out_shape=jax.ShapeDtypeStruct((rows, cols), jnp.float32),
        in_specs=[HBM],
        out_specs=pl.BlockSpec(memory_space=pltpu.VMEM),
        scratch_shapes=[buf, buf, pltpu.VMEM((rows, cols), v.dtype), SEM((2, 2)), SEM((3, 2)), SEM((3, 2))],
        cost_estimate=lasting(16),
        compiler_params=pltpu.CompilerParams(
            collective_id=cid, has_side_effects=True, vmem_limit_bytes=24 << 20
        ),
    )(v)


def finish_kernel(nz, na, there, own, far, stream, attn, mid, *refs):
    ins, refs = refs[:na], refs[na:]
    others, refs = dict(zip(there, refs)), refs[len(there) :]
    (res_o, q_o, kv_o, out_o, lat_o, router_o, side_o, stat_o), refs = refs[:8], refs[8:]
    (t_mine, t_core, t_one, t_two, t_line, ffn), refs = refs[:6], refs[6:]
    mine, refs = refs[:na], refs[na:]
    one, refs = refs[:na], refs[na:]
    line, refs = refs[:na], refs[na:]
    (q_all, kv_all, out_all, side_all, stat, stat_in), refs = refs[:6], refs[6:]
    (t_load, core_send, core_recv, tx_send, tx_recv, ty_send, ty_recv, tz_send, tz_recv,
     load, y_send, y_recv, z_send, z_recv, own_sem, q_send, q_recv, out_send, out_recv, st_send, st_recv) = refs
    z, y, c, x = place()
    nbr = neighbours(nz)
    nbr["d"] = (device(z, y, 1 - c, 1 - x), None)
    quads = 2 * nz
    linear = slot(z, y, c, x)
    target = (x * 2 + c) * quads + z * 2 + y
    group, q = linear // quads, lax.rem(linear, quads)
    source = device(q // 2, lax.rem(q, 2), lax.rem(group, 2), group // 2)
    away = target != linear
    nbr["to"] = ((target // 2, lax.rem(target, 2)), away)
    nbr["from"] = (source, away)
    here_q = z * 2 + y
    for j in range(1, quads):
        there = lax.rem(here_q + j, quads)
        nbr["q%d" % j] = (device(there // 2, lax.rem(there, 2), c, x), None)
    greet(nbr)
    order = far_first(nz, z)
    xdev, cdev, ddev, ydev = (nbr[k][0] for k in ("x", "c", "d", "y"))
    zdev = lambda right: nbr["zr" if right else "zl"][0]
    add = lambda total, other: add_rows(total, other, 0, 0, total.shape[0])
    place_of = lambda zb, yb, xb: (zb * 2 + yb) * 2 + xb
    combos = [(1 - y, 1 - x), (y, 1 - x), (1 - y, x), (y, x)]

    def t_core_copy(k):
        return remote(far.at[k], t_core.at[k], core_send.at[k], core_recv.at[k], cdev)

    def t_load_copy(k):
        return pltpu.make_async_copy(own.at[k], t_mine.at[k], t_load.at[k])

    def tx_copy(zb, yb):
        i = zb * 2 + yb
        return remote(t_mine.at[place_of(zb, yb, 1 - x)], t_one.at[i], tx_send.at[i], tx_recv.at[i], xdev)

    def ty_copy(zb):
        return remote(t_mine.at[place_of(zb, 1 - y, x)], t_two.at[zb], ty_send.at[zb], ty_recv.at[zb], ydev)

    def tz_copy(zb, right):
        d = 0 if right else 1
        return remote(t_mine.at[place_of(zb, y, x)], t_line.at[d, zb], tz_send.at[zb], tz_recv.at[d, zb], zdev(right))

    def t_stage0(zb):
        for i, (yb, xb) in enumerate(combos):
            k = place_of(zb, yb, xb)
            t_core_copy(k).wait_recv()
            t_load_copy(k).wait()
            add(t_mine.at[k], t_core.at[k])
            if i < 2:
                tx_copy(zb, yb).start()

    def t_stage1(zb):
        for yb in (1 - y, y):
            tx_copy(zb, yb).wait_recv()
            add(t_mine.at[place_of(zb, yb, x)], t_one.at[zb * 2 + yb])
            if yb is not y:
                ty_copy(zb).start()

    def on_line(zb, arrive, leave):
        when(jnp.logical_and(zb > z, z >= 1), lambda: arrive(True))
        when(jnp.logical_and(zb < z, z + 1 < nz), lambda: arrive(False))
        when(zb > z, lambda: leave(True))
        when(zb < z, lambda: leave(False))

    def t_stage2(zb):
        total = t_mine.at[place_of(zb, y, x)]
        ty_copy(zb).wait_recv()
        add(total, t_two.at[zb])

        def arrive(right):
            tz_copy(zb, right).wait_recv()
            add(total, t_line.at[0 if right else 1, zb])

        on_line(zb, arrive, lambda right: tz_copy(zb, right).start())

    apart = [a for a in range(na) if a not in others]

    def w_load(a, k):
        src = ins[a].at[k, c * 2 + x] if len(ins[a].shape) == 4 else ins[a].at[k]
        return pltpu.make_async_copy(src, mine[a].at[k], load.at[a, k])

    def wy_copy(a, zb):
        if a in others:
            return pltpu.make_async_copy(others[a].at[zb], one[a].at[zb], y_recv.at[a, zb])
        return remote(mine[a].at[zb * 2 + 1 - y], one[a].at[zb], y_send.at[a, zb], y_recv.at[a, zb], ydev)

    def wz_copy(a, zb, right):
        d = 0 if right else 1
        return remote(mine[a].at[zb * 2 + y], line[a].at[d, zb], z_send.at[a, zb], z_recv.at[d, a, zb], zdev(right))

    def w_stage0(zb):
        for a in apart:
            w_load(a, zb * 2 + 1 - y).wait()
            wy_copy(a, zb).start()

    def w_stage1(zb):
        for a in range(na):
            total = mine[a].at[zb * 2 + y]
            w_load(a, zb * 2 + y).wait()
            d = wy_copy(a, zb)
            d.wait() if a in others else d.wait_recv()
            add(total, one[a].at[zb])

            def arrive(right):
                wz_copy(a, zb, right).wait_recv()
                add(total, line[a].at[0 if right else 1, zb])

            on_line(zb, arrive, lambda right: wz_copy(a, zb, right).start())

    for zb in order:
        for yb, xb in combos:
            k = place_of(zb, yb, xb)
            t_core_copy(k).start()
            t_load_copy(k).start()
        for a in apart:
            w_load(a, zb * 2 + 1 - y).start()
        for a in range(na):
            w_load(a, zb * 2 + y).start()
        for a in others:
            wy_copy(a, zb).start()
    for i in range(nz):
        if i < 2:
            w_stage0(order[i])
        t_stage0(order[i])
    for i in range(nz):
        t_stage1(order[i])
        if i + 2 < nz:
            w_stage0(order[i + 2])
        w_stage1(order[i])
        t_stage2(order[i])

    here = t_mine.at[place_of(z, y, x)]
    for right, ok in ((True, z >= 1), (False, z + 1 < nz)):

        def last(right=right):
            tz_copy(z, right).wait_recv()

        when(ok, last)
    rows = 16

    def body(i, sums):
        r = pl.ds(pl.multiple_of(i * rows, rows), rows)
        left = jnp.where(z >= 1, t_line[0, z, r].astype(jnp.float32), 0.0)
        right = jnp.where(z + 1 < nz, t_line[1, z, r].astype(jnp.float32), 0.0)
        v = here[r].astype(jnp.float32) + left + right
        total = mid[r] + v
        res_o[r] = total.astype(res_o.dtype)
        fold = lambda u: jnp.sum((u * u).reshape(rows, -1, 128), axis=(0, 1))[None]
        terms = (stream[r].astype(jnp.float32), attn[r], mid[r], v, total)
        return tuple(s + fold(u) for s, u in zip(sums, terms))

    sums = lax.fori_loop(0, mid.shape[0] // rows, body, (jnp.zeros((1, 128), jnp.float32),) * 5)
    stat[...] = jnp.concatenate(sums + (jnp.zeros((3, 128), jnp.float32),), axis=0)
    near, wide = ["x", "c", "d"], ["q%d" % j for j in range(1, quads)]

    def stat_copy(keys, key):
        i = 3 * (keys is wide) + keys.index(key)
        return remote(stat, stat_in.at[i], st_send.at[i], st_recv.at[i], nbr[key][0])

    def stat_start(keys):
        for key in keys:
            stat_copy(keys, key).start()

    def stat_end(keys):
        for key in keys:
            stat_copy(keys, key).wait()
        total = stat[...]
        for i in range(len(keys)):
            total = total + stat_in[3 * (keys is wide) + i]
        stat[...] = total

    stat_start(near)

    k = z * 2 + y
    member, group = c * 2 + x, x * 2 + c
    waits = []
    spread = {0: q_all, 1: kv_all, na - 1: side_all}
    for n_done, a in enumerate((2, 0, 1, 3, 4, na - 1)):
        total = mine[a].at[k]

        def fin(right):
            wz_copy(a, z, right).wait_recv()
            add(total, line[a].at[0 if right else 1, z])

        when(z >= 1, lambda: fin(True))
        when(z + 1 < nz, lambda: fin(False))
        if a in spread:
            dst = spread[a]
            part = dst.shape[1]
            piece = lambda m: total if a == na - 1 else total.at[pl.ds(pl.multiple_of(m * part, part), part)]
            d = pltpu.make_async_copy(piece(member), dst.at[group], own_sem.at[a])
            d.start()
            waits.append(d)
            for i, (dev, cc, xx) in enumerate(((xdev, c, 1 - x), (cdev, 1 - c, x), (ddev, 1 - c, 1 - x))):
                d = remote(piece(cc * 2 + xx), dst.at[group], q_send.at[a, i], q_recv.at[a, i], dev)
                d.start()
                waits.append(d)
        elif a == 2:
            to = remote(total, out_all, out_send, out_recv, nbr["to"][0])
            stay = pltpu.make_async_copy(total, out_all, own_sem.at[a])
            when(away, lambda: to.start())
            when(jnp.logical_not(away), lambda: stay.start())

        if n_done == 1:
            stat_end(near)
            stat_start(wide)
    stat_end(wide)
    stat_o[...] = stat[...]
    router_o[...] = mine[4][k].astype(jnp.float32)
    lat_o[...] = mine[3][k].astype(jnp.float32)
    when(away, lambda: to.wait())
    when(jnp.logical_not(away), lambda: stay.wait())
    out_o[...] = out_all[...].astype(jnp.float32)
    for d in waits:
        d.wait()
    for g in range(4):
        for dst, src in ((q_o, q_all), (kv_o, kv_all)):
            n = src.shape[2]
            dst[:, g * n : (g + 1) * n] = src[g].astype(jnp.float32)
    side_o[...] = side_all[0] + side_all[1] + side_all[2] + side_all[3]

    for zb in order:
        for yb, xb in combos:
            t_core_copy(place_of(zb, yb, xb)).wait_send()
        for yb in (1 - y, y):
            tx_copy(zb, yb).wait_send()
        ty_copy(zb).wait_send()
        on_line(zb, lambda right: None, lambda right: tz_copy(zb, right).wait_send())
        for a in range(na):
            if a in apart:
                wy_copy(a, zb).wait_send()
            on_line(zb, lambda right: None, lambda right: wz_copy(a, zb, right).wait_send())


def finish(own, far, stream, attn, mid, arrays, swapped, nz, cid):
    na = len(arrays)
    tok, width = mid.shape
    n, quads = 4 * nz, 2 * nz
    f32, b16, sd = jnp.float32, own.dtype, jax.ShapeDtypeStruct
    q, kv, out, lat, router, side = arrays
    vmem = pl.BlockSpec(memory_space=pltpu.VMEM)
    shapes = [
        sd((tok, width), b16), sd((q.shape[1] // 4, 4 * q.shape[2]), f32), sd((kv.shape[1] // 4, 4 * kv.shape[2]), f32),
        sd(out.shape[1:], f32), sd(lat.shape[2:], f32), sd(router.shape[2:], f32), sd(side.shape[1:], f32), sd((8, 128), f32),
    ]
    buf = lambda *shape: pltpu.VMEM(shape, b16)
    return pl.pallas_call(
        functools.partial(finish_kernel, nz, na, tuple(swapped)),
        out_shape=shapes,
        in_specs=[HBM, HBM, vmem, vmem, vmem] + [HBM] * (na + len(swapped)),
        out_specs=[vmem] * 8,
        scratch_shapes=[buf(n, tok, width), buf(n, tok, width), buf(quads, tok, width), buf(nz, tok, width),
                        buf(2, nz, tok, width), pltpu.VMEM((8, 128), f32)]
        + [pltpu.VMEM((quads,) + v.shape[-2:], v.dtype) for v in arrays]
        + [pltpu.VMEM((nz,) + v.shape[-2:], v.dtype) for v in arrays]
        + [pltpu.VMEM((2, nz) + v.shape[-2:], v.dtype) for v in arrays]
        + [buf(4, q.shape[1] // 4, q.shape[2]), buf(4, kv.shape[1] // 4, kv.shape[2]), buf(*out.shape[1:]),
           pltpu.VMEM((4,) + side.shape[1:], f32), pltpu.VMEM((8, 128), f32), pltpu.VMEM((quads + 2, 8, 128), f32)]
        + [SEM((n,)), SEM((n,)), SEM((n,)), SEM((quads,)), SEM((quads,)), SEM((nz,)), SEM((nz,)), SEM((nz,)), SEM((2, nz)),
           SEM((na, quads)), SEM((na, nz)), SEM((na, nz)), SEM((na, nz)), SEM((2, na, nz)), SEM((na,)), SEM((na, 3)),
           SEM((na, 3)), SEM, SEM, SEM((quads + 2,)), SEM((quads + 2,))],
        cost_estimate=lasting(130),
        compiler_params=pltpu.CompilerParams(collective_id=cid, has_side_effects=True, vmem_limit_bytes=58 << 20),
    )(own, far, stream, attn, mid, *arrays, *swapped.values())


def silu_parts(values):
    sigmoid = jax.nn.sigmoid(values)
    return values * sigmoid, sigmoid * (1.0 + values * (1.0 - sigmoid))


def experts_kernel(nt_ref, sg_ref, tail_ref, wg_ref, wu_ref, wd_ref, ws_ref, wsd_ref,
                   own_ref, far_ref, ng_ref, x_ref, g_ref, hid_ref, dg_ref, du_ref, dws_out, dsd_ref,
                   dws_ref, *, slots):
    f32, b16 = jnp.float32, jnp.bfloat16
    i = pl.program_id(0)
    @pl.when(i == 0)
    def _():
        for r in (dws_ref, dsd_ref):
            r[...] = jnp.zeros_like(r)
    tokens = nt_ref.shape[0] * nt_ref.shape[1]
    width = nt_ref.shape[2]
    nt = nt_ref[...].reshape(tokens, width)
    sg = sg_ref[...].reshape(tokens, width)
    blocks, tok = nt_ref.shape[:2]
    lines = tail_ref.shape[1] // 2
    me = lax.axis_index("rep")
    gate_row = tail_ref[:, pl.ds(me, 1), :].reshape(blocks, tok)
    named = tail_ref[:, pl.ds(lines + me, 1), :].reshape(blocks, tok)
    before = lax.broadcasted_iota(jnp.int32, (tok, tok), 0) < lax.broadcasted_iota(jnp.int32, (tok, tok), 1)
    rank = wide_product(named.astype(b16), before.astype(f32).astype(b16)).astype(jnp.int32)
    rank = rank + lax.broadcasted_iota(jnp.int32, (blocks, tok), 0) * (slots // blocks)
    place_of = jnp.where(named > 0, rank, -1)
    in_row = lambda v: jnp.concatenate([v[j : j + 1] for j in range(blocks)], axis=1)
    hit = lax.broadcasted_iota(jnp.int32, (slots, tokens), 0) == in_row(place_of)
    pick = hit.astype(f32).astype(b16)
    x = wide_product(pick, nt).astype(b16)
    x_ref[...] = x
    g0 = wide_product(pick, sg)
    gate = jnp.sum(jnp.where(hit, in_row(gate_row), 0.0), axis=1, keepdims=True)
    g = (gate * g0).astype(b16)
    g_ref[...] = g
    gv = dot_nt(x, wg_ref[...])
    uv = dot_nt(x, wu_ref[...])
    act, slope = silu_parts(gv)
    hid = (act * uv).astype(b16)
    part = wide_product(hid, wd_ref[...])
    gg = jnp.sum(g0 * part, axis=1, keepdims=True)
    gg_high = gg.astype(b16).astype(f32)
    column = lax.axis_index("rep") * 4 + lax.axis_index("shard") * 2
    lane = lax.broadcasted_iota(jnp.int32, (slots, 128), 1)
    gg = jnp.where(lane == column, gg_high, jnp.where(lane == column + 1, gg - gg_high, 0.0)).astype(b16)
    e_out = (gate * part).astype(b16)
    hid_ref[...] = hid
    hg = dot_nt(g, wd_ref[...])
    dg = (hg * uv * slope).astype(b16)
    du = (hg * act).astype(b16)
    dg_ref[...] = dg
    du_ref[...] = du
    ing = (wide_product(dg, wg_ref[...]) + wide_product(du, wu_ref[...])).astype(b16)
    fs = wsd_ref.shape[0]
    s = wide_product(nt, ws_ref[...])
    sgv, suv = s[:, :fs], s[:, fs:]
    sact, sslope = silu_parts(sgv)
    sh = (sact * suv).astype(b16)
    shg = dot_nt(sg, wsd_ref[...])
    ds = jnp.concatenate([shg * suv * sslope, shg * sact], axis=1).astype(b16)
    dsd_ref[...] += dot_tn(sh, sg)
    dws_ref[...] += dot_tn(ds, nt)
    out = wide_product(sh, wsd_ref[...]) + dot_tn(pick, e_out)
    out = out.astype(b16).reshape(nt_ref.shape)
    c = lax.rem(lax.axis_index("rep"), 2)
    for j in (0, 1):

        @pl.when(c == j)
        def _(j=j):
            own_ref[...] = out[2 * j : 2 * j + 2]
            far_ref[...] = out[2 - 2 * j : 4 - 2 * j]

    ng = dot_nt(ds, ws_ref[...]) + dot_tn(pick, ing)
    ng_ref[:, :, :width] = ng.astype(b16).reshape(nt_ref.shape)
    ng_ref[:, :, width:] = dot_tn(pick, gg).astype(b16).reshape(ng_ref.shape[:2] + (128,))
    @pl.when(i == pl.num_programs(0) - 1)
    def _():
        dws_out[...] = dws_ref[...].T.astype(b16)

def experts_both(nt, sg, tails, wg, wu, wd, ws, wsd, capacity, blocks=4):
    n, tok, width = nt.shape
    steps = n // blocks
    f = wg.shape[0]; fs = wsd.shape[0]
    f32 = jnp.float32
    one = lambda a: pl.BlockSpec(a.shape, lambda i: (0,) * a.ndim, pipeline_mode=pl.Buffered(1))
    blk = pl.BlockSpec((blocks, tok, width), lambda i: (i, 0, 0))
    half = pl.BlockSpec((blocks // 2, tok, width), lambda i: (i, 0, 0))
    row = pl.BlockSpec((blocks,) + tails.shape[1:], lambda i: (i, 0, 0))
    sd = jax.ShapeDtypeStruct
    kept = lambda k: pl.BlockSpec((blocks * capacity, k), lambda i: (i, 0))
    return pl.pallas_call(
        functools.partial(experts_kernel, slots=blocks * capacity),
        grid=(steps,),
        in_specs=[blk, blk, row] + [one(w) for w in (wg, wu, wd, ws, wsd)],
        out_specs=[half, half, pl.BlockSpec((blocks, tok, width + 128), lambda i: (i, 0, 0)), kept(width), kept(width)]
        + [kept(f)] * 3
        + [pl.BlockSpec((width, 2 * fs), lambda i: (0, 0)), pl.BlockSpec((fs, width), lambda i: (0, 0))],
        out_shape=[sd((n // 2, tok, width), nt.dtype)] * 2
        + [sd((n, tok, width + 128), nt.dtype)]
        + [sd((n * capacity, k), nt.dtype) for k in (width, width, f, f, f)]
        + [sd((width, 2 * fs), nt.dtype), sd((fs, width), f32)],
        scratch_shapes=[pltpu.VMEM((2 * fs, width), f32)],
        compiler_params=pltpu.CompilerParams(vmem_limit_bytes=62 << 20, dimension_semantics=("arbitrary",)),
        cost_estimate=lasting(110),
    )(nt, sg, tails, wg, wu, wd, ws, wsd)


def swap(v, nz, f):
    pairs = [
        (slot(*f(z, y, c, x)), slot(z, y, c, x))
        for z in range(nz) for y in range(2) for c in range(2) for x in range(2)
    ]
    return lax.ppermute(v, ("rep", "shard"), pairs)


def on_device(
    stream_in, stream_grad, prefix_len, routes, route_weight, attn_gain, query_proj, latent_proj, rope_key_proj,
    latent_gain, kv_up_proj, out_proj, ffn_gain, router_proj, shared_gate, shared_up, shared_down, expert_gate,
    expert_up, expert_down,
):
    f32, b16 = jnp.float32, jnp.bfloat16
    both = ("rep", "shard")
    n_shard, n_rep = lax.axis_size("shard"), lax.axis_size("rep")
    n_dev = n_rep * n_shard
    nz = n_rep // 4
    quads = n_rep // 2
    rep, x = lax.axis_index("rep"), lax.axis_index("shard")
    c = lax.rem(rep, 2)
    member, group = c * 2 + x, x * 2 + c
    tok, width = stream_in.shape
    experts = router_proj.shape[1]
    capacity = max(2, tok * TOP_K * 7 // (6 * experts))
    seq = n_shard * tok
    scale = (DN + DR) ** (-0.5)
    heads = H // 4
    qcols, kcols = heads * (DN + DR), heads * (DN + DV)
    kvr = latent_proj.shape[1]
    lanes = kvr + DR

    dh = width // n_shard
    gl = jnp.pad(latent_gain, (0, dh - kvr // n_shard))
    tiny = jnp.concatenate([rope_key_proj.T, router_proj.T, attn_gain[None], ffn_gain[None], gl[None]], axis=0)
    tiny = jnp.pad(tiny, ((0, -tiny.shape[0] % 16), (0, 0)))
    stream_all, mat_q, mat_kv, mat_lat, tiny = open_quad(stream_in, query_proj, kv_up_proj, latent_proj, tiny, nz, 1)
    mat_q = mat_q.reshape(width, qcols)
    mat_kv = mat_kv.reshape(kvr, kcols)
    mat_lat = mat_lat.reshape(width, kvr)
    joined = jnp.concatenate([tiny[0], tiny[1]], axis=1)
    rope_t, router_t = joined[:DR], joined[DR : DR + experts]
    gain_attn = joined[DR + experts].astype(f32)
    gain_ffn = joined[DR + experts + 1].astype(f32)
    gain_latent = tiny[:, DR + experts + 2, : kvr // n_shard].reshape(kvr).astype(f32)
    mat_out = lax.dynamic_slice_in_dim(out_proj, c * heads * DV, heads * DV, 0)

    late_grad, stream_all = lax.optimization_barrier((stream_grad, stream_all))
    grad_all = lax.all_gather(late_grad, both, axis=0)
    one_hot = (routes[:, :, None] == jnp.arange(experts)[None, None, :]).astype(f32)
    mask = jnp.sum(one_hot, axis=1)
    weight = jnp.sum(one_hot * route_weight[:, :, None], axis=1)
    fs = shared_down.shape[0]
    lanes_s = -(-fs // 128) * 128
    own_w = width // n_dev
    split = split_units(shared_gate, shared_up, n_dev, fs)
    w_s = lax.all_to_all(split, both, split_axis=0, concat_axis=0, tiled=True).reshape(width, 2 * lanes_s)
    w_sd = jnp.pad(shared_down, ((0, lanes_s - fs), (0, 0)))

    stream4 = stream_all.reshape(4 * tok, width).astype(f32)
    normed = (stream4 * rms_scale(stream4) * gain_attn).astype(b16)
    positions = jnp.arange(seq)
    cosine, sine = rope_tables(positions, DR)
    q_raw = wide_product(normed, mat_q).reshape(2, seq, heads, DN + DR)
    q_nope = q_raw[..., :DN].astype(b16)
    q_rot = rotate(q_raw[..., DN:], cosine[:, None], sine[:, None]).astype(b16)
    latent = wide_product(normed, mat_lat)
    scale_lat = rms_scale(latent)
    latent_normed = (latent * scale_lat * gain_latent).astype(b16)
    k_rot = rotate(dot_nt(normed, rope_t).reshape(2, seq, DR), cosine, sine).astype(b16)
    keyval = wide_product(latent_normed, mat_kv).astype(b16).reshape(2, seq, heads, DN + DV)
    k_nope, values = keyval[..., :DN], keyval[..., DN:]
    prefix = lax.dynamic_slice_in_dim(prefix_len, rep - c, 2)
    allowed = (positions[None, None, :] <= positions[None, :, None]) | (positions[None, None, :] < prefix[:, None, None])
    allowed = allowed[:, None]
    raw = contract(q_nope, k_nope, ((3,), (3,)), ((0, 2), (0, 2)))
    raw = raw + jnp.swapaxes(contract(q_rot, k_rot, ((3,), (2,)), ((0,), (0,))), 1, 2)
    scores = jnp.where(allowed, raw * scale, MASKED)
    expo = jnp.exp(scores - jnp.max(scores, axis=-1, keepdims=True))
    probs = expo / jnp.sum(expo, axis=-1, keepdims=True)
    probs_low = probs.astype(b16)
    attended = jnp.swapaxes(contract(probs_low, values, ((3,), (1,)), ((0, 1), (0, 2))), 1, 2)
    attended = attended.astype(b16).reshape(4 * tok, heads * DV)
    part = wide_product(attended, mat_out).astype(b16).reshape(4, tok, width)
    attn_out = quad_scatter(part, 3)
    stream = stream_in.astype(f32)
    mid = stream + attn_out
    scale_two = rms_scale(mid)
    normed_two = (mid * scale_two * gain_ffn).astype(b16)

    router_prob = jax.nn.softmax(dot_nt(normed_two, router_t), axis=-1)
    picked = mask * router_prob
    picked_sum = jnp.sum(picked, axis=-1, keepdims=True)
    gates = weight * picked / picked_sum
    nt_all, tails = all_gather(normed_two, jnp.concatenate([gates.T, mask.T], axis=0), n_dev, nz, 4)

    mats = (jnp.swapaxes(expert_gate, 1, 2)[0], jnp.swapaxes(expert_up, 1, 2)[0], expert_down[0], w_s, w_sd)
    out_own, out_far, n_grad, *kept, grad_s, grad_sd = experts_both(
        nt_all, grad_all, tails, *mats, capacity, 4)
    n_grad, grad_eg, grad_eu, grad_ed = reduce_scatter(n_grad, *kept, nz, 16)
    back = lax.all_to_all(grad_s.reshape(n_dev, own_w, 2 * lanes_s), both, split_axis=0, concat_axis=0, tiled=True)
    back = join_units(back, n_dev * fs, fs)
    gate_grad = jnp.sum(n_grad[:, width : width + 4 * experts].reshape(tok, experts, 4), axis=-1)
    n_grad = n_grad[:, :width]

    weighted = weight * gate_grad
    picked_grad = weighted / picked_sum - jnp.sum(weighted * picked, axis=-1, keepdims=True) / (picked_sum * picked_sum)
    prob_grad = mask * picked_grad
    logit_grad = (router_prob * (prob_grad - jnp.sum(router_prob * prob_grad, axis=-1, keepdims=True))).astype(b16)
    n_grad = n_grad + wide_product(logit_grad, router_t)
    norm_part, ffn_gain_grad = norm_back(n_grad, mid, scale_two, gain_ffn)
    mid_grad = stream_grad.astype(f32) + norm_part
    aog = mid_grad.astype(b16)
    tail = jnp.pad(logit_grad, ((0, 0), (0, 128 - experts)))
    aog_all = quad_gather(jnp.concatenate([aog, tail], axis=1), 7).reshape(4 * tok, width + 128)
    logit_all = aog_all[:, width:]
    aog_all = aog_all[:, :width]

    att_grad = dot_nt(aog_all, mat_out).astype(b16)
    grad_out = dot_tn(attended, aog_all)
    grad_out = grad_out.astype(b16).reshape(quads, -1, width)
    y_of = lax.rem(rep // 2, 2)

    def over_y(v):
        far = lax.dynamic_index_in_dim(v.reshape((nz, 2) + v.shape[1:]), 1 - y_of, 1, False)
        return swap(far, nz, lambda z, y, c, x: (z, 1 - y, c, x))

    out_y = over_y(grad_out)
    att_grad = att_grad.reshape(2, seq, heads, DV)
    value_grad = jnp.swapaxes(contract(probs_low, att_grad, ((2,), (1,)), ((0, 1), (0, 2))), 1, 2)
    prob_grad_a = contract(att_grad, values, ((3,), (3,)), ((0, 2), (0, 2)))
    s_grad = probs * (prob_grad_a - jnp.sum(probs * prob_grad_a, axis=-1, keepdims=True))
    s_grad = s_grad.astype(b16)
    qn_grad = scale * jnp.swapaxes(contract(s_grad, k_nope, ((3,), (1,)), ((0, 1), (0, 2))), 1, 2)
    qr_grad = scale * jnp.swapaxes(contract(s_grad, k_rot, ((3,), (1,)), ((0,), (0,))), 1, 2)
    kn_grad = scale * jnp.swapaxes(contract(s_grad, q_nope, ((2,), (1,)), ((0, 1), (0, 2))), 1, 2)
    kr_grad = scale * contract(s_grad, q_rot, ((1, 2), (2, 1)), ((0,), (0,)))
    keyval_grad = jnp.concatenate([kn_grad, value_grad], axis=-1).astype(b16).reshape(4 * tok, kcols)
    qr_grad = rotate(qr_grad, cosine[:, None], -sine[:, None])
    query_grad = jnp.concatenate([qn_grad, qr_grad], axis=-1).astype(b16).reshape(4 * tok, qcols)
    lat_part = dot_nt(keyval_grad, mat_kv)
    lat_part = jnp.concatenate([lat_part, kr_grad.reshape(4 * tok, DR)], axis=1).astype(b16)
    lat_part = lat_part.astype(f32) + swap(lat_part, nz, lambda z, y, c, x: (z, y, c, 1 - x)).astype(f32)
    lat_part = lat_part.astype(b16)
    lat_sum = lat_part.astype(f32) + swap(lat_part, nz, lambda z, y, c, x: (z, y, 1 - c, x)).astype(f32)
    lat_sum, kr_sum = lat_sum[:, :kvr], lat_sum[:, kvr:lanes].reshape(2, seq, DR)
    key_pre = rotate(kr_sum, cosine, -sine).reshape(4 * tok, DR).astype(b16)
    weighted_l = lat_sum * gain_latent
    inner = jnp.mean(weighted_l * latent, axis=-1, keepdims=True)
    latent_pre = scale_lat * weighted_l - latent * (scale_lat * scale_lat * scale_lat) * inner
    lat_gain_rows = lat_sum * latent * scale_lat
    lat_gain_grad = jnp.sum(lax.dynamic_slice_in_dim(lat_gain_rows, member * tok, tok, 0), axis=0)
    lat_grad = jnp.concatenate([latent_pre.astype(b16), key_pre], axis=1)
    part = dot_nt(query_grad, mat_q)
    normed_grad = quad_scatter(part.astype(b16).reshape(4, tok, width), 9)
    lat_own = lax.dynamic_slice_in_dim(lat_grad, member * tok, tok, 0)
    normed_grad = normed_grad + dot_nt(lat_own[:, :kvr], mat_lat) + wide_product(lat_own[:, kvr:], rope_t)
    attn_part, attn_gain_grad = norm_back(normed_grad, stream, rms_scale(stream), gain_attn)
    grad_stream = (mid_grad + attn_part).astype(b16)

    gq = dot_tn(normed, query_grad).astype(b16)
    gkv = dot_tn(latent_normed, keyval_grad).astype(b16).reshape(quads, -1, kcols)
    kv_y = over_y(gkv)
    nt_quad = lax.dynamic_slice_in_dim(nt_all, (rep // 2) * 4, 4, 0).reshape(4 * tok, width)
    lat_grad = jnp.pad(lat_grad, ((0, 0), (0, -lanes % 128)))
    glat = dot_tn(normed, lat_grad).astype(b16).reshape(quads, 4, own_w, -1)
    grouter = dot_tn(nt_quad, logit_all).astype(b16).reshape(quads, 4, own_w, -1)
    side = jnp.concatenate([v.reshape(quads, -1) for v in (attn_gain_grad, ffn_gain_grad, lat_gain_grad)], axis=1)
    side = jnp.pad(side, ((0, 0), (0, 1024 - side.shape[1]))).reshape(quads, 8, 128)
    stream_out, o_q, o_kv, o_out, o_lat, o_router, o_side, o_stat = finish(
        out_own, out_far, stream_in, attn_out, mid,
        [gq.reshape(quads, -1, qcols), gkv, grad_out, glat, grouter, side], {1: kv_y, 2: out_y}, nz, 10)
    o_side = o_side.reshape(-1)
    per = width // quads
    perl = kvr // quads
    ga = lax.dynamic_slice_in_dim(o_side, member * own_w, own_w)
    gf = lax.dynamic_slice_in_dim(o_side, per + member * own_w, own_w)
    gla = lax.dynamic_slice_in_dim(o_side, 2 * per + member * (perl // 4), perl // 4)
    stats = jnp.sqrt(jnp.sum(o_stat[:5], axis=1) / (tok * n_dev * width))
    return (
        stream_out, grad_stream, stats, ga, o_q, o_lat[:, :kvr], o_lat[:, kvr:lanes], gla, o_kv, o_out, gf,
        o_router[:, :experts], back[0], back[1], grad_sd[:fs], jnp.swapaxes(grad_eg.astype(f32)[None], 1, 2), jnp.swapaxes(grad_eu.astype(f32)[None], 1, 2), grad_ed.astype(f32)[None],
    )


def on_device_weights(
    stream_in,
    stream_grad,
    prefix_len,
    routes,
    route_weight,
    attn_gain,
    query_proj,
    latent_proj,
    rope_key_proj,
    latent_gain,
    kv_up_proj,
    out_proj,
    ffn_gain,
    router_proj,
    shared_gate,
    shared_up,
    shared_down,
    expert_gate,
    expert_up,
    expert_down,
):
    n_shard = lax.axis_size("shard")
    n_rep = lax.axis_size("rep")
    rep_index = lax.axis_index("rep")
    shard_index = lax.axis_index("shard")
    tok_rows = stream_in.shape[0]
    seq_len = n_shard * tok_rows
    experts = router_proj.shape[1]
    capacity = max(2, tok_rows * TOP_K * 7 // (6 * experts))
    head_width = H * (DN + DV)
    kv_rows = tok_rows * head_width // 128
    rope_rows = tok_rows * DR // 128
    piece_rows = kv_rows + rope_rows
    score_scale = (DN + DR) ** (-0.5)
    weights = (
        attn_gain,
        query_proj,
        latent_proj,
        rope_key_proj,
        latent_gain,
        kv_up_proj,
        out_proj,
        ffn_gain,
        router_proj,
    )
    shared_mats = (shared_gate, shared_up, shared_down)
    (
        gain_attn,
        mat_query,
        mat_latent,
        mat_rope,
        gain_latent,
        mat_kv,
        mat_out,
        gain_ffn,
        mat_router,
    ) = (
        lax.all_gather(weights[0], "shard", axis=0, tiled=True),
        lax.all_gather(weights[1], "shard", axis=0, tiled=True),
        lax.all_gather(weights[2], "shard", axis=0, tiled=True),
        lax.all_gather(weights[3], "shard", axis=0, tiled=True),
        lax.all_gather(weights[4], "shard", axis=0, tiled=True),
        lax.all_gather(weights[5], "shard", axis=0, tiled=True),
        lax.all_gather(weights[6], "shard", axis=0, tiled=True),
        lax.all_gather(weights[7], "shard", axis=0, tiled=True),
        lax.all_gather(weights[8], "shard", axis=0, tiled=True),
    )
    mat_sgate, mat_sup, mat_sdown = (
        lax.all_gather(shared_mats[0], ("rep", "shard"), axis=0, tiled=True),
        lax.all_gather(shared_mats[1], ("rep", "shard"), axis=0, tiled=True),
        lax.all_gather(shared_mats[2], ("rep", "shard"), axis=0, tiled=True),
    )
    gain_attn = gain_attn.astype(jnp.float32)
    gain_latent = gain_latent.astype(jnp.float32)
    gain_ffn = gain_ffn.astype(jnp.float32)
    stream = stream_in.astype(jnp.float32)
    scale_one = rms_scale(stream)
    normed = (stream * scale_one * gain_attn).astype(jnp.bfloat16)
    positions = shard_index * tok_rows + jnp.arange(tok_rows)
    cosine, sine_vals = rope_tables(positions, DR)
    query_raw = wide_product(normed, mat_query).reshape(tok_rows, H, DN + DR)
    query_nope = query_raw[:, :, :DN].astype(jnp.bfloat16)
    query_rot = rotate(query_raw[:, :, DN:], cosine[:, None], sine_vals[:, None]).astype(
        jnp.bfloat16
    )
    latent = wide_product(normed, mat_latent)
    scale_lat = rms_scale(latent)
    latent_normed = (latent * scale_lat * gain_latent).astype(jnp.bfloat16)
    keyval_own = wide_product(latent_normed, mat_kv).astype(jnp.bfloat16)
    key_rot_own = rotate(wide_product(normed, mat_rope), cosine, sine_vals).astype(jnp.bfloat16)
    packed = jnp.concatenate(
        [keyval_own.reshape(kv_rows, 128), key_rot_own.reshape(rope_rows, 128)], axis=0
    )
    seq_keys = lax.all_gather(packed, "shard", axis=0, tiled=True).reshape(n_shard, piece_rows, 128)
    keyval = seq_keys[:, :kv_rows].reshape(seq_len, H, DN + DV)
    key_rot = seq_keys[:, kv_rows:].reshape(seq_len, DR)
    key_nope = keyval[:, :, :DN]
    values = keyval[:, :, DN:]
    prefix = lax.dynamic_index_in_dim(prefix_len, rep_index, keepdims=False)
    key_pos = jnp.arange(seq_len)
    allowed = (key_pos[None, :] <= positions[:, None]) | (key_pos[None, :] < prefix)

    def score_block():
        raw = contract(query_nope, key_nope, ((2,), (2,)), ((1,), (1,)))
        raw = raw + jnp.transpose(contract(query_rot, key_rot, ((2,), (1,)), ((), ())), (1, 0, 2))
        return jnp.where(allowed[None], raw * score_scale, MASKED)

    scores = score_block()
    top_score = jnp.max(scores, axis=-1, keepdims=True)
    expo = jnp.exp(scores - top_score)
    total_exp = jnp.sum(expo, axis=-1, keepdims=True)
    log_total = top_score + jnp.log(total_exp)
    probs_low = (expo / total_exp).astype(jnp.bfloat16)
    attended = jnp.transpose(contract(probs_low, values, ((2,), (0,)), ((0,), (1,))), (1, 0, 2))
    attended = attended.reshape(tok_rows, H * DV).astype(jnp.bfloat16)
    attn_out = wide_product(attended, mat_out)
    mid = stream + attn_out
    scale_two = rms_scale(mid)
    normed_two = (mid * scale_two * gain_ffn).astype(jnp.bfloat16)
    router_prob = jax.nn.softmax(wide_product(normed_two, mat_router), axis=-1)
    one_hot = (routes[:, :, None] == jnp.arange(experts)[None, None, :]).astype(jnp.float32)
    picked = jnp.sum(one_hot * router_prob[:, None, :], axis=-1)
    picked_sum = jnp.sum(picked, axis=-1, keepdims=True)
    gates = route_weight * picked / picked_sum
    sgate_val = wide_product(normed_two, mat_sgate)
    sup_val = wide_product(normed_two, mat_sup)
    shared_hidden = (jax.nn.silu(sgate_val) * sup_val).astype(jnp.bfloat16)
    shared_out = wide_product(shared_hidden, mat_sdown)
    flat_routes = routes.reshape(-1)
    route_hot = (flat_routes[:, None] == jnp.arange(experts)[None, :]).astype(jnp.int32)
    route_rank = jnp.sum((jnp.cumsum(route_hot, axis=0) - route_hot) * route_hot, axis=1)
    slot_index = flat_routes * capacity + route_rank
    send_rows = (
        jnp.zeros((experts * capacity, D), jnp.bfloat16)
        .at[slot_index]
        .set(jnp.repeat(normed_two, TOP_K, axis=0))
    )
    doubled = jnp.broadcast_to(
        send_rows.reshape(experts, 1, capacity, D), (experts, n_shard, capacity, D)
    ).reshape(-1, D)
    incoming_rows = lax.all_to_all(
        doubled, ("rep", "shard"), split_axis=0, concat_axis=0, tiled=True
    )
    gate_local = expert_gate[0]
    local_up_weight = expert_up[0]
    down_local = expert_down[0]
    expert_gate_value = wide_product(incoming_rows, gate_local)
    expert_up_value = wide_product(incoming_rows, local_up_weight)
    expert_inner_state = (jax.nn.silu(expert_gate_value) * expert_up_value).astype(jnp.bfloat16)
    expert_part = wide_product(expert_inner_state, down_local).astype(jnp.bfloat16)
    returned = lax.all_to_all(
        expert_part, ("rep", "shard"), split_axis=0, concat_axis=0, tiled=True
    )
    expert_sum = jnp.sum(
        returned.reshape(experts, n_shard, capacity, D).astype(jnp.float32), axis=1
    ).reshape(experts * capacity, D)
    picked_rows = expert_sum[slot_index].reshape(tok_rows, TOP_K, D)
    ffn_out = shared_out + jnp.sum(gates[:, :, None] * picked_rows, axis=1)
    residual = mid + ffn_out
    squares = jnp.stack(
        [
            jnp.sum(stream * stream),
            jnp.sum(attn_out * attn_out),
            jnp.sum(mid * mid),
            jnp.sum(ffn_out * ffn_out),
            jnp.sum(residual * residual),
        ]
    )
    totals = lax.psum(squares, ("rep", "shard"))
    stats = jnp.sqrt(totals / (tok_rows * n_rep * n_shard * D))
    (
        gain_attn,
        mat_query,
        mat_latent,
        mat_rope,
        gain_latent,
        mat_kv,
        mat_out,
        gain_ffn,
        mat_router,
    ) = (
        lax.all_gather(weights[0], "shard", axis=0, tiled=True),
        lax.all_gather(weights[1], "shard", axis=0, tiled=True),
        lax.all_gather(weights[2], "shard", axis=0, tiled=True),
        lax.all_gather(weights[3], "shard", axis=0, tiled=True),
        lax.all_gather(weights[4], "shard", axis=0, tiled=True),
        lax.all_gather(weights[5], "shard", axis=0, tiled=True),
        lax.all_gather(weights[6], "shard", axis=0, tiled=True),
        lax.all_gather(weights[7], "shard", axis=0, tiled=True),
        lax.all_gather(weights[8], "shard", axis=0, tiled=True),
    )
    mat_sgate, mat_sup, mat_sdown = (
        lax.all_gather(shared_mats[0], ("rep", "shard"), axis=0, tiled=True),
        lax.all_gather(shared_mats[1], ("rep", "shard"), axis=0, tiled=True),
        lax.all_gather(shared_mats[2], ("rep", "shard"), axis=0, tiled=True),
    )
    gain_attn = gain_attn.astype(jnp.float32)
    gain_latent = gain_latent.astype(jnp.float32)
    gain_ffn = gain_ffn.astype(jnp.float32)
    grad_top = stream_grad.astype(jnp.float32)
    gate_grad = jnp.sum(grad_top[:, None, :] * picked_rows, axis=-1)
    expert_grad = (gates[:, :, None] * grad_top[:, None, :]).astype(jnp.bfloat16).reshape(-1, D)
    send_grad = jnp.zeros((experts * capacity, D), jnp.bfloat16).at[slot_index].set(expert_grad)
    doubled_grad = jnp.broadcast_to(
        send_grad.reshape(experts, 1, capacity, D), (experts, n_shard, capacity, D)
    ).reshape(-1, D)
    received_grad = lax.all_to_all(
        doubled_grad, ("rep", "shard"), split_axis=0, concat_axis=0, tiled=True
    )
    grad_edown = contract(expert_inner_state, received_grad, ((0,), (0,)), ((), ()))
    inner_state_gradient = contract(received_grad, down_local, ((1,), (1,)), ((), ()))
    gate_value_gradient = (
        inner_state_gradient * expert_up_value * swish_derivative(expert_gate_value)
    ).astype(jnp.bfloat16)
    up_value_gradient = (inner_state_gradient * jax.nn.silu(expert_gate_value)).astype(jnp.bfloat16)
    grad_egate = contract(incoming_rows, gate_value_gradient, ((0,), (0,)), ((), ()))
    expert_up_gradient = contract(incoming_rows, up_value_gradient, ((0,), (0,)), ((), ()))
    part_in_grad = contract(gate_value_gradient, gate_local, ((1,), (1,)), ((), ()))
    part_in_grad = (
        part_in_grad
        + contract(up_value_gradient, local_up_weight, ((1,), (1,)), ((), ()))
    ).astype(jnp.bfloat16)
    returned_grad = lax.all_to_all(
        part_in_grad, ("rep", "shard"), split_axis=0, concat_axis=0, tiled=True
    )
    slot_grad = jnp.sum(
        returned_grad.reshape(experts, n_shard, capacity, D).astype(jnp.float32), axis=1
    ).reshape(experts * capacity, D)
    routed_grad = jnp.sum(slot_grad[slot_index].reshape(tok_rows, TOP_K, D), axis=1)
    shared_hidden_grad = contract(stream_grad, mat_sdown, ((1,), (1,)), ((), ()))
    dshared_gate = (shared_hidden_grad * sup_val * swish_derivative(sgate_val)).astype(jnp.bfloat16)
    dshared_up = (shared_hidden_grad * jax.nn.silu(sgate_val)).astype(jnp.bfloat16)
    weighted_grad = route_weight * gate_grad
    picked_grad = weighted_grad / picked_sum - jnp.sum(
        weighted_grad * picked, axis=-1, keepdims=True
    ) / (picked_sum * picked_sum)
    prob_grad = jnp.sum(one_hot * picked_grad[:, :, None], axis=1)
    logit_grad = (
        router_prob * (prob_grad - jnp.sum(router_prob * prob_grad, axis=-1, keepdims=True))
    ).astype(jnp.bfloat16)
    normed_two_grad = contract(dshared_gate, mat_sgate, ((1,), (1,)), ((), ()))
    normed_two_grad = normed_two_grad + contract(dshared_up, mat_sup, ((1,), (1,)), ((), ()))
    normed_two_grad = normed_two_grad + contract(logit_grad, mat_router, ((1,), (1,)), ((), ()))
    normed_two_grad = normed_two_grad + routed_grad
    norm_part, grad_gain_ffn = norm_back(normed_two_grad, mid, scale_two, gain_ffn)
    mid_grad = grad_top + norm_part
    attn_out_grad = mid_grad.astype(jnp.bfloat16)
    attended_grad = contract(attn_out_grad, mat_out, ((1,), (1,)), ((), ()))
    attended_grad = attended_grad.astype(jnp.bfloat16).reshape(tok_rows, H, DV)
    probs_full = jnp.where(allowed[None], jnp.exp(score_block() - log_total), 0.0)
    value_grad = jnp.transpose(contract(probs_full.astype(jnp.bfloat16), attended_grad, ((1,), (0,)), ((0,), (1,))), (1, 0, 2))
    prob_att_grad = contract(attended_grad, values, ((2,), (2,)), ((1,), (1,)))
    scores_grad = probs_full * (
        prob_att_grad - jnp.sum(probs_full * prob_att_grad, axis=-1, keepdims=True)
    )
    scores_grad = scores_grad.astype(jnp.bfloat16)
    query_nope_grad = score_scale * jnp.transpose(contract(scores_grad, key_nope, ((2,), (0,)), ((0,), (1,))), (1, 0, 2))
    query_rot_grad = score_scale * jnp.transpose(contract(scores_grad, key_rot, ((2,), (0,)), ((), ())), (1, 0, 2))
    key_nope_grad = score_scale * jnp.transpose(contract(scores_grad, query_nope, ((1,), (0,)), ((0,), (1,))), (1, 0, 2))
    key_rot_grad = score_scale * contract(scores_grad, query_rot, ((0, 1,), (1, 0,)), ((), ()))
    keyval_grad_all = jnp.concatenate([key_nope_grad, value_grad], axis=-1).reshape(
        n_shard, kv_rows, 128
    )
    key_grad_pieces = jnp.concatenate(
        [keyval_grad_all, key_rot_grad.reshape(n_shard, rope_rows, 128)], axis=1
    )
    own_keys = lax.psum_scatter(
        key_grad_pieces.reshape(-1, 128).astype(jnp.bfloat16),
        "shard",
        scatter_dimension=0,
        tiled=True,
    ).astype(jnp.float32)
    keyval_grad = own_keys[:kv_rows].reshape(tok_rows, head_width).astype(jnp.bfloat16)
    key_pre_grad = rotate(own_keys[kv_rows:].reshape(tok_rows, DR), cosine, -sine_vals).astype(
        jnp.bfloat16
    )
    query_rot_back = rotate(query_rot_grad, cosine[:, None], -sine_vals[:, None])
    query_grad = (
        jnp.concatenate([query_nope_grad, query_rot_back], axis=-1)
        .reshape(tok_rows, H * (DN + DR))
        .astype(jnp.bfloat16)
    )
    latent_normed_grad = contract(keyval_grad, mat_kv, ((1,), (1,)), ((), ()))
    latent_pre, grad_gain_latent = norm_back(latent_normed_grad, latent, scale_lat, gain_latent)
    latent_grad = latent_pre.astype(jnp.bfloat16)
    normed_grad = contract(query_grad, mat_query, ((1,), (1,)), ((), ()))
    normed_grad = normed_grad + contract(key_pre_grad, mat_rope, ((1,), (1,)), ((), ()))
    normed_grad = normed_grad + contract(latent_grad, mat_latent, ((1,), (1,)), ((), ()))
    attn_part, grad_gain_attn = norm_back(normed_grad, stream, scale_one, gain_attn)
    grad_stream = (mid_grad + attn_part).astype(jnp.bfloat16)
    owned = (
        lax.psum_scatter(
            grad_gain_attn[None][0], ("rep", "shard"), scatter_dimension=0, tiled=True
        ),
        lax.psum_scatter(
            contract(normed, query_grad, ((0,), (0,)), ((), ())),
            ("rep", "shard"),
            scatter_dimension=0,
            tiled=True,
        ),
        lax.psum_scatter(
            contract(normed, latent_grad, ((0,), (0,)), ((), ())),
            ("rep", "shard"),
            scatter_dimension=0,
            tiled=True,
        ),
        lax.psum_scatter(
            contract(normed, key_pre_grad, ((0,), (0,)), ((), ())),
            ("rep", "shard"),
            scatter_dimension=0,
            tiled=True,
        ),
        lax.psum_scatter(
            grad_gain_latent[None][0], ("rep", "shard"), scatter_dimension=0, tiled=True
        ),
        lax.psum_scatter(
            contract(latent_normed, keyval_grad, ((0,), (0,)), ((), ())),
            ("rep", "shard"),
            scatter_dimension=0,
            tiled=True,
        ),
        lax.psum_scatter(
            contract(attended, attn_out_grad, ((0,), (0,)), ((), ())),
            ("rep", "shard"),
            scatter_dimension=0,
            tiled=True,
        ),
        lax.psum_scatter(grad_gain_ffn[None][0], ("rep", "shard"), scatter_dimension=0, tiled=True),
        lax.psum_scatter(
            contract(normed_two, logit_grad, ((0,), (0,)), ((), ())),
            ("rep", "shard"),
            scatter_dimension=0,
            tiled=True,
        ),
        lax.psum_scatter(
            contract(normed_two, dshared_gate, ((0,), (0,)), ((), ())),
            ("rep", "shard"),
            scatter_dimension=0,
            tiled=True,
        ),
        lax.psum_scatter(
            contract(normed_two, dshared_up, ((0,), (0,)), ((), ())),
            ("rep", "shard"),
            scatter_dimension=0,
            tiled=True,
        ),
        lax.psum_scatter(
            contract(shared_hidden, stream_grad, ((0,), (0,)), ((), ())),
            ("rep", "shard"),
            scatter_dimension=0,
            tiled=True,
        ),
    )
    return (
        residual.astype(jnp.bfloat16),
        grad_stream,
        stats,
        owned[0],
        owned[1],
        owned[2],
        owned[3],
        owned[4],
        owned[5],
        owned[6],
        owned[7],
        owned[8],
        owned[9],
        owned[10],
        owned[11],
        grad_egate[None],
        expert_up_gradient[None],
        grad_edown[None],
    )


def by_size(*args):
    tokens = lax.axis_size("rep") * lax.axis_size("shard") * args[0].shape[0]
    return (on_device if tokens * args[0].shape[1] <= 1 << 23 else on_device_weights)(*args)


def solution(mesh):
    placed = (
        P(("rep", "shard"), None),
        P(("rep", "shard"), None),
        P(),
        P(("rep", "shard"), None),
        P(("rep", "shard"), None),
        P("shard"),
        P("shard", None),
        P("shard", None),
        P("shard", None),
        P("shard"),
        P("shard", None),
        P("shard", None),
        P("shard"),
        P("shard", None),
        P(("rep", "shard"), None),
        P(("rep", "shard"), None),
        P(("rep", "shard"), None),
        P("rep", None, "shard"),
        P("rep", None, "shard"),
        P("rep", "shard", None),
    )
    return jax.shard_map(
        by_size,
        mesh=mesh,
        in_specs=placed,
        out_specs=(
            P(("rep", "shard"), None),
            P(("rep", "shard"), None),
            P(),
            P(("rep", "shard")),
            P(("rep", "shard"), None),
            P(("rep", "shard"), None),
            P(("rep", "shard"), None),
            P(("rep", "shard")),
            P(("rep", "shard"), None),
            P(("rep", "shard"), None),
            P(("rep", "shard")),
            P(("rep", "shard"), None),
            P(("rep", "shard"), None),
            P(("rep", "shard"), None),
            P(("rep", "shard"), None),
            P("rep", None, "shard"),
            P("rep", None, "shard"),
            P("rep", "shard", None),
        ),
        check_vma=False,
    )
```

```python
import functools
import jax
import jax.numpy as jnp
from jax import lax
from jax.experimental import pallas as pl
from jax.experimental.pallas import tpu as pltpu
from jax.sharding import PartitionSpec as P

D = 2048
H = 16
DN = 128
DR = 64
DV = 128
TOP_K = 6


EPS = 1e-06
ROPE_BASE = 10000.0
MASKED = -1e30


def wide_product(left, right):
    return jnp.dot(left, right, preferred_element_type=jnp.float32)


def contract(left, right, over, batch=((), ())):
    return lax.dot_general(left, right, (over, batch), preferred_element_type=jnp.float32)


def dot_nt(left, right):
    return contract(left, right, ((1,), (1,)))


def dot_tn(left, right):
    return contract(left, right, ((0,), (0,)))


def rms_scale(values):
    return lax.rsqrt(jnp.mean(values * values, axis=-1, keepdims=True) + EPS)


def norm_back(grad_out, inputs, row_scale, gain_vec):
    weighted = grad_out * gain_vec
    inner_mean = jnp.mean(weighted * inputs, axis=-1, keepdims=True)
    grad_in = row_scale * weighted - inputs * (row_scale * row_scale * row_scale) * inner_mean
    grad_gain = jnp.sum(grad_out * inputs * row_scale, axis=0)
    return (grad_in, grad_gain)


def rope_tables(positions, rope_width):
    frequency = ROPE_BASE ** (-2.0 * jnp.arange(rope_width // 2, dtype=jnp.float32) / rope_width)
    angles = positions.astype(jnp.float32)[:, None] * frequency[None, :]
    return (jnp.cos(angles), jnp.sin(angles))


def rotate(values, cosine, sine_vals):
    half_dim = values.shape[-1] // 2
    low_half = values[..., :half_dim]
    high_half = values[..., half_dim:]
    return jnp.concatenate(
        [low_half * cosine - high_half * sine_vals, high_half * cosine + low_half * sine_vals],
        axis=-1,
    )


def swish_derivative(values):
    sigmoid = jax.nn.sigmoid(values)
    return sigmoid * (1.0 + values * (1.0 - sigmoid))


MESH = pl.DeviceIdType.MESH
SEM = pltpu.SemaphoreType.DMA
HBM = pl.BlockSpec(memory_space=pl.ANY)

def when(ok, f):
    if ok is None: f()
    else: pl.when(ok)(f)

def place():
    rep, x = lax.axis_index("rep"), lax.axis_index("shard")
    return rep // 4, lax.rem(rep // 2, 2), lax.rem(rep, 2), x

def device(z, y, c, x):
    return ((z * 2 + y) * 2 + c, x)

def slot(z, y, c, x):
    return ((z * 2 + y) * 2 + c) * 2 + x

def neighbours(nz):
    z, y, c, x = place()
    return dict(
        zr=(device(z + 1, y, c, x), z + 1 < nz),
        zl=(device(z - 1, y, c, x), z >= 1),
        y=(device(z, 1 - y, c, x), None),
        x=(device(z, y, c, 1 - x), None),
        c=(device(z, y, 1 - c, x), None),
    )

def greet(nbr):
    bar = pltpu.get_barrier_semaphore()
    count = 0
    for dev, ok in nbr.values():
        when(ok, lambda dev=dev: pl.semaphore_signal(bar, inc=1, device_id=dev, device_id_type=MESH))
        count = count + (1 if ok is None else jnp.where(ok, 1, 0))
    pl.semaphore_wait(bar, count)

def gather_kernel(nz, x_ref, t_ref, o_ref, ot_ref, own_sem, z_send, y_send, x_send, c_send, recv, crecv):
    z, y, c, x = place()
    nbr = neighbours(nz)
    greet(nbr)
    half = x_ref.shape[0] // 2
    own = slot(z, y, c, x)
    sems = dict(zr=z_send.at[0], zl=z_send.at[1], y=y_send, x=x_send, c=c_send)

    def move(kind, h, b, mine=False):
        if h == 2:
            src, dst = t_ref if mine else ot_ref.at[b], ot_ref.at[b]
        else:
            rows = pl.ds(h * half, half)
            src, dst = x_ref.at[rows] if mine else o_ref.at[b, rows], o_ref.at[b, rows]
        return pltpu.make_async_remote_copy(
            src_ref=src, dst_ref=dst, send_sem=sems[kind].at[h, b],
            recv_sem=(crecv if kind == "c" else recv).at[h, b], device_id=nbr[kind][0], device_id_type=MESH)

    def schedule(go):
        def send(kind, h, b, mine=False):
            def f():
                for hh in (2, 0) if h == 0 else (1,):
                    d = move(kind, hh, b, mine)
                    d.start() if go else d.wait_send()

            when(nbr[kind][1], f)

        def arrive(h, b):
            if go:
                for hh in (2, 0) if h == 0 else (1,):
                    move("x", hh, b).wait_recv()

        second, third = ("y", "x"), ("x", "y")
        for h in (0, 1):
            send("zr", h, own, True)
            send("zl", h, own, True)
            send(second[h], h, own, True)
        for h in (0, 1):
            send(third[h], h, own, True)
            send("c", h, own, True)
        rounds = [[(z, None)]]
        for s in range(nz - 1):
            rounds.append([(z - 1 - s, z - 1 - s >= 0), (z + 1 + s, z + 1 + s < nz)])

        def drain1(rnd):
            for i, (zb, ok) in enumerate(rnd):
                for h in (0, 1):
                    def f(zb=zb, h=h, i=i):
                        b = slot(zb, y, c, x)
                        arrive(h, b)
                        send("zr" if i == 0 else "zl", h, b)
                        send(second[h], h, b)
                        send(third[h], h, b)
                        send("c", h, b)
                    when(ok, f)

        def drain2(rnd):
            for zb, ok in rnd:
                for h in (0, 1):
                    def f(zb=zb, h=h):
                        b = slot(zb, 1 - y, c, x) if h == 0 else slot(zb, y, c, 1 - x)
                        arrive(h, b)
                        send(third[h], h, b)
                        send("c", h, b)
                    when(ok, f)

        def drain3(rnd):
            for zb, ok in rnd:
                for h in (0, 1):
                    def f(zb=zb, h=h):
                        b = slot(zb, y, c, 1 - x) if h == 0 else slot(zb, 1 - y, c, x)
                        arrive(h, b)
                        send("c", h, b)
                        b = slot(zb, 1 - y, c, 1 - x)
                        arrive(h, b)
                        send("c", h, b)
                    when(ok, f)

        for s in range(nz - 1):
            drain1(rounds[s + 1])
            drain2(rounds[s])
            if s >= 1:
                drain3(rounds[s - 1])
        drain2(rounds[nz - 1])
        drain3(rounds[nz - 2])
        drain3(rounds[nz - 1])

    local = [
        pltpu.make_async_copy(x_ref, o_ref.at[own], own_sem.at[0]),
        pltpu.make_async_copy(t_ref, ot_ref.at[own], own_sem.at[1]),
    ]
    for d in local:
        d.start()
    schedule(True)
    for zb in range(nz):
        for yb in range(2):
            for xb in range(2):
                for h in (2, 0, 1):
                    move("c", h, slot(zb, yb, 1 - c, xb)).wait_recv()
    for d in local:
        d.wait()
    schedule(False)


def all_gather(x, t, n, nz, cid):
    return pl.pallas_call(
        functools.partial(gather_kernel, nz),
        out_shape=[jax.ShapeDtypeStruct((n,) + v.shape, v.dtype) for v in (x, t)],
        in_specs=[pl.BlockSpec(memory_space=pl.ANY)] * 2,
        out_specs=[pl.BlockSpec(memory_space=pl.ANY)] * 2,
        scratch_shapes=[SEM((2,)), SEM((2, 3, n)), SEM((3, n)), SEM((3, n)), SEM((3, n)), SEM((3, n)), SEM((3, n))],
        cost_estimate=lasting(85),
        compiler_params=pltpu.CompilerParams(collective_id=cid, has_side_effects=True),
    )(x, t)


def far_first(nz, z):
    def pick(i):
        total = 0
        for k in range(nz):
            ranked = sorted(range(nz), key=lambda d: (-abs(d - k), -d if k < nz // 2 else d))
            total = total + jnp.where(z == k, ranked[i], 0)
        return total
    return [pick(i) for i in range(nz)]

def add_rows(total, other, lo, other_lo, count):
    step = next(k for k in (32, 16, 8) if count % k == 0)

    def body(i, carry):
        r = pl.ds(pl.multiple_of(lo + i * step, step), step)
        s = pl.ds(pl.multiple_of(other_lo + i * step, step), step)
        total[r] = total[r] + other[s]
        return carry

    lax.fori_loop(0, count // step, body, 0)


SCATTERING = [
    ("s0", 0), ("s0", 1), ("n", 0), ("c", 0), ("f", 0), ("c", 1), ("c", 2), ("f", 1), ("s0", 2), ("s2", 0), ("n", 1), ("f", 2),
    ("s0", 3), ("s2", 1), ("n", 2), ("s2", 2), ("f", 3), ("n", 3), ("c", 3), ("s2", 3),
]


def scatter_kernel(nz, x_ref, rows_in, rows_grad, hid, dg, du, o_ref, dwg_o, dwu_o, dwd_o, mine, core, one, two, line,
                   dwg, dwu, dwd, b_in, b_grad, b_hid, b_dg, b_du, load_sem, core_send, core_recv, one_send, one_recv,
                   two_send, two_recv, line_send, line_recv, chunk_sem, out_sem):
    z, y, c, x = place()
    nbr = neighbours(nz)
    greet(nbr)
    T = mine.shape[1]
    half = T // 2
    rows = lambda h: pl.ds(h * half, half)
    place_of = lambda zb, yb, xb: (zb * 2 + yb) * 2 + xb
    count = b_in.shape[1]
    chunks = rows_in.shape[0] // count

    def chunk_copies(i):
        r = pl.ds(i * count, count)
        pairs = ((rows_in, b_in), (rows_grad, b_grad), (hid, b_hid), (dg, b_dg), (du, b_du))
        return [pltpu.make_async_copy(a.at[r], b.at[i % 2], chunk_sem.at[i % 2, j]) for j, (a, b) in enumerate(pairs)]

    def result(j):
        out, b = ((dwg_o, b_in), (dwu_o, b_grad), (dwd_o, b_in))[j]
        spans = [(k, lo, min(count, out.shape[0] - lo)) for k, lo in enumerate(range(0, out.shape[0], count))]
        return spans, [
            pltpu.make_async_copy(b.at[k, pl.ds(0, n)], out.at[pl.ds(lo, n)], out_sem.at[j, k]) for k, lo, n in spans
        ]

    def write(j):
        total, b = ((dwg, b_in), (dwu, b_grad), (dwd, b_in))[j]
        spans, copies = result(j)
        for k, lo, n in spans:
            b[k, 0:n] = total[lo : lo + n].astype(b.dtype)
        for d in copies:
            d.start()

    def written(j):
        for d in result(j)[1]:
            d.wait()

    def chunk(i):
        if i >= chunks:
            return
        for d in chunk_copies(i):
            d.wait()
        k = i % 2
        terms = ((dwd, b_hid, b_grad), (dwg, b_dg, b_in), (dwu, b_du, b_in))
        for total, a, b in terms:
            v = dot_tn(a[k], b[k])
            total[...] = v if i == 0 else total[...] + v
        if i + 2 < chunks:
            for d in chunk_copies(i + 2):
                d.start()
        if i == chunks - 1:
            write(0)
            write(1)

    order = far_first(nz, z)
    combos = [(1 - y, 1 - x), (y, 1 - x), (1 - y, x), (y, x)]

    def core_copy(zb, yb, xb):
        k = place_of(zb, yb, xb)
        return remote(x_ref.at[slot(zb, yb, 1 - c, xb)], core.at[k], core_send.at[k], core_recv.at[k], nbr["c"][0])

    def load(zb, yb, xb):
        k = place_of(zb, yb, xb)
        return pltpu.make_async_copy(x_ref.at[slot(zb, yb, c, xb)], mine.at[k], load_sem.at[k])

    def one_copy(h, zb, j):
        k = place_of(zb, j, 1 - x) if h == 0 else place_of(zb, 1 - y, j)
        i = zb * 2 + j
        return remote(mine.at[k, rows(h)], one.at[h, i], one_send.at[h, i], one_recv.at[h, i], nbr["x" if h == 0 else "y"][0])

    def two_copy(h, zb):
        k = place_of(zb, 1 - y, x) if h == 0 else place_of(zb, y, 1 - x)
        return remote(mine.at[k, rows(h)], two.at[h, zb], two_send.at[h, zb], two_recv.at[h, zb], nbr["y" if h == 0 else "x"][0])

    def line_copy(h, zb, right):
        k = place_of(zb, y, x)
        d = 0 if right else 1
        return remote(mine.at[k, rows(h)], line.at[d, h, zb], line_send.at[h, zb], line_recv.at[d, h, zb], nbr["zr" if right else "zl"][0])

    for zb in order:
        for yb, xb in combos:
            core_copy(zb, yb, xb).start()
            load(zb, yb, xb).start()
    for i in range(min(2, chunks)):
        for d in chunk_copies(i):
            d.start()

    def stage0(zb):
        for n, (yb, xb) in enumerate(combos):
            k = place_of(zb, yb, xb)
            core_copy(zb, yb, xb).wait_recv()
            load(zb, yb, xb).wait()
            add_rows(mine.at[k], core.at[k], 0, 0, T)
            if n in (0, 1):
                one_copy(0, zb, yb).start()
            if n in (0, 2):
                one_copy(1, zb, xb).start()

    def stage1(zb, far):
        for h in (0, 1):
            j = (1 - y if far else y) if h == 0 else (1 - x if far else x)
            one_copy(h, zb, j).wait_recv()
            k = place_of(zb, j, x) if h == 0 else place_of(zb, y, j)
            add_rows(mine.at[k], one.at[h, zb * 2 + j], h * half, 0, half)
            if far:
                two_copy(h, zb).start()

    def stage2(zb):
        k = place_of(zb, y, x)
        for h in (0, 1):
            two_copy(h, zb).wait_recv()
            add_rows(mine.at[k], two.at[h, zb], h * half, 0, half)
            def go(right, h=h):
                line_copy(h, zb, right).wait_recv()
                add_rows(mine.at[k], line.at[0 if right else 1, h, zb], h * half, 0, half)
            when(jnp.logical_and(zb > z, z >= 1), lambda: go(True))
            when(jnp.logical_and(zb < z, z + 1 < nz), lambda: go(False))
            when(zb > z, lambda: line_copy(h, zb, True).start())
            when(zb < z, lambda: line_copy(h, zb, False).start())

    stages = dict(s0=stage0, f=lambda zb: stage1(zb, True), n=lambda zb: stage1(zb, False), s2=stage2)
    plain = [(n, i) for i in range(max(nz, chunks)) for n in ("s0", "c", "f", "n", "s2") if n == "c" or i < nz]
    for name, i in SCATTERING if nz == chunks == 4 else plain:
        chunk(i) if name == "c" else stages[name](order[i])
    written(0)
    write(2)
    k = place_of(z, y, x)
    for h in (0, 1):
        lo = h * half
        o_ref[rows(h)] = mine[k, rows(h)].astype(jnp.float32)
        for d, ok in ((0, z >= 1), (1, z + 1 < nz)):
            def fin(d=d, h=h):
                line_copy(h, z, d == 0).wait_recv()
                o_ref[rows(h)] += line[d, h, z].astype(jnp.float32)
            when(ok, fin)
    written(1)
    written(2)
    for zb in order:
        for yb, xb in combos:
            core_copy(zb, yb, xb).wait_send()
        for h in (0, 1):
            for j in (0, 1):
                one_copy(h, zb, j).wait_send()
            two_copy(h, zb).wait_send()
            when(zb > z, lambda: line_copy(h, zb, True).wait_send())
            when(zb < z, lambda: line_copy(h, zb, False).wait_send())

def reduce_scatter(v, rows_in, rows_grad, hid, dg, du, nz, cid):
    n, tok, width = v.shape
    rows, wide = rows_in.shape
    f = hid.shape[1]
    parts = next(k for k in (4, 2, 1) if rows % (k * 16) == 0)
    b16, f32, sd = v.dtype, jnp.float32, jax.ShapeDtypeStruct
    buf = lambda *shape: pltpu.VMEM(shape, b16)
    grad = sd((f, wide), b16)
    return pl.pallas_call(
        functools.partial(scatter_kernel, nz),
        out_shape=[sd((tok, width), f32), grad, grad, grad],
        in_specs=[HBM] * 6,
        out_specs=[pl.BlockSpec(memory_space=pltpu.VMEM), HBM, HBM, HBM],
        scratch_shapes=[buf(n // 2, tok, width), buf(n // 2, tok, width), buf(2, 2 * nz, tok // 2, width),
                        buf(2, nz, tok // 2, width), buf(2, 2, nz, tok // 2, width)]
        + [pltpu.VMEM((f, wide), f32)] * 3
        + [buf(2, rows // parts, k) for k in (wide, wide, f, f, f)]
        + [SEM((n // 2,)), SEM((n // 2,)), SEM((n // 2,)), SEM((2, 2 * nz)), SEM((2, 2 * nz)), SEM((2, nz)), SEM((2, nz)),
           SEM((2, nz)), SEM((2, 2, nz)), SEM((2, 5)), SEM((3, 2))],
        cost_estimate=lasting(90),
        compiler_params=pltpu.CompilerParams(collective_id=cid, has_side_effects=True, vmem_limit_bytes=64 << 20),
    )(v, rows_in, rows_grad, hid, dg, du)


def lasting(us):
    return pl.CostEstimate(flops=0, bytes_accessed=int(us * 3.5e6), transcendentals=0)


def remote(src, dst, send_sem, recv_sem, dev):
    return pltpu.make_async_remote_copy(
        src_ref=src, dst_ref=dst, send_sem=send_sem, recv_sem=recv_sem, device_id=dev, device_id_type=MESH
    )


def quad_neighbours():
    z, y, c, x = place()
    return dict(x=(device(z, y, c, 1 - x), None), c=(device(z, y, 1 - c, x), None))


def open_kernel(nz, stream, wq, kv, lat, tiny, stream_all, wq_o, kv_o, lat_o, tiny_o, b0, b1, b2, b3, b4,
                load, store, send, recv, x_send, x_recv, zr_send, zl_send, y_send, p_recv):
    z, y, c, x = place()
    nbr = neighbours(nz)
    greet(nbr)
    quads = 2 * nz
    own, side, other = c * 2 + x, c * 2 + 1 - x, 1 - x
    rows = lat.shape[0] // 2
    xdev, cdev = nbr["x"][0], nbr["c"][0]

    def heads(ref, out, xx):
        n = out.shape[2]
        return ref.at[:, pl.ds(pl.multiple_of((xx * 2 + c) * n, 128), n)]

    def rows_of(a, j):
        n = (wq.shape[0] // quads, kv.shape[0] // quads, rows // quads)[a]
        return pl.ds(pl.multiple_of((c * rows if a == 2 else 0) + j * n, n), n)

    def piece(a, j):
        return (wq_o, kv_o, lat_o)[a].at[other, rows_of(a, j)]

    mine = z * 2 + y

    def first(a):
        r = rows_of(a, mine)
        if a == 2:
            src, dst = lat.at[r], lat_o.at[x, r]
        else:
            ref, out = ((wq, wq_o), (kv, kv_o))[a]
            n = out.shape[2]
            src, dst = ref.at[r, pl.ds(pl.multiple_of((other * 2 + c) * n, 128), n)], out.at[x, r]
        return remote(src, dst, x_send.at[a], x_recv.at[a], xdev)

    def along(a, j, kind):
        sems = dict(zr=zr_send, zl=zl_send, y=y_send)[kind]
        return remote(piece(a, j), piece(a, j), sems.at[a, j], p_recv.at[a, j], nbr[kind][0])

    kinds = (2, 1, 0)
    for a in kinds:
        first(a).start()
    xs = [
        remote(stream, stream_all.at[own], send.at[0], recv.at[0], xdev),
        remote(tiny, tiny_o.at[x], send.at[1], recv.at[1], xdev),
    ]
    for d in xs:
        d.start()
    cs = [remote(stream, stream_all.at[own], send.at[2], recv.at[2], cdev)]
    cs[0].start()
    here = [
        (stream, b0, stream_all.at[own]), (tiny, b4, tiny_o.at[x]), (lat, b3, lat_o.at[x]),
        (heads(kv, kv_o, x), b2, kv_o.at[x]), (heads(wq, wq_o, x), b1, wq_o.at[x]),
    ]
    for i, (a, b, o) in enumerate(here):
        pltpu.make_async_copy(a, b, load.at[i]).start()
    for i, (a, b, o) in enumerate(here):
        pltpu.make_async_copy(a, b, load.at[i]).wait()
        pltpu.make_async_copy(b, o, store.at[i]).start()

    def spread(go):
        def send(a, j, kind):
            d = along(a, j, kind)
            ok = nbr[kind][1]
            when(ok, (lambda: d.start()) if go else (lambda: d.wait_send()))

        for a in kinds:
            if go:
                first(a).wait_recv()
            for kind in ("zr", "zl", "y"):
                send(a, mine, kind)
        for s in range(nz - 1):
            for kind, zb, ok in (("zr", z - 1 - s, z - 1 - s >= 0), ("zl", z + 1 + s, z + 1 + s < nz)):

                def f(kind=kind, zb=zb):
                    j = zb * 2 + y
                    for a in kinds:
                        if go:
                            along(a, j, "y").wait_recv()
                        send(a, j, kind)
                        send(a, j, "y")

                pl.when(ok)(f)

    spread(True)
    xs[0].wait_recv()
    cs.append(remote(stream_all.at[side], stream_all.at[side], send.at[3], recv.at[3], cdev))
    cs[1].start()
    xs[1].wait_recv()
    for zb in range(nz):
        for a in kinds:
            along(a, zb * 2 + 1 - y, "y").wait_recv()
    half = pl.ds(pl.multiple_of(c * rows, rows), rows)
    cs.append(remote(lat_o.at[other, half], lat_o.at[other, half], send.at[4], recv.at[4], cdev))
    cs[2].start()
    for d in cs:
        d.wait_recv()
    for i, (a, b, o) in enumerate(here):
        pltpu.make_async_copy(b, o, store.at[i]).wait()
    for d in xs + cs:
        d.wait_send()
    for a in kinds:
        first(a).wait_send()
    spread(False)


def open_quad(stream, wq, kv, lat, tiny, nz, cid):
    sd = jax.ShapeDtypeStruct
    ins = (stream, wq, kv, lat, tiny)
    shapes = [(4,) + stream.shape, (2, wq.shape[0], wq.shape[1] // 4), (2, kv.shape[0], kv.shape[1] // 4), (2,) + lat.shape, (2,) + tiny.shape]
    pieces = SEM((3, 2 * nz))
    return pl.pallas_call(
        functools.partial(open_kernel, nz),
        out_shape=[sd(shape, v.dtype) for shape, v in zip(shapes, ins)],
        in_specs=[HBM] * 5,
        out_specs=[HBM] * 5,
        scratch_shapes=[pltpu.VMEM(shape[1:], v.dtype) for shape, v in zip(shapes, ins)]
        + [SEM((5,)), SEM((5,)), SEM((5,)), SEM((5,)), SEM((3,)), SEM((3,)), pieces, pieces, pieces, pieces],
        cost_estimate=lasting(50),
        compiler_params=pltpu.CompilerParams(collective_id=cid, has_side_effects=True, vmem_limit_bytes=16 << 20),
    )(*ins)


def split_kernel(units, gate, up, out):
    lanes = out.shape[2] // 2
    for j in range(out.shape[0]):
        lo = min(units * j // 128 * 128, gate.shape[1] - 2 * lanes)
        row = lax.broadcasted_iota(jnp.int32, (2 * lanes, lanes), 0)
        lane = lax.broadcasted_iota(jnp.int32, (2 * lanes, lanes), 1)
        pick = ((row == lane + (units * j - lo)) & (lane < units)).astype(jnp.float32).astype(gate.dtype)
        for k, ref in enumerate((gate, up)):
            out[j, :, k * lanes : (k + 1) * lanes] = wide_product(ref[:, lo : lo + 2 * lanes], pick).astype(out.dtype)


def split_units(gate, up, n_dev, units):
    vmem = pl.BlockSpec(memory_space=pltpu.VMEM)
    return pl.pallas_call(
        functools.partial(split_kernel, units),
        out_shape=jax.ShapeDtypeStruct((n_dev, gate.shape[0], 256), gate.dtype),
        in_specs=[vmem, vmem],
        out_specs=vmem,
        cost_estimate=lasting(4),
        compiler_params=pltpu.CompilerParams(vmem_limit_bytes=16 << 20),
    )(gate, up)


def join_kernel(units, blocks, gate, up):
    lanes = blocks.shape[2] // 2
    row = lax.broadcasted_iota(jnp.int32, (lanes, lanes), 0)
    lane = lax.broadcasted_iota(jnp.int32, (lanes, lanes), 1)
    for t in range(gate.shape[1] // lanes):
        totals = [None, None]
        for j in range(lanes * t // units, (lanes * t + lanes - 1) // units + 1):
            pick = ((row + (units * j - lanes * t) == lane) & (row < units)).astype(jnp.float32).astype(blocks.dtype)
            for k in (0, 1):
                v = wide_product(blocks[j, :, k * lanes : (k + 1) * lanes], pick)
                totals[k] = v if totals[k] is None else totals[k] + v
        for k, ref in enumerate((gate, up)):
            ref[:, t * lanes : (t + 1) * lanes] = totals[k]


def join_units(blocks, total, units):
    vmem = pl.BlockSpec(memory_space=pltpu.VMEM)
    out = jax.ShapeDtypeStruct((blocks.shape[1], total), jnp.float32)
    return pl.pallas_call(
        functools.partial(join_kernel, units),
        out_shape=[out, out],
        in_specs=[vmem],
        out_specs=[vmem, vmem],
        cost_estimate=lasting(4),
        compiler_params=pltpu.CompilerParams(vmem_limit_bytes=16 << 20),
    )(blocks)


def quad_gather_kernel(x_ref, o_ref, local, send, recv):
    z, y, c, x = place()
    nbr = quad_neighbours()
    greet(nbr)
    own, side = c * 2 + x, c * 2 + 1 - x
    half = x_ref.shape[0] // 2
    copies = []
    for h in (0, 1):
        r = pl.ds(h * half, half)
        a = remote(x_ref.at[r], o_ref.at[own, r], send.at[0, h], recv.at[0, h], nbr["x"][0])
        b = remote(x_ref.at[r], o_ref.at[own, r], send.at[1, h], recv.at[1, h], nbr["c"][0])
        d = remote(o_ref.at[side, r], o_ref.at[side, r], send.at[2, h], recv.at[2, h], nbr["c"][0])
        a.start()
        b.start()
        copies.append((a, b, d))
    here = pltpu.make_async_copy(x_ref, o_ref.at[own], local)
    here.start()
    for a, b, d in copies:
        a.wait_recv()
        d.start()
    for a, b, d in copies:
        b.wait_recv()
        d.wait_recv()
        a.wait_send()
        b.wait_send()
        d.wait_send()
    here.wait()


def quad_gather(v, cid):
    return pl.pallas_call(
        quad_gather_kernel,
        out_shape=jax.ShapeDtypeStruct((4,) + v.shape, v.dtype),
        in_specs=[HBM],
        out_specs=HBM,
        scratch_shapes=[SEM, SEM((3, 2)), SEM((3, 2))],
        cost_estimate=lasting(18),
        compiler_params=pltpu.CompilerParams(collective_id=cid, has_side_effects=True),
    )(v)


def quad_scatter_kernel(v_ref, o_ref, mine, core, far, load, send, recv):
    z, y, c, x = place()
    nbr = quad_neighbours()
    greet(nbr)
    half = o_ref.shape[0] // 2
    steps = []
    for h in (0, 1):
        r = pl.ds(h * half, half)
        for j, xb in ((0, 1 - x), (1, x)):
            a = remote(v_ref.at[(1 - c) * 2 + xb, r], core.at[j, r], send.at[j, h], recv.at[j, h], nbr["c"][0])
            b = pltpu.make_async_copy(v_ref.at[c * 2 + xb, r], mine.at[j, r], load.at[j, h])
            a.start()
            b.start()
            steps.append((a, b))
    outs = []
    for h in (0, 1):
        r = pl.ds(h * half, half)
        a, b = steps[2 * h]
        a.wait_recv()
        b.wait()
        add_rows(mine.at[0], core.at[0], h * half, h * half, half)
        f = remote(mine.at[0, r], far.at[r], send.at[2, h], recv.at[2, h], nbr["x"][0])
        f.start()
        outs.append(f)
    for h in (0, 1):
        a, b = steps[2 * h + 1]
        a.wait_recv()
        b.wait()
        outs[h].wait_recv()
        def body(i, carry, h=h):
            r = pl.ds(pl.multiple_of(h * half + i * 16, 16), 16)
            o_ref[r] = (mine[1, r].astype(jnp.float32) + core[1, r].astype(jnp.float32)) + far[r].astype(jnp.float32)
            return carry
        lax.fori_loop(0, half // 16, body, 0)
    for a, b in steps:
        a.wait_send()
    for f in outs:
        f.wait_send()


def quad_scatter(v, cid):
    _, rows, cols = v.shape
    buf = pltpu.VMEM((2, rows, cols), v.dtype)
    return pl.pallas_call(
        quad_scatter_kernel,
        out_shape=jax.ShapeDtypeStruct((rows, cols), jnp.float32),
        in_specs=[HBM],
        out_specs=pl.BlockSpec(memory_space=pltpu.VMEM),
        scratch_shapes=[buf, buf, pltpu.VMEM((rows, cols), v.dtype), SEM((2, 2)), SEM((3, 2)), SEM((3, 2))],
        cost_estimate=lasting(16),
        compiler_params=pltpu.CompilerParams(
            collective_id=cid, has_side_effects=True, vmem_limit_bytes=24 << 20
        ),
    )(v)


CLOSING = [
    ("w0", 0), ("t0", 0), ("wa", 0), ("w0", 1), ("wb", 0), ("w0", 2), ("t0", 1), ("wb", 1), ("t1", 0), ("wa", 1), ("wa", 2),
    ("w0", 3), ("t0", 2), ("t1", 1), ("t2", 0), ("wa", 3), ("wb", 2), ("t1", 2), ("t0", 3), ("t2", 1), ("t2", 2), ("t1", 3),
    ("wb", 3), ("t2", 3),
]


def finish_kernel(nz, na, there, own, far, stream, attn, mid, *refs):
    ins, refs = refs[:na], refs[na:]
    others, refs = dict(zip(there, refs)), refs[len(there) :]
    (res_o, q_o, kv_o, out_o, lat_o, router_o, side_o, stat_o), refs = refs[:8], refs[8:]
    (t_mine, t_core, t_one, t_two, t_line, ffn), refs = refs[:6], refs[6:]
    mine, refs = refs[:na], refs[na:]
    one, refs = refs[:na], refs[na:]
    line, refs = refs[:na], refs[na:]
    (q_all, kv_all, out_all, side_all, stat, stat_in), refs = refs[:6], refs[6:]
    (t_load, core_send, core_recv, tx_send, tx_recv, ty_send, ty_recv, tz_send, tz_recv,
     load, y_send, y_recv, z_send, z_recv, own_sem, q_send, q_recv, out_send, out_recv, st_send, st_recv) = refs
    z, y, c, x = place()
    nbr = neighbours(nz)
    nbr["d"] = (device(z, y, 1 - c, 1 - x), None)
    quads = 2 * nz
    linear = slot(z, y, c, x)
    target = (x * 2 + c) * quads + z * 2 + y
    group, q = linear // quads, lax.rem(linear, quads)
    source = device(q // 2, lax.rem(q, 2), lax.rem(group, 2), group // 2)
    away = target != linear
    nbr["to"] = ((target // 2, lax.rem(target, 2)), away)
    nbr["from"] = (source, away)
    here_q = z * 2 + y
    for j in range(1, quads):
        to_q = lax.rem(here_q + j, quads)
        nbr["q%d" % j] = (device(to_q // 2, lax.rem(to_q, 2), c, x), None)
    greet(nbr)
    order = far_first(nz, z)
    xdev, cdev, ddev, ydev = (nbr[k][0] for k in ("x", "c", "d", "y"))
    zdev = lambda right: nbr["zr" if right else "zl"][0]
    add = lambda total, other: add_rows(total, other, 0, 0, total.shape[0])
    place_of = lambda zb, yb, xb: (zb * 2 + yb) * 2 + xb
    combos = [(1 - y, 1 - x), (y, 1 - x), (1 - y, x), (y, x)]

    def t_core_copy(k):
        return remote(far.at[k], t_core.at[k], core_send.at[k], core_recv.at[k], cdev)

    def t_load_copy(k):
        return pltpu.make_async_copy(own.at[k], t_mine.at[k], t_load.at[k])

    def tx_copy(zb, yb):
        i = zb * 2 + yb
        return remote(t_mine.at[place_of(zb, yb, 1 - x)], t_one.at[i], tx_send.at[i], tx_recv.at[i], xdev)

    def ty_copy(zb):
        return remote(t_mine.at[place_of(zb, 1 - y, x)], t_two.at[zb], ty_send.at[zb], ty_recv.at[zb], ydev)

    def tz_copy(zb, right):
        d = 0 if right else 1
        return remote(t_mine.at[place_of(zb, y, x)], t_line.at[d, zb], tz_send.at[zb], tz_recv.at[d, zb], zdev(right))

    def t_stage0(zb):
        for i, (yb, xb) in enumerate(combos):
            k = place_of(zb, yb, xb)
            t_core_copy(k).wait_recv()
            t_load_copy(k).wait()
            add(t_mine.at[k], t_core.at[k])
            if i < 2:
                tx_copy(zb, yb).start()

    def t_stage1(zb):
        for yb in (1 - y, y):
            tx_copy(zb, yb).wait_recv()
            add(t_mine.at[place_of(zb, yb, x)], t_one.at[zb * 2 + yb])
            if yb is not y:
                ty_copy(zb).start()

    def on_line(zb, arrive, leave):
        when(jnp.logical_and(zb > z, z >= 1), lambda: arrive(True))
        when(jnp.logical_and(zb < z, z + 1 < nz), lambda: arrive(False))
        when(zb > z, lambda: leave(True))
        when(zb < z, lambda: leave(False))

    def t_stage2(zb):
        total = t_mine.at[place_of(zb, y, x)]
        ty_copy(zb).wait_recv()
        add(total, t_two.at[zb])

        def arrive(right):
            tz_copy(zb, right).wait_recv()
            add(total, t_line.at[0 if right else 1, zb])

        on_line(zb, arrive, lambda right: tz_copy(zb, right).start())

    apart = [a for a in range(na) if a not in others]

    def w_load(a, k):
        src = ins[a].at[k, c * 2 + x] if len(ins[a].shape) == 4 else ins[a].at[k]
        return pltpu.make_async_copy(src, mine[a].at[k], load.at[a, k])

    def wy_copy(a, zb):
        if a in others:
            return pltpu.make_async_copy(others[a].at[zb], one[a].at[zb], y_recv.at[a, zb])
        return remote(mine[a].at[zb * 2 + 1 - y], one[a].at[zb], y_send.at[a, zb], y_recv.at[a, zb], ydev)

    def wz_copy(a, zb, right):
        d = 0 if right else 1
        return remote(mine[a].at[zb * 2 + y], line[a].at[d, zb], z_send.at[a, zb], z_recv.at[d, a, zb], zdev(right))

    def w_stage0(zb):
        for a in apart:
            w_load(a, zb * 2 + 1 - y).wait()
            wy_copy(a, zb).start()

    def w_stage1(zb, some):
        for a in some:
            total = mine[a].at[zb * 2 + y]
            w_load(a, zb * 2 + y).wait()
            d = wy_copy(a, zb)
            d.wait() if a in others else d.wait_recv()
            add(total, one[a].at[zb])

            def arrive(right):
                wz_copy(a, zb, right).wait_recv()
                add(total, line[a].at[0 if right else 1, zb])

            on_line(zb, arrive, lambda right: wz_copy(a, zb, right).start())

    for zb in order:
        for yb, xb in combos:
            k = place_of(zb, yb, xb)
            t_core_copy(k).start()
            t_load_copy(k).start()
        for a in apart:
            w_load(a, zb * 2 + 1 - y).start()
        for a in range(na):
            w_load(a, zb * 2 + y).start()
        for a in others:
            wy_copy(a, zb).start()
    stages = dict(
        w0=w_stage0, t0=t_stage0, t1=t_stage1, t2=t_stage2,
        wa=lambda zb: w_stage1(zb, there), wb=lambda zb: w_stage1(zb, apart),
    )
    for name, i in CLOSING if nz == 4 else [(n, i) for i in range(nz) for n in ("w0", "t0", "wa", "wb", "t1", "t2")]:
        stages[name](order[i])

    here = t_mine.at[place_of(z, y, x)]
    for right, ok in ((True, z >= 1), (False, z + 1 < nz)):

        def last(right=right):
            tz_copy(z, right).wait_recv()

        when(ok, last)
    rows = 16

    def body(i, sums):
        r = pl.ds(pl.multiple_of(i * rows, rows), rows)
        left = jnp.where(z >= 1, t_line[0, z, r].astype(jnp.float32), 0.0)
        right = jnp.where(z + 1 < nz, t_line[1, z, r].astype(jnp.float32), 0.0)
        v = here[r].astype(jnp.float32) + left + right
        total = mid[r] + v
        res_o[r] = total.astype(res_o.dtype)
        fold = lambda u: jnp.sum((u * u).reshape(rows, -1, 128), axis=(0, 1))[None]
        terms = (stream[r].astype(jnp.float32), attn[r], mid[r], v, total)
        return tuple(s + fold(u) for s, u in zip(sums, terms))

    sums = lax.fori_loop(0, mid.shape[0] // rows, body, (jnp.zeros((1, 128), jnp.float32),) * 5)
    stat[...] = jnp.concatenate(sums + (jnp.zeros((3, 128), jnp.float32),), axis=0)
    near, wide = ["x", "c", "d"], ["q%d" % j for j in range(1, quads)]

    def stat_copy(keys, key):
        i = 3 * (keys is wide) + keys.index(key)
        return remote(stat, stat_in.at[i], st_send.at[i], st_recv.at[i], nbr[key][0])

    def stat_start(keys):
        for key in keys:
            stat_copy(keys, key).start()

    def stat_end(keys):
        for key in keys:
            stat_copy(keys, key).wait()
        total = stat[...]
        for i in range(len(keys)):
            total = total + stat_in[3 * (keys is wide) + i]
        stat[...] = total

    stat_start(near)

    k = z * 2 + y
    member, group = c * 2 + x, x * 2 + c
    waits = []
    spread = {0: q_all, 1: kv_all, na - 1: side_all}
    for n_done, a in enumerate((2, 0, 1, 3, 4, na - 1)):
        total = mine[a].at[k]

        def fin(right):
            wz_copy(a, z, right).wait_recv()
            add(total, line[a].at[0 if right else 1, z])

        when(z >= 1, lambda: fin(True))
        when(z + 1 < nz, lambda: fin(False))
        if a in spread:
            dst = spread[a]
            part = dst.shape[1]
            piece = lambda m: total if a == na - 1 else total.at[pl.ds(pl.multiple_of(m * part, part), part)]
            d = pltpu.make_async_copy(piece(member), dst.at[group], own_sem.at[a])
            d.start()
            waits.append(d)
            for i, (dev, cc, xx) in enumerate(((xdev, c, 1 - x), (cdev, 1 - c, x), (ddev, 1 - c, 1 - x))):
                d = remote(piece(cc * 2 + xx), dst.at[group], q_send.at[a, i], q_recv.at[a, i], dev)
                d.start()
                waits.append(d)
        elif a == 2:
            to = remote(total, out_all, out_send, out_recv, nbr["to"][0])
            stay = pltpu.make_async_copy(total, out_all, own_sem.at[a])
            when(away, lambda: to.start())
            when(jnp.logical_not(away), lambda: stay.start())

        if n_done == 1:
            stat_end(near)
            stat_start(wide)
    stat_end(wide)
    stat_o[...] = stat[...]
    router_o[...] = mine[4][k].astype(jnp.float32)
    lat_o[...] = mine[3][k].astype(jnp.float32)
    when(away, lambda: to.wait())
    when(jnp.logical_not(away), lambda: stay.wait())
    out_o[...] = out_all[...].astype(jnp.float32)
    for d in waits:
        d.wait()
    for g in range(4):
        for dst, src in ((q_o, q_all), (kv_o, kv_all)):
            n = src.shape[2]
            dst[:, g * n : (g + 1) * n] = src[g].astype(jnp.float32)
    side_o[...] = side_all[0] + side_all[1] + side_all[2] + side_all[3]

    for zb in order:
        for yb, xb in combos:
            t_core_copy(place_of(zb, yb, xb)).wait_send()
        for yb in (1 - y, y):
            tx_copy(zb, yb).wait_send()
        ty_copy(zb).wait_send()
        on_line(zb, lambda right: None, lambda right: tz_copy(zb, right).wait_send())
        for a in range(na):
            if a in apart:
                wy_copy(a, zb).wait_send()
            on_line(zb, lambda right: None, lambda right: wz_copy(a, zb, right).wait_send())


def finish(own, far, stream, attn, mid, arrays, swapped, nz, cid):
    na = len(arrays)
    tok, width = mid.shape
    n, quads = 4 * nz, 2 * nz
    f32, b16, sd = jnp.float32, own.dtype, jax.ShapeDtypeStruct
    q, kv, out, lat, router, side = arrays
    vmem = pl.BlockSpec(memory_space=pltpu.VMEM)
    shapes = [
        sd((tok, width), b16), sd((q.shape[1] // 4, 4 * q.shape[2]), f32), sd((kv.shape[1] // 4, 4 * kv.shape[2]), f32),
        sd(out.shape[1:], f32), sd(lat.shape[2:], f32), sd(router.shape[2:], f32), sd(side.shape[1:], f32), sd((8, 128), f32),
    ]
    buf = lambda *shape: pltpu.VMEM(shape, b16)
    return pl.pallas_call(
        functools.partial(finish_kernel, nz, na, tuple(swapped)),
        out_shape=shapes,
        in_specs=[HBM, HBM, vmem, vmem, vmem] + [HBM] * (na + len(swapped)),
        out_specs=[vmem] * 8,
        scratch_shapes=[buf(n, tok, width), buf(n, tok, width), buf(quads, tok, width), buf(nz, tok, width),
                        buf(2, nz, tok, width), pltpu.VMEM((8, 128), f32)]
        + [pltpu.VMEM((quads,) + v.shape[-2:], v.dtype) for v in arrays]
        + [pltpu.VMEM((nz,) + v.shape[-2:], v.dtype) for v in arrays]
        + [pltpu.VMEM((2, nz) + v.shape[-2:], v.dtype) for v in arrays]
        + [buf(4, q.shape[1] // 4, q.shape[2]), buf(4, kv.shape[1] // 4, kv.shape[2]), buf(*out.shape[1:]),
           pltpu.VMEM((4,) + side.shape[1:], f32), pltpu.VMEM((8, 128), f32), pltpu.VMEM((quads + 2, 8, 128), f32)]
        + [SEM((n,)), SEM((n,)), SEM((n,)), SEM((quads,)), SEM((quads,)), SEM((nz,)), SEM((nz,)), SEM((nz,)), SEM((2, nz)),
           SEM((na, quads)), SEM((na, nz)), SEM((na, nz)), SEM((na, nz)), SEM((2, na, nz)), SEM((na,)), SEM((na, 3)),
           SEM((na, 3)), SEM, SEM, SEM((quads + 2,)), SEM((quads + 2,))],
        cost_estimate=lasting(130),
        compiler_params=pltpu.CompilerParams(collective_id=cid, has_side_effects=True, vmem_limit_bytes=58 << 20),
    )(own, far, stream, attn, mid, *arrays, *swapped.values())


def silu_parts(values):
    sigmoid = jax.nn.sigmoid(values)
    return values * sigmoid, sigmoid * (1.0 + values * (1.0 - sigmoid))


def experts_kernel(nt_ref, sg_ref, tail_ref, wg_ref, wu_ref, wd_ref, ws_ref, wsd_ref,
                   own_ref, far_ref, ng_ref, x_ref, g_ref, hid_ref, dg_ref, du_ref, dws_out, dsd_ref,
                   dws_ref, *, slots):
    f32, b16 = jnp.float32, jnp.bfloat16
    i = pl.program_id(0)
    @pl.when(i == 0)
    def _():
        for r in (dws_ref, dsd_ref):
            r[...] = jnp.zeros_like(r)
    tokens = nt_ref.shape[0] * nt_ref.shape[1]
    width = nt_ref.shape[2]
    nt = nt_ref[...].reshape(tokens, width)
    sg = sg_ref[...].reshape(tokens, width)
    blocks, tok = nt_ref.shape[:2]
    lines = tail_ref.shape[1] // 2
    me = lax.axis_index("rep")
    gate_row = tail_ref[:, pl.ds(me, 1), :].reshape(blocks, tok)
    named = tail_ref[:, pl.ds(lines + me, 1), :].reshape(blocks, tok)
    before = lax.broadcasted_iota(jnp.int32, (tok, tok), 0) < lax.broadcasted_iota(jnp.int32, (tok, tok), 1)
    rank = wide_product(named.astype(b16), before.astype(f32).astype(b16)).astype(jnp.int32)
    rank = rank + lax.broadcasted_iota(jnp.int32, (blocks, tok), 0) * (slots // blocks)
    place_of = jnp.where(named > 0, rank, -1)
    in_row = lambda v: jnp.concatenate([v[j : j + 1] for j in range(blocks)], axis=1)
    hit = lax.broadcasted_iota(jnp.int32, (slots, tokens), 0) == in_row(place_of)
    pick = hit.astype(f32).astype(b16)
    x = wide_product(pick, nt).astype(b16)
    x_ref[...] = x
    g0 = wide_product(pick, sg)
    gate = jnp.sum(jnp.where(hit, in_row(gate_row), 0.0), axis=1, keepdims=True)
    g = (gate * g0).astype(b16)
    g_ref[...] = g
    gv = dot_nt(x, wg_ref[...])
    uv = dot_nt(x, wu_ref[...])
    act, slope = silu_parts(gv)
    hid = (act * uv).astype(b16)
    part = wide_product(hid, wd_ref[...])
    gg = jnp.sum(g0 * part, axis=1, keepdims=True)
    gg_high = gg.astype(b16).astype(f32)
    column = lax.axis_index("rep") * 4 + lax.axis_index("shard") * 2
    lane = lax.broadcasted_iota(jnp.int32, (slots, 128), 1)
    gg = jnp.where(lane == column, gg_high, jnp.where(lane == column + 1, gg - gg_high, 0.0)).astype(b16)
    e_out = (gate * part).astype(b16)
    hid_ref[...] = hid
    hg = dot_nt(g, wd_ref[...])
    dg = (hg * uv * slope).astype(b16)
    du = (hg * act).astype(b16)
    dg_ref[...] = dg
    du_ref[...] = du
    ing = (wide_product(dg, wg_ref[...]) + wide_product(du, wu_ref[...])).astype(b16)
    fs = wsd_ref.shape[0]
    s = wide_product(nt, ws_ref[...])
    sgv, suv = s[:, :fs], s[:, fs:]
    sact, sslope = silu_parts(sgv)
    sh = (sact * suv).astype(b16)
    shg = dot_nt(sg, wsd_ref[...])
    ds = jnp.concatenate([shg * suv * sslope, shg * sact], axis=1).astype(b16)
    dsd_ref[...] += dot_tn(sh, sg)
    dws_ref[...] += dot_tn(ds, nt)
    out = wide_product(sh, wsd_ref[...]) + dot_tn(pick, e_out)
    out = out.astype(b16).reshape(nt_ref.shape)
    c = lax.rem(lax.axis_index("rep"), 2)
    for j in (0, 1):

        @pl.when(c == j)
        def _(j=j):
            own_ref[...] = out[2 * j : 2 * j + 2]
            far_ref[...] = out[2 - 2 * j : 4 - 2 * j]

    ng = dot_nt(ds, ws_ref[...]) + dot_tn(pick, ing)
    ng_ref[:, :, :width] = ng.astype(b16).reshape(nt_ref.shape)
    ng_ref[:, :, width:] = dot_tn(pick, gg).astype(b16).reshape(ng_ref.shape[:2] + (128,))
    @pl.when(i == pl.num_programs(0) - 1)
    def _():
        dws_out[...] = dws_ref[...].T.astype(b16)

def experts_both(nt, sg, tails, wg, wu, wd, ws, wsd, capacity, blocks=4):
    n, tok, width = nt.shape
    steps = n // blocks
    f = wg.shape[0]; fs = wsd.shape[0]
    f32 = jnp.float32
    one = lambda a: pl.BlockSpec(a.shape, lambda i: (0,) * a.ndim, pipeline_mode=pl.Buffered(1))
    blk = pl.BlockSpec((blocks, tok, width), lambda i: (i, 0, 0))
    half = pl.BlockSpec((blocks // 2, tok, width), lambda i: (i, 0, 0))
    row = pl.BlockSpec((blocks,) + tails.shape[1:], lambda i: (i, 0, 0))
    sd = jax.ShapeDtypeStruct
    kept = lambda k: pl.BlockSpec((blocks * capacity, k), lambda i: (i, 0))
    return pl.pallas_call(
        functools.partial(experts_kernel, slots=blocks * capacity),
        grid=(steps,),
        in_specs=[blk, blk, row] + [one(w) for w in (wg, wu, wd, ws, wsd)],
        out_specs=[half, half, pl.BlockSpec((blocks, tok, width + 128), lambda i: (i, 0, 0)), kept(width), kept(width)]
        + [kept(f)] * 3
        + [pl.BlockSpec((width, 2 * fs), lambda i: (0, 0)), pl.BlockSpec((fs, width), lambda i: (0, 0))],
        out_shape=[sd((n // 2, tok, width), nt.dtype)] * 2
        + [sd((n, tok, width + 128), nt.dtype)]
        + [sd((n * capacity, k), nt.dtype) for k in (width, width, f, f, f)]
        + [sd((width, 2 * fs), nt.dtype), sd((fs, width), f32)],
        scratch_shapes=[pltpu.VMEM((2 * fs, width), f32)],
        compiler_params=pltpu.CompilerParams(vmem_limit_bytes=62 << 20, dimension_semantics=("arbitrary",)),
        cost_estimate=lasting(110),
    )(nt, sg, tails, wg, wu, wd, ws, wsd)


def swap(v, nz, f):
    pairs = [
        (slot(*f(z, y, c, x)), slot(z, y, c, x))
        for z in range(nz) for y in range(2) for c in range(2) for x in range(2)
    ]
    return lax.ppermute(v, ("rep", "shard"), pairs)


def on_device(
    stream_in, stream_grad, prefix_len, routes, route_weight, attn_gain, query_proj, latent_proj, rope_key_proj,
    latent_gain, kv_up_proj, out_proj, ffn_gain, router_proj, shared_gate, shared_up, shared_down, expert_gate,
    expert_up, expert_down,
):
    f32, b16 = jnp.float32, jnp.bfloat16
    both = ("rep", "shard")
    n_shard, n_rep = lax.axis_size("shard"), lax.axis_size("rep")
    n_dev = n_rep * n_shard
    nz = n_rep // 4
    quads = n_rep // 2
    rep, x = lax.axis_index("rep"), lax.axis_index("shard")
    c = lax.rem(rep, 2)
    member, group = c * 2 + x, x * 2 + c
    tok, width = stream_in.shape
    experts = router_proj.shape[1]
    capacity = max(2, tok * TOP_K * 7 // (6 * experts))
    seq = n_shard * tok
    scale = (DN + DR) ** (-0.5)
    heads = H // 4
    qcols, kcols = heads * (DN + DR), heads * (DN + DV)
    kvr = latent_proj.shape[1]
    lanes = kvr + DR

    dh = width // n_shard
    gl = jnp.pad(latent_gain, (0, dh - kvr // n_shard))
    tiny = jnp.concatenate([rope_key_proj.T, router_proj.T, attn_gain[None], ffn_gain[None], gl[None]], axis=0)
    tiny = jnp.pad(tiny, ((0, -tiny.shape[0] % 16), (0, 0)))
    stream_all, mat_q, mat_kv, mat_lat, tiny = open_quad(stream_in, query_proj, kv_up_proj, latent_proj, tiny, nz, 1)
    mat_q = mat_q.reshape(width, qcols)
    mat_kv = mat_kv.reshape(kvr, kcols)
    mat_lat = mat_lat.reshape(width, kvr)
    joined = jnp.concatenate([tiny[0], tiny[1]], axis=1)
    rope_t, router_t = joined[:DR], joined[DR : DR + experts]
    gain_attn = joined[DR + experts].astype(f32)
    gain_ffn = joined[DR + experts + 1].astype(f32)
    gain_latent = tiny[:, DR + experts + 2, : kvr // n_shard].reshape(kvr).astype(f32)
    mat_out = lax.dynamic_slice_in_dim(out_proj, c * heads * DV, heads * DV, 0)

    late_grad, stream_all = lax.optimization_barrier((stream_grad, stream_all))
    grad_all = lax.all_gather(late_grad, both, axis=0)
    one_hot = (routes[:, :, None] == jnp.arange(experts)[None, None, :]).astype(f32)
    mask = jnp.sum(one_hot, axis=1)
    weight = jnp.sum(one_hot * route_weight[:, :, None], axis=1)
    fs = shared_down.shape[0]
    lanes_s = -(-fs // 128) * 128
    own_w = width // n_dev
    split = split_units(shared_gate, shared_up, n_dev, fs)
    w_s = lax.all_to_all(split, both, split_axis=0, concat_axis=0, tiled=True).reshape(width, 2 * lanes_s)
    w_sd = jnp.pad(shared_down, ((0, lanes_s - fs), (0, 0)))

    stream4 = stream_all.reshape(4 * tok, width).astype(f32)
    normed = (stream4 * rms_scale(stream4) * gain_attn).astype(b16)
    positions = jnp.arange(seq)
    cosine, sine = rope_tables(positions, DR)
    q_raw = wide_product(normed, mat_q).reshape(2, seq, heads, DN + DR)
    q_nope = q_raw[..., :DN].astype(b16)
    q_rot = rotate(q_raw[..., DN:], cosine[:, None], sine[:, None]).astype(b16)
    latent = wide_product(normed, mat_lat)
    scale_lat = rms_scale(latent)
    latent_normed = (latent * scale_lat * gain_latent).astype(b16)
    k_rot = rotate(dot_nt(normed, rope_t).reshape(2, seq, DR), cosine, sine).astype(b16)
    keyval = wide_product(latent_normed, mat_kv).astype(b16).reshape(2, seq, heads, DN + DV)
    k_nope, values = keyval[..., :DN], keyval[..., DN:]
    prefix = lax.dynamic_slice_in_dim(prefix_len, rep - c, 2)
    allowed = (positions[None, None, :] <= positions[None, :, None]) | (positions[None, None, :] < prefix[:, None, None])
    allowed = allowed[:, None]
    raw = contract(q_nope, k_nope, ((3,), (3,)), ((0, 2), (0, 2)))
    raw = raw + jnp.swapaxes(contract(q_rot, k_rot, ((3,), (2,)), ((0,), (0,))), 1, 2)
    scores = jnp.where(allowed, raw * scale, MASKED)
    expo = jnp.exp(scores - jnp.max(scores, axis=-1, keepdims=True))
    probs = expo / jnp.sum(expo, axis=-1, keepdims=True)
    probs_low = probs.astype(b16)
    attended = jnp.swapaxes(contract(probs_low, values, ((3,), (1,)), ((0, 1), (0, 2))), 1, 2)
    attended = attended.astype(b16).reshape(4 * tok, heads * DV)
    part = wide_product(attended, mat_out).astype(b16).reshape(4, tok, width)
    attn_out = quad_scatter(part, 3)
    stream = stream_in.astype(f32)
    mid = stream + attn_out
    scale_two = rms_scale(mid)
    normed_two = (mid * scale_two * gain_ffn).astype(b16)

    router_prob = jax.nn.softmax(dot_nt(normed_two, router_t), axis=-1)
    picked = mask * router_prob
    picked_sum = jnp.sum(picked, axis=-1, keepdims=True)
    gates = weight * picked / picked_sum
    nt_all, tails = all_gather(normed_two, jnp.concatenate([gates.T, mask.T], axis=0), n_dev, nz, 4)

    mats = (jnp.swapaxes(expert_gate, 1, 2)[0], jnp.swapaxes(expert_up, 1, 2)[0], expert_down[0], w_s, w_sd)
    out_own, out_far, n_grad, *kept, grad_s, grad_sd = experts_both(
        nt_all, grad_all, tails, *mats, capacity, 4)
    n_grad, grad_eg, grad_eu, grad_ed = reduce_scatter(n_grad, *kept, nz, 16)
    back = lax.all_to_all(grad_s.reshape(n_dev, own_w, 2 * lanes_s), both, split_axis=0, concat_axis=0, tiled=True)
    back = join_units(back, n_dev * fs, fs)
    gate_grad = jnp.sum(n_grad[:, width : width + 4 * experts].reshape(tok, experts, 4), axis=-1)
    n_grad = n_grad[:, :width]

    weighted = weight * gate_grad
    picked_grad = weighted / picked_sum - jnp.sum(weighted * picked, axis=-1, keepdims=True) / (picked_sum * picked_sum)
    prob_grad = mask * picked_grad
    logit_grad = (router_prob * (prob_grad - jnp.sum(router_prob * prob_grad, axis=-1, keepdims=True))).astype(b16)
    n_grad = n_grad + wide_product(logit_grad, router_t)
    norm_part, ffn_gain_grad = norm_back(n_grad, mid, scale_two, gain_ffn)
    mid_grad = stream_grad.astype(f32) + norm_part
    aog = mid_grad.astype(b16)
    tail = jnp.pad(logit_grad, ((0, 0), (0, 128 - experts)))
    aog_all = quad_gather(jnp.concatenate([aog, tail], axis=1), 7).reshape(4 * tok, width + 128)
    logit_all = aog_all[:, width:]
    aog_all = aog_all[:, :width]

    att_grad = dot_nt(aog_all, mat_out).astype(b16)
    grad_out = dot_tn(attended, aog_all)
    grad_out = grad_out.astype(b16).reshape(quads, -1, width)
    y_of = lax.rem(rep // 2, 2)

    def over_y(v):
        far = lax.dynamic_index_in_dim(v.reshape((nz, 2) + v.shape[1:]), 1 - y_of, 1, False)
        return swap(far, nz, lambda z, y, c, x: (z, 1 - y, c, x))

    out_y = over_y(grad_out)
    att_grad = att_grad.reshape(2, seq, heads, DV)
    value_grad = jnp.swapaxes(contract(probs_low, att_grad, ((2,), (1,)), ((0, 1), (0, 2))), 1, 2)
    prob_grad_a = contract(att_grad, values, ((3,), (3,)), ((0, 2), (0, 2)))
    s_grad = probs * (prob_grad_a - jnp.sum(probs * prob_grad_a, axis=-1, keepdims=True))
    s_grad = s_grad.astype(b16)
    qn_grad = scale * jnp.swapaxes(contract(s_grad, k_nope, ((3,), (1,)), ((0, 1), (0, 2))), 1, 2)
    qr_grad = scale * jnp.swapaxes(contract(s_grad, k_rot, ((3,), (1,)), ((0,), (0,))), 1, 2)
    kn_grad = scale * jnp.swapaxes(contract(s_grad, q_nope, ((2,), (1,)), ((0, 1), (0, 2))), 1, 2)
    kr_grad = scale * contract(s_grad, q_rot, ((1, 2), (2, 1)), ((0,), (0,)))
    keyval_grad = jnp.concatenate([kn_grad, value_grad], axis=-1).astype(b16).reshape(4 * tok, kcols)
    qr_grad = rotate(qr_grad, cosine[:, None], -sine[:, None])
    query_grad = jnp.concatenate([qn_grad, qr_grad], axis=-1).astype(b16).reshape(4 * tok, qcols)
    lat_part = dot_nt(keyval_grad, mat_kv)
    lat_part = jnp.concatenate([lat_part, kr_grad.reshape(4 * tok, DR)], axis=1).astype(b16)
    lat_part = lat_part.astype(f32) + swap(lat_part, nz, lambda z, y, c, x: (z, y, c, 1 - x)).astype(f32)
    lat_part = lat_part.astype(b16)
    lat_sum = lat_part.astype(f32) + swap(lat_part, nz, lambda z, y, c, x: (z, y, 1 - c, x)).astype(f32)
    lat_sum, kr_sum = lat_sum[:, :kvr], lat_sum[:, kvr:lanes].reshape(2, seq, DR)
    key_pre = rotate(kr_sum, cosine, -sine).reshape(4 * tok, DR).astype(b16)
    weighted_l = lat_sum * gain_latent
    inner = jnp.mean(weighted_l * latent, axis=-1, keepdims=True)
    latent_pre = scale_lat * weighted_l - latent * (scale_lat * scale_lat * scale_lat) * inner
    lat_gain_rows = lat_sum * latent * scale_lat
    lat_gain_grad = jnp.sum(lax.dynamic_slice_in_dim(lat_gain_rows, member * tok, tok, 0), axis=0)
    lat_grad = jnp.concatenate([latent_pre.astype(b16), key_pre], axis=1)
    part = dot_nt(query_grad, mat_q)
    normed_grad = quad_scatter(part.astype(b16).reshape(4, tok, width), 9)
    lat_own = lax.dynamic_slice_in_dim(lat_grad, member * tok, tok, 0)
    normed_grad = normed_grad + dot_nt(lat_own[:, :kvr], mat_lat) + wide_product(lat_own[:, kvr:], rope_t)
    attn_part, attn_gain_grad = norm_back(normed_grad, stream, rms_scale(stream), gain_attn)
    grad_stream = (mid_grad + attn_part).astype(b16)

    gq = dot_tn(normed, query_grad).astype(b16)
    gkv = dot_tn(latent_normed, keyval_grad).astype(b16).reshape(quads, -1, kcols)
    kv_y = over_y(gkv)
    nt_quad = lax.dynamic_slice_in_dim(nt_all, (rep // 2) * 4, 4, 0).reshape(4 * tok, width)
    lat_grad = jnp.pad(lat_grad, ((0, 0), (0, -lanes % 128)))
    glat = dot_tn(normed, lat_grad).astype(b16).reshape(quads, 4, own_w, -1)
    grouter = dot_tn(nt_quad, logit_all).astype(b16).reshape(quads, 4, own_w, -1)
    side = jnp.concatenate([v.reshape(quads, -1) for v in (attn_gain_grad, ffn_gain_grad, lat_gain_grad)], axis=1)
    side = jnp.pad(side, ((0, 0), (0, 1024 - side.shape[1]))).reshape(quads, 8, 128)
    stream_out, o_q, o_kv, o_out, o_lat, o_router, o_side, o_stat = finish(
        out_own, out_far, stream_in, attn_out, mid,
        [gq.reshape(quads, -1, qcols), gkv, grad_out, glat, grouter, side], {1: kv_y, 2: out_y}, nz, 10)
    o_side = o_side.reshape(-1)
    per = width // quads
    perl = kvr // quads
    ga = lax.dynamic_slice_in_dim(o_side, member * own_w, own_w)
    gf = lax.dynamic_slice_in_dim(o_side, per + member * own_w, own_w)
    gla = lax.dynamic_slice_in_dim(o_side, 2 * per + member * (perl // 4), perl // 4)
    stats = jnp.sqrt(jnp.sum(o_stat[:5], axis=1) / (tok * n_dev * width))
    return (
        stream_out, grad_stream, stats, ga, o_q, o_lat[:, :kvr], o_lat[:, kvr:lanes], gla, o_kv, o_out, gf,
        o_router[:, :experts], back[0], back[1], grad_sd[:fs], jnp.swapaxes(grad_eg.astype(f32)[None], 1, 2), jnp.swapaxes(grad_eu.astype(f32)[None], 1, 2), grad_ed.astype(f32)[None],
    )


def on_device_weights(
    stream_in,
    stream_grad,
    prefix_len,
    routes,
    route_weight,
    attn_gain,
    query_proj,
    latent_proj,
    rope_key_proj,
    latent_gain,
    kv_up_proj,
    out_proj,
    ffn_gain,
    router_proj,
    shared_gate,
    shared_up,
    shared_down,
    expert_gate,
    expert_up,
    expert_down,
):
    n_shard = lax.axis_size("shard")
    n_rep = lax.axis_size("rep")
    rep_index = lax.axis_index("rep")
    shard_index = lax.axis_index("shard")
    tok_rows = stream_in.shape[0]
    seq_len = n_shard * tok_rows
    experts = router_proj.shape[1]
    capacity = max(2, tok_rows * TOP_K * 7 // (6 * experts))
    head_width = H * (DN + DV)
    kv_rows = tok_rows * head_width // 128
    rope_rows = tok_rows * DR // 128
    piece_rows = kv_rows + rope_rows
    score_scale = (DN + DR) ** (-0.5)
    weights = (
        attn_gain,
        query_proj,
        latent_proj,
        rope_key_proj,
        latent_gain,
        kv_up_proj,
        out_proj,
        ffn_gain,
        router_proj,
    )
    shared_mats = (shared_gate, shared_up, shared_down)
    (
        gain_attn,
        mat_query,
        mat_latent,
        mat_rope,
        gain_latent,
        mat_kv,
        mat_out,
        gain_ffn,
        mat_router,
    ) = (
        lax.all_gather(weights[0], "shard", axis=0, tiled=True),
        lax.all_gather(weights[1], "shard", axis=0, tiled=True),
        lax.all_gather(weights[2], "shard", axis=0, tiled=True),
        lax.all_gather(weights[3], "shard", axis=0, tiled=True),
        lax.all_gather(weights[4], "shard", axis=0, tiled=True),
        lax.all_gather(weights[5], "shard", axis=0, tiled=True),
        lax.all_gather(weights[6], "shard", axis=0, tiled=True),
        lax.all_gather(weights[7], "shard", axis=0, tiled=True),
        lax.all_gather(weights[8], "shard", axis=0, tiled=True),
    )
    mat_sgate, mat_sup, mat_sdown = (
        lax.all_gather(shared_mats[0], ("rep", "shard"), axis=0, tiled=True),
        lax.all_gather(shared_mats[1], ("rep", "shard"), axis=0, tiled=True),
        lax.all_gather(shared_mats[2], ("rep", "shard"), axis=0, tiled=True),
    )
    gain_attn = gain_attn.astype(jnp.float32)
    gain_latent = gain_latent.astype(jnp.float32)
    gain_ffn = gain_ffn.astype(jnp.float32)
    stream = stream_in.astype(jnp.float32)
    scale_one = rms_scale(stream)
    normed = (stream * scale_one * gain_attn).astype(jnp.bfloat16)
    positions = shard_index * tok_rows + jnp.arange(tok_rows)
    cosine, sine_vals = rope_tables(positions, DR)
    query_raw = wide_product(normed, mat_query).reshape(tok_rows, H, DN + DR)
    query_nope = query_raw[:, :, :DN].astype(jnp.bfloat16)
    query_rot = rotate(query_raw[:, :, DN:], cosine[:, None], sine_vals[:, None]).astype(
        jnp.bfloat16
    )
    latent = wide_product(normed, mat_latent)
    scale_lat = rms_scale(latent)
    latent_normed = (latent * scale_lat * gain_latent).astype(jnp.bfloat16)
    keyval_own = wide_product(latent_normed, mat_kv).astype(jnp.bfloat16)
    key_rot_own = rotate(wide_product(normed, mat_rope), cosine, sine_vals).astype(jnp.bfloat16)
    packed = jnp.concatenate(
        [keyval_own.reshape(kv_rows, 128), key_rot_own.reshape(rope_rows, 128)], axis=0
    )
    seq_keys = lax.all_gather(packed, "shard", axis=0, tiled=True).reshape(n_shard, piece_rows, 128)
    keyval = seq_keys[:, :kv_rows].reshape(seq_len, H, DN + DV)
    key_rot = seq_keys[:, kv_rows:].reshape(seq_len, DR)
    key_nope = keyval[:, :, :DN]
    values = keyval[:, :, DN:]
    prefix = lax.dynamic_index_in_dim(prefix_len, rep_index, keepdims=False)
    key_pos = jnp.arange(seq_len)
    allowed = (key_pos[None, :] <= positions[:, None]) | (key_pos[None, :] < prefix)

    def score_block():
        raw = contract(query_nope, key_nope, ((2,), (2,)), ((1,), (1,)))
        raw = raw + jnp.transpose(contract(query_rot, key_rot, ((2,), (1,)), ((), ())), (1, 0, 2))
        return jnp.where(allowed[None], raw * score_scale, MASKED)

    scores = score_block()
    top_score = jnp.max(scores, axis=-1, keepdims=True)
    expo = jnp.exp(scores - top_score)
    total_exp = jnp.sum(expo, axis=-1, keepdims=True)
    log_total = top_score + jnp.log(total_exp)
    probs_low = (expo / total_exp).astype(jnp.bfloat16)
    attended = jnp.transpose(contract(probs_low, values, ((2,), (0,)), ((0,), (1,))), (1, 0, 2))
    attended = attended.reshape(tok_rows, H * DV).astype(jnp.bfloat16)
    attn_out = wide_product(attended, mat_out)
    mid = stream + attn_out
    scale_two = rms_scale(mid)
    normed_two = (mid * scale_two * gain_ffn).astype(jnp.bfloat16)
    router_prob = jax.nn.softmax(wide_product(normed_two, mat_router), axis=-1)
    one_hot = (routes[:, :, None] == jnp.arange(experts)[None, None, :]).astype(jnp.float32)
    picked = jnp.sum(one_hot * router_prob[:, None, :], axis=-1)
    picked_sum = jnp.sum(picked, axis=-1, keepdims=True)
    gates = route_weight * picked / picked_sum
    sgate_val = wide_product(normed_two, mat_sgate)
    sup_val = wide_product(normed_two, mat_sup)
    shared_hidden = (jax.nn.silu(sgate_val) * sup_val).astype(jnp.bfloat16)
    shared_out = wide_product(shared_hidden, mat_sdown)
    flat_routes = routes.reshape(-1)
    route_hot = (flat_routes[:, None] == jnp.arange(experts)[None, :]).astype(jnp.int32)
    route_rank = jnp.sum((jnp.cumsum(route_hot, axis=0) - route_hot) * route_hot, axis=1)
    slot_index = flat_routes * capacity + route_rank
    send_rows = (
        jnp.zeros((experts * capacity, D), jnp.bfloat16)
        .at[slot_index]
        .set(jnp.repeat(normed_two, TOP_K, axis=0))
    )
    doubled = jnp.broadcast_to(
        send_rows.reshape(experts, 1, capacity, D), (experts, n_shard, capacity, D)
    ).reshape(-1, D)
    incoming_rows = lax.all_to_all(
        doubled, ("rep", "shard"), split_axis=0, concat_axis=0, tiled=True
    )
    gate_local = expert_gate[0]
    local_up_weight = expert_up[0]
    down_local = expert_down[0]
    expert_gate_value = wide_product(incoming_rows, gate_local)
    expert_up_value = wide_product(incoming_rows, local_up_weight)
    expert_inner_state = (jax.nn.silu(expert_gate_value) * expert_up_value).astype(jnp.bfloat16)
    expert_part = wide_product(expert_inner_state, down_local).astype(jnp.bfloat16)
    returned = lax.all_to_all(
        expert_part, ("rep", "shard"), split_axis=0, concat_axis=0, tiled=True
    )
    expert_sum = jnp.sum(
        returned.reshape(experts, n_shard, capacity, D).astype(jnp.float32), axis=1
    ).reshape(experts * capacity, D)
    picked_rows = expert_sum[slot_index].reshape(tok_rows, TOP_K, D)
    ffn_out = shared_out + jnp.sum(gates[:, :, None] * picked_rows, axis=1)
    residual = mid + ffn_out
    squares = jnp.stack(
        [
            jnp.sum(stream * stream),
            jnp.sum(attn_out * attn_out),
            jnp.sum(mid * mid),
            jnp.sum(ffn_out * ffn_out),
            jnp.sum(residual * residual),
        ]
    )
    totals = lax.psum(squares, ("rep", "shard"))
    stats = jnp.sqrt(totals / (tok_rows * n_rep * n_shard * D))
    (
        gain_attn,
        mat_query,
        mat_latent,
        mat_rope,
        gain_latent,
        mat_kv,
        mat_out,
        gain_ffn,
        mat_router,
    ) = (
        lax.all_gather(weights[0], "shard", axis=0, tiled=True),
        lax.all_gather(weights[1], "shard", axis=0, tiled=True),
        lax.all_gather(weights[2], "shard", axis=0, tiled=True),
        lax.all_gather(weights[3], "shard", axis=0, tiled=True),
        lax.all_gather(weights[4], "shard", axis=0, tiled=True),
        lax.all_gather(weights[5], "shard", axis=0, tiled=True),
        lax.all_gather(weights[6], "shard", axis=0, tiled=True),
        lax.all_gather(weights[7], "shard", axis=0, tiled=True),
        lax.all_gather(weights[8], "shard", axis=0, tiled=True),
    )
    mat_sgate, mat_sup, mat_sdown = (
        lax.all_gather(shared_mats[0], ("rep", "shard"), axis=0, tiled=True),
        lax.all_gather(shared_mats[1], ("rep", "shard"), axis=0, tiled=True),
        lax.all_gather(shared_mats[2], ("rep", "shard"), axis=0, tiled=True),
    )
    gain_attn = gain_attn.astype(jnp.float32)
    gain_latent = gain_latent.astype(jnp.float32)
    gain_ffn = gain_ffn.astype(jnp.float32)
    grad_top = stream_grad.astype(jnp.float32)
    gate_grad = jnp.sum(grad_top[:, None, :] * picked_rows, axis=-1)
    expert_grad = (gates[:, :, None] * grad_top[:, None, :]).astype(jnp.bfloat16).reshape(-1, D)
    send_grad = jnp.zeros((experts * capacity, D), jnp.bfloat16).at[slot_index].set(expert_grad)
    doubled_grad = jnp.broadcast_to(
        send_grad.reshape(experts, 1, capacity, D), (experts, n_shard, capacity, D)
    ).reshape(-1, D)
    received_grad = lax.all_to_all(
        doubled_grad, ("rep", "shard"), split_axis=0, concat_axis=0, tiled=True
    )
    grad_edown = contract(expert_inner_state, received_grad, ((0,), (0,)), ((), ()))
    inner_state_gradient = contract(received_grad, down_local, ((1,), (1,)), ((), ()))
    gate_value_gradient = (
        inner_state_gradient * expert_up_value * swish_derivative(expert_gate_value)
    ).astype(jnp.bfloat16)
    up_value_gradient = (inner_state_gradient * jax.nn.silu(expert_gate_value)).astype(jnp.bfloat16)
    grad_egate = contract(incoming_rows, gate_value_gradient, ((0,), (0,)), ((), ()))
    expert_up_gradient = contract(incoming_rows, up_value_gradient, ((0,), (0,)), ((), ()))
    part_in_grad = contract(gate_value_gradient, gate_local, ((1,), (1,)), ((), ()))
    part_in_grad = (
        part_in_grad
        + contract(up_value_gradient, local_up_weight, ((1,), (1,)), ((), ()))
    ).astype(jnp.bfloat16)
    returned_grad = lax.all_to_all(
        part_in_grad, ("rep", "shard"), split_axis=0, concat_axis=0, tiled=True
    )
    slot_grad = jnp.sum(
        returned_grad.reshape(experts, n_shard, capacity, D).astype(jnp.float32), axis=1
    ).reshape(experts * capacity, D)
    routed_grad = jnp.sum(slot_grad[slot_index].reshape(tok_rows, TOP_K, D), axis=1)
    shared_hidden_grad = contract(stream_grad, mat_sdown, ((1,), (1,)), ((), ()))
    dshared_gate = (shared_hidden_grad * sup_val * swish_derivative(sgate_val)).astype(jnp.bfloat16)
    dshared_up = (shared_hidden_grad * jax.nn.silu(sgate_val)).astype(jnp.bfloat16)
    weighted_grad = route_weight * gate_grad
    picked_grad = weighted_grad / picked_sum - jnp.sum(
        weighted_grad * picked, axis=-1, keepdims=True
    ) / (picked_sum * picked_sum)
    prob_grad = jnp.sum(one_hot * picked_grad[:, :, None], axis=1)
    logit_grad = (
        router_prob * (prob_grad - jnp.sum(router_prob * prob_grad, axis=-1, keepdims=True))
    ).astype(jnp.bfloat16)
    normed_two_grad = contract(dshared_gate, mat_sgate, ((1,), (1,)), ((), ()))
    normed_two_grad = normed_two_grad + contract(dshared_up, mat_sup, ((1,), (1,)), ((), ()))
    normed_two_grad = normed_two_grad + contract(logit_grad, mat_router, ((1,), (1,)), ((), ()))
    normed_two_grad = normed_two_grad + routed_grad
    norm_part, grad_gain_ffn = norm_back(normed_two_grad, mid, scale_two, gain_ffn)
    mid_grad = grad_top + norm_part
    attn_out_grad = mid_grad.astype(jnp.bfloat16)
    attended_grad = contract(attn_out_grad, mat_out, ((1,), (1,)), ((), ()))
    attended_grad = attended_grad.astype(jnp.bfloat16).reshape(tok_rows, H, DV)
    probs_full = jnp.where(allowed[None], jnp.exp(score_block() - log_total), 0.0)
    value_grad = jnp.transpose(contract(probs_full.astype(jnp.bfloat16), attended_grad, ((1,), (0,)), ((0,), (1,))), (1, 0, 2))
    prob_att_grad = contract(attended_grad, values, ((2,), (2,)), ((1,), (1,)))
    scores_grad = probs_full * (
        prob_att_grad - jnp.sum(probs_full * prob_att_grad, axis=-1, keepdims=True)
    )
    scores_grad = scores_grad.astype(jnp.bfloat16)
    query_nope_grad = score_scale * jnp.transpose(contract(scores_grad, key_nope, ((2,), (0,)), ((0,), (1,))), (1, 0, 2))
    query_rot_grad = score_scale * jnp.transpose(contract(scores_grad, key_rot, ((2,), (0,)), ((), ())), (1, 0, 2))
    key_nope_grad = score_scale * jnp.transpose(contract(scores_grad, query_nope, ((1,), (0,)), ((0,), (1,))), (1, 0, 2))
    key_rot_grad = score_scale * contract(scores_grad, query_rot, ((0, 1,), (1, 0,)), ((), ()))
    keyval_grad_all = jnp.concatenate([key_nope_grad, value_grad], axis=-1).reshape(
        n_shard, kv_rows, 128
    )
    key_grad_pieces = jnp.concatenate(
        [keyval_grad_all, key_rot_grad.reshape(n_shard, rope_rows, 128)], axis=1
    )
    own_keys = lax.psum_scatter(
        key_grad_pieces.reshape(-1, 128).astype(jnp.bfloat16),
        "shard",
        scatter_dimension=0,
        tiled=True,
    ).astype(jnp.float32)
    keyval_grad = own_keys[:kv_rows].reshape(tok_rows, head_width).astype(jnp.bfloat16)
    key_pre_grad = rotate(own_keys[kv_rows:].reshape(tok_rows, DR), cosine, -sine_vals).astype(
        jnp.bfloat16
    )
    query_rot_back = rotate(query_rot_grad, cosine[:, None], -sine_vals[:, None])
    query_grad = (
        jnp.concatenate([query_nope_grad, query_rot_back], axis=-1)
        .reshape(tok_rows, H * (DN + DR))
        .astype(jnp.bfloat16)
    )
    latent_normed_grad = contract(keyval_grad, mat_kv, ((1,), (1,)), ((), ()))
    latent_pre, grad_gain_latent = norm_back(latent_normed_grad, latent, scale_lat, gain_latent)
    latent_grad = latent_pre.astype(jnp.bfloat16)
    normed_grad = contract(query_grad, mat_query, ((1,), (1,)), ((), ()))
    normed_grad = normed_grad + contract(key_pre_grad, mat_rope, ((1,), (1,)), ((), ()))
    normed_grad = normed_grad + contract(latent_grad, mat_latent, ((1,), (1,)), ((), ()))
    attn_part, grad_gain_attn = norm_back(normed_grad, stream, scale_one, gain_attn)
    grad_stream = (mid_grad + attn_part).astype(jnp.bfloat16)
    owned = (
        lax.psum_scatter(
            grad_gain_attn[None][0], ("rep", "shard"), scatter_dimension=0, tiled=True
        ),
        lax.psum_scatter(
            contract(normed, query_grad, ((0,), (0,)), ((), ())),
            ("rep", "shard"),
            scatter_dimension=0,
            tiled=True,
        ),
        lax.psum_scatter(
            contract(normed, latent_grad, ((0,), (0,)), ((), ())),
            ("rep", "shard"),
            scatter_dimension=0,
            tiled=True,
        ),
        lax.psum_scatter(
            contract(normed, key_pre_grad, ((0,), (0,)), ((), ())),
            ("rep", "shard"),
            scatter_dimension=0,
            tiled=True,
        ),
        lax.psum_scatter(
            grad_gain_latent[None][0], ("rep", "shard"), scatter_dimension=0, tiled=True
        ),
        lax.psum_scatter(
            contract(latent_normed, keyval_grad, ((0,), (0,)), ((), ())),
            ("rep", "shard"),
            scatter_dimension=0,
            tiled=True,
        ),
        lax.psum_scatter(
            contract(attended, attn_out_grad, ((0,), (0,)), ((), ())),
            ("rep", "shard"),
            scatter_dimension=0,
            tiled=True,
        ),
        lax.psum_scatter(grad_gain_ffn[None][0], ("rep", "shard"), scatter_dimension=0, tiled=True),
        lax.psum_scatter(
            contract(normed_two, logit_grad, ((0,), (0,)), ((), ())),
            ("rep", "shard"),
            scatter_dimension=0,
            tiled=True,
        ),
        lax.psum_scatter(
            contract(normed_two, dshared_gate, ((0,), (0,)), ((), ())),
            ("rep", "shard"),
            scatter_dimension=0,
            tiled=True,
        ),
        lax.psum_scatter(
            contract(normed_two, dshared_up, ((0,), (0,)), ((), ())),
            ("rep", "shard"),
            scatter_dimension=0,
            tiled=True,
        ),
        lax.psum_scatter(
            contract(shared_hidden, stream_grad, ((0,), (0,)), ((), ())),
            ("rep", "shard"),
            scatter_dimension=0,
            tiled=True,
        ),
    )
    return (
        residual.astype(jnp.bfloat16),
        grad_stream,
        stats,
        owned[0],
        owned[1],
        owned[2],
        owned[3],
        owned[4],
        owned[5],
        owned[6],
        owned[7],
        owned[8],
        owned[9],
        owned[10],
        owned[11],
        grad_egate[None],
        expert_up_gradient[None],
        grad_edown[None],
    )


def by_size(*args):
    tokens = lax.axis_size("rep") * lax.axis_size("shard") * args[0].shape[0]
    return (on_device if tokens * args[0].shape[1] <= 1 << 23 else on_device_weights)(*args)


def solution(mesh):
    placed = (
        P(("rep", "shard"), None),
        P(("rep", "shard"), None),
        P(),
        P(("rep", "shard"), None),
        P(("rep", "shard"), None),
        P("shard"),
        P("shard", None),
        P("shard", None),
        P("shard", None),
        P("shard"),
        P("shard", None),
        P("shard", None),
        P("shard"),
        P("shard", None),
        P(("rep", "shard"), None),
        P(("rep", "shard"), None),
        P(("rep", "shard"), None),
        P("rep", None, "shard"),
        P("rep", None, "shard"),
        P("rep", "shard", None),
    )
    return jax.shard_map(
        by_size,
        mesh=mesh,
        in_specs=placed,
        out_specs=(
            P(("rep", "shard"), None),
            P(("rep", "shard"), None),
            P(),
            P(("rep", "shard")),
            P(("rep", "shard"), None),
            P(("rep", "shard"), None),
            P(("rep", "shard"), None),
            P(("rep", "shard")),
            P(("rep", "shard"), None),
            P(("rep", "shard"), None),
            P(("rep", "shard")),
            P(("rep", "shard"), None),
            P(("rep", "shard"), None),
            P(("rep", "shard"), None),
            P(("rep", "shard"), None),
            P("rep", None, "shard"),
            P("rep", None, "shard"),
            P("rep", "shard", None),
        ),
        check_vma=False,
    )
```
